32 devices in a mesh: batch: 8 (over z, y), tp: 4 (over x, core).
Axes of the slice: x: 2, y: 2, z: 4, core: 2. Of those that a mesh axis runs over, the one named last changes fastest.
Arguments:
- tokens: bfloat16 [8192, 1024], P(('batch', 'tp')), may hold values from -6 to 6
- lengths: int32 [16], P('batch'), may hold values from 1 to 512, as said below
- w_query: bfloat16 [1024, 1024], P(None, 'tp'), may hold values from -0.1875 to 0.1875
- b_query: bfloat16 [1024], P('tp'), may hold values from -3 to 3
- w_key: bfloat16 [1024, 1024], P(None, 'tp'), may hold values from -0.1875 to 0.1875
- w_value: bfloat16 [1024, 1024], P(None, 'tp'), may hold values from -0.1875 to 0.1875
- b_value: bfloat16 [1024], P('tp'), may hold values from -3 to 3
- w_out: bfloat16 [1024, 1024], P('tp'), may hold values from -3 to 3
- b_out: bfloat16 [1024], replicated, may hold values from -3 to 3
- gain_one: float32 [1024], replicated, may hold values from 0.5 to 1.5
- shift_one: float32 [1024], replicated, may hold values from -3 to 3
- w_up: bfloat16 [1024, 4096], P(None, 'tp'), may hold values from -0.1875 to 0.1875
- b_up: bfloat16 [4096], P('tp'), may hold values from -3 to 3
- w_down: bfloat16 [4096, 1024], P('tp'), may hold values from -0.09375 to 0.09375
- b_down: bfloat16 [1024], replicated, may hold values from -3 to 3
- gain_two: float32 [1024], replicated, may hold values from 0.5 to 1.5
- shift_two: float32 [1024], replicated, may hold values from -3 to 3
- cotangent: bfloat16 [8192, 1024], P(('batch', 'tp')), may hold values from -6 to 6
Outputs:
- output: bfloat16 [8192, 1024], P(('batch', 'tp'))
- grad_tokens: bfloat16 [8192, 1024], P(('batch', 'tp'))
- grad_w_query: float32 [1024, 1024], P('batch', 'tp')
- grad_b_query: float32 [1024], replicated
- grad_w_key: float32 [1024, 1024], P('batch', 'tp')
- grad_w_value: float32 [1024, 1024], P('batch', 'tp')
- grad_b_value: float32 [1024], replicated
- grad_w_out: float32 [1024, 1024], P('tp', 'batch')
- grad_b_out: float32 [1024], replicated
- grad_gain_one: float32 [1024], replicated
- grad_shift_one: float32 [1024], replicated
- grad_w_up: float32 [1024, 4096], P('batch', 'tp')
- grad_b_up: float32 [4096], replicated
- grad_w_down: float32 [4096, 1024], P('tp', 'batch')
- grad_b_down: float32 [1024], replicated
- grad_gain_two: float32 [1024], replicated
- grad_shift_two: float32 [1024], replicated
The draws below stay inside these ranges and needn't reach their ends.
Inputs may be any that keep to these rules, and one draw needn't show every extreme that they name: `lengths`: lengths of 1 to 512, many short; in each aligned block of 2 sequences (those of one index of batch) one sequence, drawn from the seed, has length 512.
All inputs are finite; a program needn't handle non-finite values.
Results may differ from the reference program's by a relative error of at most 0.022.
Values may be sent and summed in bfloat16 or wider, within the bound.
No kernel may reach another device: no remote copies, remote signals or barrier semaphores. Data moves between devices by JAX's collectives and lax.ppermute only.
A program may use at most 128 MiB of HBM per device.

```python
import math
import jax
import jax.numpy as jnp
from jax import lax

D = 1024
HEADS = 16
HEAD_DIM = 64
FF = 4096
SEQ = 512
SEQ_GROUP = 2
SEQS = 16
TOKENS = 8192


def draw_lengths(key, part):
    key = jax.random.fold_in(key, 7)
    first, second, third = jax.random.split(key, 3)
    left = jax.random.randint(first, (SEQS,), 1, SEQ + 1)
    right = jax.random.randint(second, (SEQS,), 1, SEQ + 1)
    ragged = jnp.maximum(left * right // SEQ, 1)
    groups = SEQS // SEQ_GROUP
    chosen = jax.random.randint(third, (groups, 1), 0, SEQ_GROUP)
    slots = jnp.arange(SEQ_GROUP, dtype=jnp.int32)[None, :]
    ragged = jnp.where(slots == chosen, SEQ, ragged.reshape(groups, SEQ_GROUP))
    return ragged.reshape(SEQS).astype(jnp.int32)


def block_levels(key, extent, cuts, smallest, high):
    factor_of, own = 1.0, jax.random.fold_in(key, 6)
    for position, shards_of in cuts:
        draws = jnp.exp(jax.random.uniform(jax.random.fold_in(own, position), (shards_of,), jnp.float32, smallest / len(cuts), high / len(cuts)))
        factor_of = factor_of * jnp.repeat(draws, extent[position] // shards_of).reshape([-1 if axis == position else 1 for axis in range(len(extent))])
    return factor_of


def gaussian(stream_key, shape, scale, most, shards=(), kind=jnp.bfloat16):
    array = scale * jax.random.normal(stream_key, shape, jnp.float32)
    if shards:
        array = array * block_levels(stream_key, shape, shards, -0.22, 0.18)
    return jnp.clip(array, -most, most).astype(kind)


def setup_inputs(seed: int = 0) -> dict:
    key_list = jax.random.split(jax.random.key(seed), 19)
    return {
        "tokens": gaussian(key_list[0], (TOKENS, D), 1.0, 6.0, ((0, 32),)),
        "lengths": draw_lengths(jax.random.fold_in(key_list[18], 71), 0),
        "w_query": gaussian(key_list[2], (D, D), D ** -0.5, 0.1875, ((1, 4),)),
        "b_query": gaussian(key_list[3], (D,), 0.5, 3.0, ((0, 4),)),
        "w_key": gaussian(key_list[4], (D, D), D ** -0.5, 0.1875, ((1, 4),)),
        "w_value": gaussian(key_list[5], (D, D), D ** -0.5, 0.1875, ((1, 4),)),
        "b_value": gaussian(key_list[6], (D,), 0.5, 3.0, ((0, 4),)),
        "w_out": gaussian(key_list[7], (D, D), (max(4, D // 256)) ** -0.5, 3.0, ((0, 4),)),
        "b_out": gaussian(key_list[8], (D,), 0.5, 3.0),
        "gain_one": jnp.clip(1.0 + 0.1 * jax.random.normal(key_list[9], (D,), jnp.float32), 0.5, 1.5),
        "shift_one": gaussian(key_list[10], (D,), 0.5, 3.0, (), jnp.float32),
        "w_up": gaussian(key_list[11], (D, FF), D ** -0.5, 0.1875, ((1, 4),)),
        "b_up": gaussian(key_list[12], (FF,), 0.5, 3.0, ((0, 4),)),
        "w_down": gaussian(key_list[13], (FF, D), FF ** -0.5, 0.09375, ((0, 4),)),
        "b_down": gaussian(key_list[14], (D,), 0.5, 3.0),
        "gain_two": jnp.clip(1.0 + 0.1 * jax.random.normal(key_list[15], (D,), jnp.float32), 0.5, 1.5),
        "shift_two": gaussian(key_list[16], (D,), 0.5, 3.0, (), jnp.float32),
        "cotangent": gaussian(key_list[17], (TOKENS, D), 1.0, 6.0, ((0, 32),)),
    }


@jax.custom_vjp
def low(v):
    return lax.optimization_barrier(v.astype(jnp.bfloat16)).astype(jnp.float32)

@jax.custom_vjp
def low_back(v):
    return v

def low_keep(v):
    return (low(v), None)

def low_pass(kept, grad):
    return (grad,)

def back_keep(v):
    return (v, None)

def back_low(kept, grad):
    return (low(grad),)
low.defvjp(low_keep, low_pass)
low_back.defvjp(back_keep, back_low)
epsilon = 1e-05
negative = -1e+30

def both_round(value):
    return low(low_back(value))

def product(left, right):
    return jnp.dot(left, right, precision=lax.Precision.HIGHEST, preferred_element_type=jnp.float32)

def norm_rows(resid, gain, shift):
    middle = lax.optimization_barrier(jnp.mean(resid, axis=-1, keepdims=True))
    centred = resid - middle
    variance = lax.optimization_barrier(jnp.mean(centred * centred, axis=-1, keepdims=True))
    return centred * lax.rsqrt(variance + epsilon) * gain + shift

def attend_one(item):
    query, key_rows, value_rows, length = item
    scores = jnp.einsum('qhd,khd->hqk', query, key_rows, precision=lax.Precision.HIGHEST)
    scores = low_back(scores)
    valid = jnp.arange(SEQ, dtype=jnp.int32) < length
    scores = jnp.where(valid[None, None, :], scores, negative)
    probs = low(jax.nn.softmax(scores, axis=-1))
    return jnp.einsum('hqk,khd->qhd', probs, value_rows, precision=lax.Precision.HIGHEST)

def layer(weights, inputs, seq_lengths):
    w_query, b_query, w_key, w_value, b_value, w_out, b_out, gain_one, shift_one, w_up, b_up, w_down, b_down, gain_two, shift_two = weights
    count = inputs.shape[0]
    scale = HEAD_DIM ** (-0.5)
    query = both_round((product(inputs, w_query) + b_query) * scale)
    keys = both_round(product(inputs, w_key))
    values = both_round(product(inputs, w_value) + b_value)
    shaped = (count // SEQ, SEQ, HEADS, HEAD_DIM)
    mixed = lax.map(jax.checkpoint(attend_one), (query.reshape(shaped), keys.reshape(shaped), values.reshape(shaped), seq_lengths))
    mixed = both_round(mixed.reshape(count, D))
    branch = low_back(product(mixed, w_out) + b_out)
    hidden = norm_rows(inputs + branch, gain_one, shift_one)
    inner = low_back(product(low(hidden), w_up) + b_up)
    act = low(jax.nn.gelu(inner, approximate=False))
    second = low_back(product(act, w_down) + b_down)
    return norm_rows(hidden + second, gain_two, shift_two)

def reference(tokens, lengths, w_query, b_query, w_key, w_value, b_value, w_out, b_out, gain_one, shift_one, w_up, b_up, w_down, b_down, gain_two, shift_two, cotangent):
    weights = tuple((item.astype(jnp.float32) for item in (w_query, b_query, w_key, w_value, b_value, w_out, b_out, gain_one, shift_one, w_up, b_up, w_down, b_down, gain_two, shift_two)))
    per_block = math.gcd(SEQS, max(1, 4096 // SEQ))
    blocks = SEQS // per_block
    inputs_all = tokens.astype(jnp.float32).reshape(blocks, per_block * SEQ, D)
    upstream_all = cotangent.astype(jnp.float32).reshape(blocks, per_block * SEQ, D)
    lengths_all = lengths.reshape(blocks, per_block)

    def advance(running, item):
        inputs, seq_lengths, upstream = item

        def apply_layer(weight_set, rows_in):
            return layer(weight_set, rows_in, seq_lengths)
        result, pullback = jax.vjp(apply_layer, weights, inputs)
        grad_weights, grad_inputs = pullback(upstream)
        running = jax.tree.map(lambda first, second: first + second, running, grad_weights)
        return (running, (result.astype(jnp.bfloat16), grad_inputs.astype(jnp.bfloat16)))
    zeros = jax.tree.map(jnp.zeros_like, weights)
    grads, (results, grad_rows) = lax.scan(advance, zeros, (inputs_all, lengths_all, upstream_all))
    return (results.reshape(TOKENS, D), grad_rows.reshape(TOKENS, D), grads[0], grads[1], grads[2], grads[3], grads[4], grads[5], grads[6], grads[7], grads[8], grads[9], grads[10], grads[11], grads[12], grads[13], grads[14])
```

```python
import math

import jax
import jax.numpy as jnp
from jax import lax
from jax.sharding import PartitionSpec as P

HEAD_DIM = 64


epsilon = 1e-05
negative = -1e30


def product(left, right):
    return jnp.dot(left, right, preferred_element_type=jnp.float32)


def over_rows(left, right):
    return lax.dot_general(
        left, right, (((0,), (0,)), ((), ())), preferred_element_type=jnp.float32
    )


def against(left, right):
    return lax.dot_general(
        left, right, (((1,), (1,)), ((), ())), preferred_element_type=jnp.float32
    )


def norm_forward(resid, gain, shift):
    middle = jnp.mean(resid, axis=-1, keepdims=True)
    centred = resid - middle
    variance = jnp.mean(centred * centred, axis=-1, keepdims=True)
    inverse = lax.rsqrt(variance + epsilon)
    normed = centred * inverse
    return (normed * gain + shift, normed, inverse)


def norm_backward(upstream, normed, inverse, gain):
    scaled = upstream * gain
    first = jnp.mean(scaled, axis=-1, keepdims=True)
    second = jnp.mean(scaled * normed, axis=-1, keepdims=True)
    grad_resid = inverse * (scaled - first - normed * second)
    return (grad_resid, jnp.sum(upstream * normed, axis=0), jnp.sum(upstream, axis=0))


def gelu_slope(inner):
    cumulative = 0.5 * (1.0 + lax.erf(inner * 2.0 ** (-0.5)))
    density = jnp.exp(-0.5 * inner * inner) * (2.0 * math.pi) ** (-0.5)
    return cumulative + inner * density


def attend_forward(query, keys, values, valid):
    scores = jnp.einsum("qhd,khd->hqk", query, keys, preferred_element_type=jnp.float32)
    scores = jnp.where(valid[None, None, :], scores, negative)
    highest = jnp.max(scores, axis=-1, keepdims=True)
    exponent = jnp.exp(scores - highest)
    total = jnp.sum(exponent, axis=-1, keepdims=True)
    probs = (exponent / total).astype(jnp.bfloat16)
    mixed = jnp.einsum("hqk,khd->qhd", probs, values, preferred_element_type=jnp.float32)
    return (mixed.astype(jnp.bfloat16), highest + jnp.log(total))


def attend_backward(query, keys, values, valid, log_total, grad_mixed):
    scores = jnp.einsum("qhd,khd->hqk", query, keys, preferred_element_type=jnp.float32)
    scores = jnp.where(valid[None, None, :], scores, negative)
    probs = jnp.exp(scores - log_total)
    rounded = probs.astype(jnp.bfloat16)
    grad_values = jnp.einsum(
        "hqk,qhd->khd", rounded, grad_mixed, preferred_element_type=jnp.float32
    )
    grad_probs = jnp.einsum("qhd,khd->hqk", grad_mixed, values, preferred_element_type=jnp.float32)
    centre = jnp.sum(probs * grad_probs, axis=-1, keepdims=True)
    grad_scores = (probs * (grad_probs - centre)).astype(jnp.bfloat16)
    grad_query = jnp.einsum("hqk,khd->qhd", grad_scores, keys, preferred_element_type=jnp.float32)
    grad_keys = jnp.einsum("hqk,qhd->khd", grad_scores, query, preferred_element_type=jnp.float32)
    return (grad_query, grad_keys, grad_values)


def spread(piece):
    return lax.all_gather(piece, "tp", axis=0, tiled=True)


def collect(piece):
    return lax.psum_scatter(
        piece.astype(jnp.bfloat16), "tp", scatter_dimension=0, tiled=True
    ).astype(jnp.float32)


def forward_item(item):
    return attend_forward(item[0], item[1], item[2], item[3])


def backward_item(item):
    return attend_backward(item[0], item[1], item[2], item[3], item[4], item[5])


def body(
    tokens,
    lengths,
    w_query,
    b_query,
    w_key,
    w_value,
    b_value,
    w_out,
    b_out,
    gain_one,
    shift_one,
    w_up,
    b_up,
    w_down,
    b_down,
    gain_two,
    shift_two,
    cotangent,
):
    head_dim = HEAD_DIM
    scale = head_dim ** (-0.5)
    own_rows = tokens.shape[0]
    seq_len = 2 * own_rows
    tp_index = lax.axis_index("tp")
    upstream = cotangent.astype(jnp.float32)
    gathered = spread(tokens)
    groups = gathered.shape[0] // seq_len
    local_width = w_query.shape[1]
    local_heads = local_width // head_dim
    query = ((product(gathered, w_query) + b_query) * scale).astype(jnp.bfloat16)
    keys = product(gathered, w_key).astype(jnp.bfloat16)
    values = (product(gathered, w_value) + b_value).astype(jnp.bfloat16)
    shaped = (groups, seq_len, local_heads, head_dim)
    positions = jnp.arange(seq_len, dtype=jnp.int32)
    valid = positions[None, :] < lengths[:, None]
    query_s = query.reshape(shaped)
    keys_s = keys.reshape(shaped)
    values_s = values.reshape(shaped)
    mixed_s, log_total = lax.map(forward_item, (query_s, keys_s, values_s, valid))
    mixed = mixed_s.reshape(-1, local_width)
    branch = collect(product(mixed, w_out)) + b_out
    hidden, normed_one, inverse_one = norm_forward(
        tokens.astype(jnp.float32) + branch, gain_one, shift_one
    )
    hidden_all = spread(hidden.astype(jnp.bfloat16))
    inner = product(hidden_all, w_up) + b_up
    act = jax.nn.gelu(inner, approximate=False).astype(jnp.bfloat16)
    second = collect(product(act, w_down)) + b_down
    result, normed_two, inverse_two = norm_forward(hidden + second, gain_two, shift_two)
    grad_resid_two, grad_gain_two, grad_shift_two = norm_backward(
        upstream, normed_two, inverse_two, gain_two
    )
    grad_second = grad_resid_two.astype(jnp.bfloat16)
    grad_second_all = spread(grad_second)
    grad_w_down = over_rows(act, grad_second_all)
    grad_inner = (against(grad_second_all, w_down) * gelu_slope(inner)).astype(jnp.bfloat16)
    grad_w_up = over_rows(hidden_all, grad_inner)
    grad_hidden = collect(against(grad_inner, w_up)) + grad_resid_two
    grad_resid_one, grad_gain_one, grad_shift_one = norm_backward(
        grad_hidden, normed_one, inverse_one, gain_one
    )
    grad_branch = grad_resid_one.astype(jnp.bfloat16)
    grad_branch_all = spread(grad_branch)
    grad_w_out = over_rows(mixed, grad_branch_all)
    grad_mixed = against(grad_branch_all, w_out).astype(jnp.bfloat16)
    grad_query_s, grad_keys_s, grad_values_s = lax.map(
        backward_item, (query_s, keys_s, values_s, valid, log_total, grad_mixed.reshape(shaped))
    )
    grad_query = (grad_query_s.astype(jnp.bfloat16) * scale).reshape(-1, local_width)
    grad_keys = grad_keys_s.astype(jnp.bfloat16).reshape(-1, local_width)
    grad_values = grad_values_s.astype(jnp.bfloat16).reshape(-1, local_width)
    grad_w_query = over_rows(gathered, grad_query)
    grad_w_key = over_rows(gathered, grad_keys)
    grad_w_value = over_rows(gathered, grad_values)
    grad_input_part = (
        against(grad_query, w_query) + against(grad_keys, w_key) + against(grad_values, w_value)
    )
    grad_tokens = (collect(grad_input_part) + grad_resid_one).astype(jnp.bfloat16)
    width = w_query.shape[0]
    hidden_units = w_up.shape[1] * lax.axis_size("tp")
    query_bias = lax.dynamic_update_slice(
        jnp.zeros((width,), jnp.float32),
        jnp.sum(grad_query.astype(jnp.float32), axis=0),
        (tp_index * local_width,),
    )
    value_bias = lax.dynamic_update_slice(
        jnp.zeros((width,), jnp.float32),
        jnp.sum(grad_values.astype(jnp.float32), axis=0),
        (tp_index * local_width,),
    )
    up_bias = lax.dynamic_update_slice(
        jnp.zeros((hidden_units,), jnp.float32),
        jnp.sum(grad_inner.astype(jnp.float32), axis=0),
        (tp_index * w_up.shape[1],),
    )
    big = (grad_w_query, grad_w_key, grad_w_value, grad_w_out, grad_w_up, grad_w_down)
    out_bias = jnp.sum(grad_branch.astype(jnp.float32), axis=0)
    down_bias = jnp.sum(grad_second.astype(jnp.float32), axis=0)
    small = (
        query_bias,
        value_bias,
        out_bias,
        grad_gain_one,
        grad_shift_one,
        up_bias,
        down_bias,
        grad_gain_two,
        grad_shift_two,
    )
    summed = lax.psum(
        (small[0], small[1], small[2], small[3], small[4], small[5], small[6], small[7], small[8]),
        ("batch", "tp"),
    )
    shards = (
        lax.psum_scatter(
            big[0].astype(jnp.bfloat16), "batch", scatter_dimension=0, tiled=True
        ).astype(jnp.float32),
        lax.psum_scatter(
            big[1].astype(jnp.bfloat16), "batch", scatter_dimension=0, tiled=True
        ).astype(jnp.float32),
        lax.psum_scatter(
            big[2].astype(jnp.bfloat16), "batch", scatter_dimension=0, tiled=True
        ).astype(jnp.float32),
        lax.psum_scatter(
            big[3].astype(jnp.bfloat16), "batch", scatter_dimension=1, tiled=True
        ).astype(jnp.float32),
        lax.psum_scatter(
            big[4].astype(jnp.bfloat16), "batch", scatter_dimension=0, tiled=True
        ).astype(jnp.float32),
        lax.psum_scatter(
            big[5].astype(jnp.bfloat16), "batch", scatter_dimension=1, tiled=True
        ).astype(jnp.float32),
    )
    output = result.astype(jnp.bfloat16)
    return (
        output,
        grad_tokens,
        shards[0],
        summed[0],
        shards[1],
        shards[2],
        summed[1],
        shards[3],
        summed[2],
        summed[3],
        summed[4],
        shards[4],
        summed[5],
        shards[5],
        summed[6],
        summed[7],
        summed[8],
    )


def keep_order(value, *after):
    return lax.optimization_barrier((value,) + after)[0]


def swap_core(piece):
    return lax.ppermute(piece, "tp", [(i, i ^ 1) for i in range(4)])


def swap_chip(piece):
    return lax.ppermute(piece, "tp", [(i, i ^ 2) for i in range(4)])


def swap_batch(piece, bits):
    return lax.ppermute(piece, "batch", [(i, i ^ bits) for i in range(8)])


def halves(rows):
    half = rows.shape[0] // 2
    return rows[:half], rows[half:]


def chip_sum(part):
    mine, theirs = halves(part)
    return (mine.astype(jnp.float32) + swap_core(theirs).astype(jnp.float32)).astype(jnp.bfloat16)


def both(rows):
    return jnp.concatenate([rows, swap_core(rows)], axis=0)


def relative_blocks(grad, batch_index):
    blocks = grad.astype(jnp.bfloat16).reshape(8, grad.shape[0] // 8, grad.shape[1])
    pick = lambda r: lax.dynamic_index_in_dim(blocks, batch_index ^ r, 0, keepdims=False)
    return (
        jnp.stack([pick(0), pick(2), pick(4), pick(6)]),
        jnp.stack([pick(1), pick(3), pick(5), pick(7)]),
    )


def reduce_blocks(kept, sent):
    got = swap_batch(sent, 1)
    full = kept.astype(jnp.float32) + got.astype(jnp.float32)
    low = full.astype(jnp.bfloat16)
    return (
        full[0]
        + swap_batch(low[1], 2).astype(jnp.float32)
        + swap_batch(low[2], 4).astype(jnp.float32)
        + swap_batch(low[3], 6).astype(jnp.float32)
    )


def fast_body(
    tokens,
    lengths,
    w_query,
    b_query,
    w_key,
    w_value,
    b_value,
    w_out,
    b_out,
    gain_one,
    shift_one,
    w_up,
    b_up,
    w_down,
    b_down,
    gain_two,
    shift_two,
    cotangent,
):
    scale = HEAD_DIM ** (-0.5)
    bf16, f32 = jnp.bfloat16, jnp.float32
    rows, width = tokens.shape
    tp_index = lax.axis_index("tp")
    batch_index = lax.axis_index("batch")
    core, chip = tp_index % 2, tp_index // 2
    local_width = w_query.shape[1]
    heads = local_width // HEAD_DIM
    place = jnp.arange(2 * rows, dtype=jnp.int32)
    place = (place + core * rows) % (2 * rows)
    length_own = lax.dynamic_index_in_dim(lengths, chip, 0, keepdims=False)
    length_other = lax.dynamic_index_in_dim(lengths, 1 - chip, 0, keepdims=False)

    def attention_forward(seq_rows, length):
        query = ((product(seq_rows, w_query) + b_query) * scale).astype(bf16)
        keys = product(seq_rows, w_key).astype(bf16)
        values = (product(seq_rows, w_value) + b_value).astype(bf16)
        shaped = (2 * rows, heads, HEAD_DIM)
        valid = place < length
        mixed, lse = attend_forward(
            query.reshape(shaped), keys.reshape(shaped), values.reshape(shaped), valid
        )
        mixed = mixed.reshape(2 * rows, local_width)
        return product(mixed, w_out).astype(bf16), (query, keys, values, valid, lse, mixed)

    def attention_backward(kept, grad_branch):
        query, keys, values, valid, lse, _ = kept
        shaped = (2 * rows, heads, HEAD_DIM)
        grad_mixed = against(grad_branch, w_out).astype(bf16)
        gq, gk, gv = attend_backward(
            query.reshape(shaped), keys.reshape(shaped), values.reshape(shaped), valid, lse,
            grad_mixed.reshape(shaped),
        )
        gq = (gq.astype(bf16) * scale).astype(bf16).reshape(2 * rows, local_width)
        gk = gk.astype(bf16).reshape(2 * rows, local_width)
        gv = gv.astype(bf16).reshape(2 * rows, local_width)
        part = against(gq, w_query) + against(gk, w_key) + against(gv, w_value)
        return part.astype(bf16), gq, gk, gv

    def norm_one(tok, mine, got):
        resid = tok.astype(f32) + (mine.astype(f32) + got.astype(f32) + b_out)
        return norm_forward(resid, gain_one, shift_one)

    def ffn_forward(hid):
        inner = product(hid, w_up) + b_up
        act = (inner * (0.5 * (1.0 + lax.erf(inner * 2.0 ** (-0.5))))).astype(bf16)
        slope = gelu_slope(inner).astype(bf16)
        return product(act, w_down).astype(bf16), act, slope

    def norm_two(hidden, mine, got, cot):
        resid = hidden + (mine.astype(f32) + got.astype(f32) + b_down)
        result, normed, inverse = norm_forward(resid, gain_two, shift_two)
        grad_resid, grad_gain, grad_shift = norm_backward(cot.astype(f32), normed, inverse, gain_two)
        low = grad_resid.astype(bf16)
        return result.astype(bf16), grad_resid, low, grad_gain, grad_shift, jnp.sum(low.astype(f32), axis=0)

    def ffn_backward(grad_second, slope):
        grad_inner = (against(grad_second, w_down) * slope.astype(f32)).astype(bf16)
        return against(grad_inner, w_up).astype(bf16), grad_inner

    def norm_one_back(mine, got, grad_resid_two, normed, inverse):
        grad_hidden = mine.astype(f32) + got.astype(f32) + grad_resid_two
        grad_resid, grad_gain, grad_shift = norm_backward(grad_hidden, normed, inverse, gain_one)
        low = grad_resid.astype(bf16)
        return grad_resid, low, grad_gain, grad_shift, jnp.sum(low.astype(f32), axis=0)

    tok_own = tokens
    tok_other = swap_chip(tokens)
    seq_own = both(tok_own)
    part, kept_own = attention_forward(seq_own, length_own)
    mine_own = chip_sum(part)
    got_other = swap_chip(mine_own)
    seq_other = both(tok_other)
    part, kept_other = attention_forward(seq_other, length_other)
    mine_other = chip_sum(part)
    got_own = swap_chip(mine_other)
    cot_own = cotangent
    cot_other = swap_chip(cotangent)
    hidden_other, n1_other, r1_other = norm_one(tok_other, mine_other, got_other)
    hid_other = both(hidden_other.astype(bf16))
    part, act_other, slope_other = ffn_forward(hid_other)
    mine_other = chip_sum(part)
    send_other = swap_chip(mine_other)
    hidden_own, n1_own, r1_own = norm_one(tok_own, mine_own, got_own)
    hid_own = both(hidden_own.astype(bf16))
    part, act_own, slope_own = ffn_forward(hid_own)
    mine_own = chip_sum(part)
    got_own = send_other
    got_other = swap_chip(mine_own)
    output, dr2_own, low_own, gg2_own, gs2_own, gbd_own = norm_two(hidden_own, mine_own, got_own, cot_own)
    ds_own = both(low_own)
    part, di_own = ffn_backward(ds_own, slope_own)
    mine_own = chip_sum(part)
    send_own = swap_chip(mine_own)
    _, dr2_other, low_other, gg2_other, gs2_other, gbd_other = norm_two(
        hidden_other, mine_other, got_other, cot_other
    )
    ds_other = both(low_other)
    part, di_other = ffn_backward(ds_other, slope_other)
    mine_other = chip_sum(part)
    got_other = send_own
    got_own = swap_chip(mine_other)
    act = jnp.concatenate([act_own, act_other], axis=0)
    ds = jnp.concatenate([ds_own, ds_other], axis=0)
    hid = jnp.concatenate([hid_own, hid_other], axis=0)
    di = jnp.concatenate([di_own, di_other], axis=0)
    g_down = reduce_blocks(*relative_blocks(over_rows(ds, act), batch_index))
    g_up = reduce_blocks(*relative_blocks(over_rows(hid, di), batch_index))
    dr1_other, low_other, gg1_other, gs1_other, gbo_other = norm_one_back(
        mine_other, got_other, dr2_other, n1_other, r1_other
    )
    db_other = both(low_other)
    part, gq_other, gk_other, gv_other = attention_backward(kept_other, db_other)
    mine_other = chip_sum(part)
    got_final = swap_chip(mine_other)
    dr1_own, low_own, gg1_own, gs1_own, gbo_own = norm_one_back(
        mine_own, got_own, dr2_own, n1_own, r1_own
    )
    db_own = both(low_own)
    part, gq_own, gk_own, gv_own = attention_backward(kept_own, db_own)
    mine_own = chip_sum(part)
    grad_tokens = (mine_own.astype(f32) + got_final.astype(f32) + dr1_own).astype(bf16)
    db = jnp.concatenate([db_own, db_other], axis=0)
    mixed = jnp.concatenate([kept_own[5], kept_other[5]], axis=0)
    g_out = over_rows(db, mixed)
    seq = jnp.concatenate([seq_own, seq_other], axis=0)
    gqkv = jnp.concatenate(
        [
            jnp.concatenate([gq_own, gq_other], axis=0),
            jnp.concatenate([gk_own, gk_other], axis=0),
            jnp.concatenate([gv_own, gv_other], axis=0),
        ],
        axis=1,
    )
    g_out = reduce_blocks(*relative_blocks(g_out, batch_index))
    g_qkv = reduce_blocks(*relative_blocks(over_rows(seq, gqkv), batch_index))
    shared = [
        gbo_own + gbo_other,
        gg1_own + gg1_other,
        gs1_own + gs1_other,
        gbd_own + gbd_other,
        gg2_own + gg2_other,
        gs2_own + gs2_other,
    ]
    split = [
        jnp.sum(gqkv[:, :local_width].astype(f32), axis=0),
        jnp.sum(gqkv[:, 2 * local_width :].astype(f32), axis=0),
        jnp.sum(di.astype(f32), axis=0),
    ]
    wide = []
    for item in split:
        wide.append(
            lax.dynamic_update_slice(
                jnp.zeros((4 * item.shape[0],), f32), item, (tp_index * item.shape[0],)
            )
        )
    small = jnp.concatenate([item * 0.5 for item in shared] + wide).reshape(-1, 128)
    for bits in (1, 2, 4):
        small = small + swap_batch(small, bits)
    small = small + swap_core(small)
    small = small + swap_chip(small)
    small = small.reshape(-1)
    cut = [small[i * width : (i + 1) * width] for i in range(8)]
    hidden_units = 4 * w_up.shape[1]
    g_bup = small[8 * width : 8 * width + hidden_units]
    return (
        output,
        grad_tokens,
        g_qkv[:, :local_width],
        cut[6],
        g_qkv[:, local_width : 2 * local_width],
        g_qkv[:, 2 * local_width :],
        cut[7],
        g_out.T,
        cut[0],
        cut[1],
        cut[2],
        g_up,
        g_bup,
        g_down.T,
        cut[3],
        cut[4],
        cut[5],
    )


def solution(mesh):
    fast = mesh.shape["tp"] == 4 and mesh.shape["batch"] == 8
    return jax.shard_map(
        fast_body if fast else body,
        mesh=mesh,
        in_specs=(
            P(("batch", "tp"), None),
            P("batch"),
            P(None, "tp"),
            P("tp"),
            P(None, "tp"),
            P(None, "tp"),
            P("tp"),
            P("tp", None),
            P(),
            P(),
            P(),
            P(None, "tp"),
            P("tp"),
            P("tp", None),
            P(),
            P(),
            P(),
            P(("batch", "tp"), None),
        ),
        out_specs=(
            P(("batch", "tp"), None),
            P(("batch", "tp"), None),
            P("batch", "tp"),
            P(),
            P("batch", "tp"),
            P("batch", "tp"),
            P(),
            P("tp", "batch"),
            P(),
            P(),
            P(),
            P("batch", "tp"),
            P(),
            P("tp", "batch"),
            P(),
            P(),
            P(),
        ),
        check_vma=False,
    )
```

```python
import functools
import math

import jax
import jax.numpy as jnp
from jax import lax
from jax.experimental import pallas as pl
from jax.experimental.pallas import tpu as pltpu
from jax.sharding import PartitionSpec as P

HEAD_DIM = 64


epsilon = 1e-05
negative = -1e30


def product(left, right):
    return jnp.dot(left, right, preferred_element_type=jnp.float32)


def over_rows(left, right):
    return lax.dot_general(
        left, right, (((0,), (0,)), ((), ())), preferred_element_type=jnp.float32
    )


def against(left, right):
    return lax.dot_general(
        left, right, (((1,), (1,)), ((), ())), preferred_element_type=jnp.float32
    )


def norm_forward(resid, gain, shift):
    middle = jnp.mean(resid, axis=-1, keepdims=True)
    centred = resid - middle
    variance = jnp.mean(centred * centred, axis=-1, keepdims=True)
    inverse = lax.rsqrt(variance + epsilon)
    normed = centred * inverse
    return (normed * gain + shift, normed, inverse)


def norm_backward(upstream, normed, inverse, gain):
    scaled = upstream * gain
    first = jnp.mean(scaled, axis=-1, keepdims=True)
    second = jnp.mean(scaled * normed, axis=-1, keepdims=True)
    grad_resid = inverse * (scaled - first - normed * second)
    return (grad_resid, jnp.sum(upstream * normed, axis=0), jnp.sum(upstream, axis=0))


def gelu_slope(inner):
    cumulative = 0.5 * (1.0 + lax.erf(inner * 2.0 ** (-0.5)))
    density = jnp.exp(-0.5 * inner * inner) * (2.0 * math.pi) ** (-0.5)
    return cumulative + inner * density


def attend_forward(query, keys, values, valid):
    scores = jnp.einsum("qhd,khd->hqk", query, keys, preferred_element_type=jnp.float32)
    scores = jnp.where(valid[None, None, :], scores, negative)
    highest = jnp.max(scores, axis=-1, keepdims=True)
    exponent = jnp.exp(scores - highest)
    total = jnp.sum(exponent, axis=-1, keepdims=True)
    probs = (exponent / total).astype(jnp.bfloat16)
    mixed = jnp.einsum("hqk,khd->qhd", probs, values, preferred_element_type=jnp.float32)
    return (mixed.astype(jnp.bfloat16), highest + jnp.log(total))


def attend_backward(query, keys, values, valid, log_total, grad_mixed):
    scores = jnp.einsum("qhd,khd->hqk", query, keys, preferred_element_type=jnp.float32)
    scores = jnp.where(valid[None, None, :], scores, negative)
    probs = jnp.exp(scores - log_total)
    rounded = probs.astype(jnp.bfloat16)
    grad_values = jnp.einsum(
        "hqk,qhd->khd", rounded, grad_mixed, preferred_element_type=jnp.float32
    )
    grad_probs = jnp.einsum("qhd,khd->hqk", grad_mixed, values, preferred_element_type=jnp.float32)
    centre = jnp.sum(probs * grad_probs, axis=-1, keepdims=True)
    grad_scores = (probs * (grad_probs - centre)).astype(jnp.bfloat16)
    grad_query = jnp.einsum("hqk,khd->qhd", grad_scores, keys, preferred_element_type=jnp.float32)
    grad_keys = jnp.einsum("hqk,qhd->khd", grad_scores, query, preferred_element_type=jnp.float32)
    return (grad_query, grad_keys, grad_values)


def spread(piece):
    return lax.all_gather(piece, "tp", axis=0, tiled=True)


def collect(piece):
    return lax.psum_scatter(
        piece.astype(jnp.bfloat16), "tp", scatter_dimension=0, tiled=True
    ).astype(jnp.float32)


def forward_item(item):
    return attend_forward(item[0], item[1], item[2], item[3])


def backward_item(item):
    return attend_backward(item[0], item[1], item[2], item[3], item[4], item[5])


def body(
    tokens,
    lengths,
    w_query,
    b_query,
    w_key,
    w_value,
    b_value,
    w_out,
    b_out,
    gain_one,
    shift_one,
    w_up,
    b_up,
    w_down,
    b_down,
    gain_two,
    shift_two,
    cotangent,
):
    head_dim = HEAD_DIM
    scale = head_dim ** (-0.5)
    own_rows = tokens.shape[0]
    seq_len = 2 * own_rows
    tp_index = lax.axis_index("tp")
    upstream = cotangent.astype(jnp.float32)
    gathered = spread(tokens)
    groups = gathered.shape[0] // seq_len
    local_width = w_query.shape[1]
    local_heads = local_width // head_dim
    query = ((product(gathered, w_query) + b_query) * scale).astype(jnp.bfloat16)
    keys = product(gathered, w_key).astype(jnp.bfloat16)
    values = (product(gathered, w_value) + b_value).astype(jnp.bfloat16)
    shaped = (groups, seq_len, local_heads, head_dim)
    positions = jnp.arange(seq_len, dtype=jnp.int32)
    valid = positions[None, :] < lengths[:, None]
    query_s = query.reshape(shaped)
    keys_s = keys.reshape(shaped)
    values_s = values.reshape(shaped)
    mixed_s, log_total = lax.map(forward_item, (query_s, keys_s, values_s, valid))
    mixed = mixed_s.reshape(-1, local_width)
    branch = collect(product(mixed, w_out)) + b_out
    hidden, normed_one, inverse_one = norm_forward(
        tokens.astype(jnp.float32) + branch, gain_one, shift_one
    )
    hidden_all = spread(hidden.astype(jnp.bfloat16))
    inner = product(hidden_all, w_up) + b_up
    act = jax.nn.gelu(inner, approximate=False).astype(jnp.bfloat16)
    second = collect(product(act, w_down)) + b_down
    result, normed_two, inverse_two = norm_forward(hidden + second, gain_two, shift_two)
    grad_resid_two, grad_gain_two, grad_shift_two = norm_backward(
        upstream, normed_two, inverse_two, gain_two
    )
    grad_second = grad_resid_two.astype(jnp.bfloat16)
    grad_second_all = spread(grad_second)
    grad_w_down = over_rows(act, grad_second_all)
    grad_inner = (against(grad_second_all, w_down) * gelu_slope(inner)).astype(jnp.bfloat16)
    grad_w_up = over_rows(hidden_all, grad_inner)
    grad_hidden = collect(against(grad_inner, w_up)) + grad_resid_two
    grad_resid_one, grad_gain_one, grad_shift_one = norm_backward(
        grad_hidden, normed_one, inverse_one, gain_one
    )
    grad_branch = grad_resid_one.astype(jnp.bfloat16)
    grad_branch_all = spread(grad_branch)
    grad_w_out = over_rows(mixed, grad_branch_all)
    grad_mixed = against(grad_branch_all, w_out).astype(jnp.bfloat16)
    grad_query_s, grad_keys_s, grad_values_s = lax.map(
        backward_item, (query_s, keys_s, values_s, valid, log_total, grad_mixed.reshape(shaped))
    )
    grad_query = (grad_query_s.astype(jnp.bfloat16) * scale).reshape(-1, local_width)
    grad_keys = grad_keys_s.astype(jnp.bfloat16).reshape(-1, local_width)
    grad_values = grad_values_s.astype(jnp.bfloat16).reshape(-1, local_width)
    grad_w_query = over_rows(gathered, grad_query)
    grad_w_key = over_rows(gathered, grad_keys)
    grad_w_value = over_rows(gathered, grad_values)
    grad_input_part = (
        against(grad_query, w_query) + against(grad_keys, w_key) + against(grad_values, w_value)
    )
    grad_tokens = (collect(grad_input_part) + grad_resid_one).astype(jnp.bfloat16)
    width = w_query.shape[0]
    hidden_units = w_up.shape[1] * lax.axis_size("tp")
    query_bias = lax.dynamic_update_slice(
        jnp.zeros((width,), jnp.float32),
        jnp.sum(grad_query.astype(jnp.float32), axis=0),
        (tp_index * local_width,),
    )
    value_bias = lax.dynamic_update_slice(
        jnp.zeros((width,), jnp.float32),
        jnp.sum(grad_values.astype(jnp.float32), axis=0),
        (tp_index * local_width,),
    )
    up_bias = lax.dynamic_update_slice(
        jnp.zeros((hidden_units,), jnp.float32),
        jnp.sum(grad_inner.astype(jnp.float32), axis=0),
        (tp_index * w_up.shape[1],),
    )
    big = (grad_w_query, grad_w_key, grad_w_value, grad_w_out, grad_w_up, grad_w_down)
    out_bias = jnp.sum(grad_branch.astype(jnp.float32), axis=0)
    down_bias = jnp.sum(grad_second.astype(jnp.float32), axis=0)
    small = (
        query_bias,
        value_bias,
        out_bias,
        grad_gain_one,
        grad_shift_one,
        up_bias,
        down_bias,
        grad_gain_two,
        grad_shift_two,
    )
    summed = lax.psum(
        (small[0], small[1], small[2], small[3], small[4], small[5], small[6], small[7], small[8]),
        ("batch", "tp"),
    )
    shards = (
        lax.psum_scatter(
            big[0].astype(jnp.bfloat16), "batch", scatter_dimension=0, tiled=True
        ).astype(jnp.float32),
        lax.psum_scatter(
            big[1].astype(jnp.bfloat16), "batch", scatter_dimension=0, tiled=True
        ).astype(jnp.float32),
        lax.psum_scatter(
            big[2].astype(jnp.bfloat16), "batch", scatter_dimension=0, tiled=True
        ).astype(jnp.float32),
        lax.psum_scatter(
            big[3].astype(jnp.bfloat16), "batch", scatter_dimension=1, tiled=True
        ).astype(jnp.float32),
        lax.psum_scatter(
            big[4].astype(jnp.bfloat16), "batch", scatter_dimension=0, tiled=True
        ).astype(jnp.float32),
        lax.psum_scatter(
            big[5].astype(jnp.bfloat16), "batch", scatter_dimension=1, tiled=True
        ).astype(jnp.float32),
    )
    output = result.astype(jnp.bfloat16)
    return (
        output,
        grad_tokens,
        shards[0],
        summed[0],
        shards[1],
        shards[2],
        summed[1],
        shards[3],
        summed[2],
        summed[3],
        summed[4],
        shards[4],
        summed[5],
        shards[5],
        summed[6],
        summed[7],
        summed[8],
    )


def swap_core(piece):
    return lax.ppermute(piece, "tp", [(i, i ^ 1) for i in range(4)])


def swap_chip(piece):
    return lax.ppermute(piece, "tp", [(i, i ^ 2) for i in range(4)])


def swap_batch(piece, bits):
    return lax.ppermute(piece, "batch", [(i, i ^ bits) for i in range(8)])


MEBI = 1024 * 1024
PIECES = 2


def run_kernel(kernel, inputs, outputs, after=(), scalars=(), hbm=(), through=(), scratch=(), final=(), limit=16):
    read = len(scalars) + len(hbm) + len(inputs)
    first = read + len(after)

    def wrapped(*refs):
        outs = refs[first + len(through) :]
        kernel(*refs[:read], *outs[: len(outputs)], *outs[len(outputs) + len(through) :])

    return pl.pallas_call(
        wrapped,
        out_shape=[
            jax.ShapeDtypeStruct(shape, kind) if i in final else pltpu.VMEM(shape, kind)
            for i, (shape, kind) in enumerate(outputs)
        ]
        + [jax.ShapeDtypeStruct(item.shape, item.dtype) for item in through],
        in_specs=[pl.BlockSpec(memory_space=pltpu.SMEM)] * len(scalars)
        + [pl.BlockSpec(memory_space=pltpu.HBM)] * len(hbm)
        + [pl.BlockSpec(memory_space=pltpu.VMEM)] * len(inputs)
        + [pl.BlockSpec(memory_space=pl.ANY)] * (len(after) + len(through)),
        out_specs=[pl.BlockSpec(memory_space=pltpu.VMEM)] * len(outputs)
        + [pl.BlockSpec(memory_space=pl.ANY)] * len(through),
        input_output_aliases={first + i: len(outputs) + i for i in range(len(through))},
        scratch_shapes=list(scratch),
        compiler_params=pltpu.CompilerParams(vmem_limit_bytes=limit * MEBI),
        cost_estimate=pl.CostEstimate(flops=1, bytes_accessed=1, transcendentals=0),
    )(*scalars, *[pltpu.with_memory_space_constraint(item, pltpu.HBM) for item in hbm], *inputs, *after, *through)


def fetch(sources, targets, sems):
    copies = [pltpu.make_async_copy(a, b, sems.at[i]) for i, (a, b) in enumerate(zip(sources, targets))]
    for copy in copies:
        copy.start()
    return copies


def wide(ref):
    return ref[...].astype(jnp.float32)


def joined(refs):
    return refs[0][...] if len(refs) == 1 else jnp.concatenate([ref[...] for ref in refs], axis=0)


def cut_rows(whole, refs):
    at = 0
    for ref in refs:
        ref[...] = whole[at : at + ref.shape[0]]
        at += ref.shape[0]


def valid_slots(shape, axis, which, lengths):
    seq = shape[axis]
    tp_index = lax.axis_index("tp")
    slot = lax.broadcasted_iota(jnp.int32, shape, axis) + (tp_index % 2) * (seq // 2)
    slot = jnp.where(slot >= seq, slot - seq, slot)
    return slot < lengths[(tp_index // 2) ^ which]


def attention_forward_kernel(which, lengths, wq_hbm, wk_hbm, wv_hbm, wo_hbm, bq, bv, xm, xc, *refs):
    q_ref, k_ref, v_ref, lse_ref, mixed_ref, pm_ref, *pc_refs = refs[: 6 + PIECES]
    wq, wk, wv, wo, sems = refs[6 + PIECES :]
    copies = fetch((wq_hbm, wk_hbm, wv_hbm, wo_hbm), (wq, wk, wv, wo), sems)
    rows = xm.shape[0]
    seq = 2 * rows
    local = wq.shape[1]
    scale = HEAD_DIM ** (-0.5)
    copies[0].wait()
    for i, x in enumerate((xm, xc)):
        part = pl.ds(i * rows, rows)
        q_ref[part, :] = ((product(x[...], wq[...]) + wide(bq)) * scale).astype(jnp.bfloat16)
    copies[1].wait()
    copies[2].wait()
    for i, x in enumerate((xm, xc)):
        part = pl.ds(i * rows, rows)
        k_ref[part, :] = product(x[...], wk[...]).astype(jnp.bfloat16)
        v_ref[part, :] = (product(x[...], wv[...]) + wide(bv)).astype(jnp.bfloat16)
    valid = valid_slots((1, seq), 1, which, lengths)
    lane = lax.broadcasted_iota(jnp.int32, (seq, 128), 1)
    lse_all = jnp.zeros((seq, 128), jnp.float32)
    for h in range(local // HEAD_DIM):
        cut = slice(h * HEAD_DIM, (h + 1) * HEAD_DIM)
        scores = jnp.where(valid, against(q_ref[:, cut], k_ref[:, cut]), negative)
        highest = jnp.max(scores, axis=-1, keepdims=True)
        exponent = jnp.exp(scores - highest)
        total = jnp.sum(exponent, axis=-1, keepdims=True)
        probs = (exponent * (1.0 / total)).astype(jnp.bfloat16)
        mixed_ref[:, cut] = product(probs, v_ref[:, cut]).astype(jnp.bfloat16)
        lse_all = jnp.where(lane == h, highest + jnp.log(total), lse_all)
    lse_ref[...] = lse_all.T[:8, :]
    copies[3].wait()
    cut_rows(product(mixed_ref[rows:, :], wo[...]).astype(jnp.bfloat16), pc_refs)
    pm_ref[...] = product(mixed_ref[:rows, :], wo[...]).astype(jnp.bfloat16)


def attention_backward_kernel(which, lengths, wo_hbm, wq_hbm, wk_hbm, wv_hbm, *refs):
    db, refs = refs[: 2 * PIECES], refs[2 * PIECES :]
    q_ref, k_ref, v_ref, lse_ref, mixed_ref, g_ref, bias_ref, pm_ref, *pc_refs = refs[: 8 + PIECES]
    wo, wq, wk, wv, sems, dm_ref = refs[8 + PIECES :]
    copies = fetch((wo_hbm, wq_hbm, wk_hbm, wv_hbm), (wo, wq, wk, wv), sems)
    seq, local = q_ref.shape
    rows = seq // 2
    scale = HEAD_DIM ** (-0.5)
    copies[0].wait()
    for i in range(2):
        grad = joined(db[i * PIECES : (i + 1) * PIECES])
        dm_ref[i * rows : (i + 1) * rows, :] = against(grad, wo[...]).astype(jnp.bfloat16)
    crossed = (wide(dm_ref) * wide(mixed_ref)).T
    valid = valid_slots((seq, 1), 0, which, lengths)
    for h in range(local // HEAD_DIM):
        cut = slice(h * HEAD_DIM, (h + 1) * HEAD_DIM)
        q, k, v, dm = q_ref[:, cut], k_ref[:, cut], v_ref[:, cut], dm_ref[:, cut]
        centre = jnp.sum(crossed[cut, :], axis=0, keepdims=True)
        scores = jnp.where(valid, against(k, q), negative)
        probs = jnp.exp(scores - lse_ref[h : h + 1, :])
        g_ref[:, 2 * local + h * HEAD_DIM : 2 * local + (h + 1) * HEAD_DIM] = product(
            probs.astype(jnp.bfloat16), dm
        ).astype(jnp.bfloat16)
        grad = (probs * (against(v, dm) - centre)).astype(jnp.bfloat16)
        g_ref[:, local + h * HEAD_DIM : local + (h + 1) * HEAD_DIM] = product(grad, q).astype(jnp.bfloat16)
        grad_q = product(k.T, grad).astype(jnp.bfloat16) * scale
        g_ref[:, cut] = grad_q.T.astype(jnp.bfloat16)
    bias_ref[...] = jnp.sum(wide(g_ref), axis=0, keepdims=True)
    for copy in copies[1:]:
        copy.wait()
    for i in (1, 0):
        part = slice(i * rows, (i + 1) * rows)
        total = (
            against(g_ref[part, :local], wq[...])
            + against(g_ref[part, local : 2 * local], wk[...])
            + against(g_ref[part, 2 * local :], wv[...])
        ).astype(jnp.bfloat16)
        cut_rows(total, pc_refs if i else [pm_ref])


def feed_forward_kernel(*refs):
    h, refs = refs[: 2 * PIECES], refs[2 * PIECES :]
    wu, bu, wd, act_ref, slope_ref, pm_ref, *pc_refs = refs
    units = wu.shape[1]
    step = 256
    for i in (1, 0):
        x = joined(h[i * PIECES : (i + 1) * PIECES])
        rows = x.shape[0]
        part = slice(i * rows, (i + 1) * rows)
        total = jnp.zeros(x.shape, jnp.float32)
        for j in range(units // step):
            cut = slice(j * step, (j + 1) * step)
            inner = product(x, wu[:, cut]) + bu[:, cut].astype(jnp.float32)
            cumulative = 0.5 * (1.0 + lax.erf(inner * 2.0 ** (-0.5)))
            density = jnp.exp(-0.5 * inner * inner) * (2.0 * math.pi) ** (-0.5)
            act = (inner * cumulative).astype(jnp.bfloat16)
            act_ref[part, cut] = act
            slope_ref[part, cut] = (cumulative + inner * density).astype(jnp.bfloat16)
            total = total + product(act, wd[cut, :])
        cut_rows(total.astype(jnp.bfloat16), pc_refs if i else [pm_ref])


def feed_backward_kernel(*refs):
    d, refs = refs[: 2 * PIECES], refs[2 * PIECES :]
    slope, wd, wu, grad_ref, bias_ref, pm_ref, *pc_refs = refs
    units = wu.shape[1]
    step = 256
    for i in (1, 0):
        x = joined(d[i * PIECES : (i + 1) * PIECES])
        rows = x.shape[0]
        part = slice(i * rows, (i + 1) * rows)
        total = jnp.zeros(x.shape, jnp.float32)
        for j in range(units // step):
            cut = slice(j * step, (j + 1) * step)
            grad = (against(x, wd[cut, :]) * slope[part, cut].astype(jnp.float32)).astype(jnp.bfloat16)
            grad_ref[part, cut] = grad
            total = total + against(grad, wu[:, cut])
        cut_rows(total.astype(jnp.bfloat16), pc_refs if i else [pm_ref])
    bias_ref[...] = jnp.sum(wide(grad_ref), axis=0, keepdims=True)


def weight_grad_kernel(order, count, columns, *refs):
    lefts, (r0, r1, keep_ref, send_ref, left_ref, low_ref) = refs[:count], refs[count:]
    at = 0
    for left in lefts:
        left_ref[:, at : at + left.shape[0]] = left[...].T
        at += left.shape[0]
    half = r0.shape[0]
    me = lax.axis_index("batch")
    block = low_ref.shape[0] // 8
    step = 256
    for j in range(low_ref.shape[1] // step):
        cut = slice(j * step, (j + 1) * step)
        taken = slice(columns + j * step, columns + (j + 1) * step)
        total = product(left_ref[:, :half], r0[:, taken]) + product(left_ref[:, half:], r1[:, taken])
        low_ref[:, cut] = total.astype(jnp.bfloat16)
        for place in range(8):
            bits = [(place >> bit) & 1 for bit in (2, 1, 0)]
            r = sum(value << bit for value, bit in zip(bits, order))
            rows = pl.ds(pl.multiple_of((me ^ r) * block, block), block)
            out = send_ref if bits[0] else keep_ref
            out[place % 4, :, cut] = low_ref[rows, cut]


def chip_sum_kernel(mine, *refs):
    *got, out_ref = refs
    out_ref[...] = (wide(mine) + joined(got).astype(jnp.float32)).astype(jnp.bfloat16)


def last_sum_kernel(mine, *refs):
    *got, other, resid, out_ref = refs
    out_ref[...] = (wide(mine) + joined(got).astype(jnp.float32) + wide(other) + resid[...]).astype(jnp.bfloat16)


def norm_one_kernel(tok, mine, got, bias, gain, shift, hidden_ref, normed_ref, inverse_ref, *low_refs):
    resid = wide(tok) + (wide(mine) + wide(got) + wide(bias))
    hidden, normed, inverse = norm_forward(resid, gain[...], shift[...])
    hidden_ref[...] = hidden
    normed_ref[...] = normed
    inverse_ref[...] = inverse
    cut_rows(hidden.astype(jnp.bfloat16), low_refs)


def norm_two_kernel(hidden, mine, got, bias, gain, shift, cot, out_ref, grad_ref, sums_ref, *low_refs):
    resid = hidden[...] + (wide(mine) + wide(got) + wide(bias))
    result, normed, inverse = norm_forward(resid, gain[...], shift[...])
    out_ref[...] = result.astype(jnp.bfloat16)
    grad, gain_sum, shift_sum = norm_backward(wide(cot), normed, inverse, gain[...])
    low = grad.astype(jnp.bfloat16)
    grad_ref[...] = grad
    cut_rows(low, low_refs)
    sums_ref[0:1, :] = gain_sum[None]
    sums_ref[1:2, :] = shift_sum[None]
    sums_ref[2:3, :] = jnp.sum(low.astype(jnp.float32), axis=0, keepdims=True)


def norm_one_back_kernel(count, mine, got, *refs):
    resid, (normed, inverse, gain, grad_ref, sums_ref, *low_refs) = refs[:count], refs[count:]
    upstream = wide(mine) + wide(got) + joined(resid).astype(jnp.float32)
    grad, gain_sum, shift_sum = norm_backward(upstream, normed[...], inverse[...], gain[...])
    low = grad.astype(jnp.bfloat16)
    grad_ref[...] = grad
    cut_rows(low, low_refs)
    sums_ref[0:1, :] = gain_sum[None]
    sums_ref[1:2, :] = shift_sum[None]
    sums_ref[2:3, :] = jnp.sum(low.astype(jnp.float32), axis=0, keepdims=True)


def fold_kernel(turn, keep, got, *out):
    count = keep.shape[0]
    if count == 1:
        full = keep[0].astype(jnp.float32) + got[0].astype(jnp.float32)
        full = full.T if turn else full
        at = 0
        for ref in out:
            ref[...] = full[:, at : at + ref.shape[1]]
            at += ref.shape[1]
        return
    for r in range(count):
        full = keep[r].astype(jnp.float32) + got[r].astype(jnp.float32)
        out[(2 * r) // count][r % (count // 2)] = full.astype(jnp.bfloat16)


def pack_kernel(one, two, bias0, bias1, up0, up1, out_ref):
    tp_index = lax.axis_index("tp")
    out_ref[...] = jnp.zeros(out_ref.shape, jnp.float32)
    out_ref[0:3, :] = one[0:3, :]
    out_ref[3:6, :] = two[0:3, :]
    local = bias0.shape[1] // 3
    lanes = pl.ds(pl.multiple_of(tp_index * local, 128), local)
    bias = bias0[...] + bias1[...]
    out_ref[6:7, lanes] = bias[:, :local]
    out_ref[7:8, lanes] = bias[:, 2 * local :]
    out_ref[pl.ds(8 + tp_index, 1), :] = up0[...] + up1[...]


def add_kernel(a, b, out_ref):
    out_ref[...] = a[...] + b[...]


def fast_body(
    tokens,
    lengths,
    w_query,
    b_query,
    w_key,
    w_value,
    b_value,
    w_out,
    b_out,
    gain_one,
    shift_one,
    w_up,
    b_up,
    w_down,
    b_down,
    gain_two,
    shift_two,
    cotangent,
):
    bf16, f32 = jnp.bfloat16, jnp.float32
    rows, width = tokens.shape
    seq = 2 * rows
    local = w_query.shape[1]
    units = w_up.shape[1]
    row = lambda item: item.reshape(1, -1)
    piece_rows = [((rows // PIECES, width), bf16)] * PIECES
    part_rows = [((rows, width), bf16)] + piece_rows

    def attention_forward(which, xm, xc, after=()):
        return run_kernel(
            functools.partial(attention_forward_kernel, which),
            (row(b_query), row(b_value), xm, xc),
            [((seq, local), bf16)] * 3 + [((8, seq), f32), ((seq, local), bf16)] + part_rows,
            after, (lengths,), (w_query, w_key, w_value, w_out),
            scratch=[pltpu.VMEM((width, local), bf16)] * 3
            + [pltpu.VMEM((local, width), bf16), pltpu.SemaphoreType.DMA((4,))],
        )

    def attention_backward(which, db, kept, after=()):
        return run_kernel(
            functools.partial(attention_backward_kernel, which),
            (*db, *kept),
            [((seq, 3 * local), bf16), ((1, 3 * local), f32)] + part_rows,
            after, (lengths,), (w_out, w_query, w_key, w_value),
            scratch=[pltpu.VMEM((local, width), bf16)]
            + [pltpu.VMEM((width, local), bf16)] * 3
            + [pltpu.SemaphoreType.DMA((4,)), pltpu.VMEM((seq, local), bf16)],
        )

    def feed_forward(h, after=()):
        return run_kernel(
            feed_forward_kernel, (*h, w_up, row(b_up), w_down), [((seq, units), bf16)] * 2 + part_rows, after
        )

    def feed_backward(d, slope, after=()):
        return run_kernel(
            feed_backward_kernel,
            (*d, slope, w_down, w_up),
            [((seq, units), bf16), ((1, units), f32)] + part_rows,
            after,
        )

    def weight_grad(order, lefts, rights, columns=0, n=None, after=()):
        n = n or rights[0].shape[1]
        return run_kernel(
            functools.partial(weight_grad_kernel, order, len(lefts), columns),
            (*lefts, *rights),
            [((4, width // 8, n), bf16)] * 2,
            after,
            scratch=[pltpu.VMEM((width, 4 * rows), bf16), pltpu.VMEM((width, n), bf16)],
        )

    def chip_sum(mine, *theirs, through=()):
        return run_kernel(
            chip_sum_kernel, (mine, *map(swap_core, theirs)), [((rows, width), bf16)], through=through
        )

    def norm_one(tok, mine, got, after=()):
        return run_kernel(
            norm_one_kernel,
            (tok, mine, got, row(b_out), row(gain_one), row(shift_one)),
            [((rows, width), f32), ((rows, width), f32), ((rows, 1), f32)] + piece_rows,
            after,
        )

    def norm_two(hidden, mine, got, after=()):
        return run_kernel(
            norm_two_kernel,
            (hidden, mine, got, row(b_down), row(gain_two), row(shift_two), cotangent),
            [((rows, width), bf16), ((rows, width), f32), ((8, width), f32)] + piece_rows,
            after, final=(0,),
        )

    def norm_one_back(mine, got, resid, normed, inverse, after=()):
        return run_kernel(
            functools.partial(norm_one_back_kernel, len(resid)),
            (mine, got, *resid, normed, inverse, row(gain_one)),
            [((rows, width), f32), ((8, width), f32)] + piece_rows,
            after,
        )

    def fold(keep, got, after=()):
        count, block, n = keep.shape
        return run_kernel(
            functools.partial(fold_kernel, False), (keep, got), [((count // 2, block, n), bf16)] * 2, after
        )

    def fold_last(keep, got, after=(), turn=False, parts=1):
        _, block, n = keep.shape
        shape = (n, block) if turn else (block, n // parts)
        return run_kernel(
            functools.partial(fold_kernel, turn), (keep, got), [(shape, f32)] * parts, after, final=range(parts)
        )

    def add(a, b, after=(), final=()):
        return run_kernel(add_kernel, (a, b), [(a.shape, f32)], after, final=final)[0]

    def both(low):
        return (*low, *map(swap_core, low))

    Y, Z1, Z2 = 1, 2, 4
    y_first, z_first = (0, 1, 2), (1, 2, 0)
    tok_other = swap_chip(tokens)
    tok_own_c = swap_core(tokens)
    *kept_own, pm, pc0, pc1 = attention_forward(0, tokens, tok_own_c)
    mine_own, tok_other = chip_sum(pm, pc0, pc1, through=(tok_other,))
    from_own = swap_chip(mine_own)
    tok_other_c = swap_core(tok_other)
    *kept_other, pm, pc0, pc1 = attention_forward(1, tok_other, tok_other_c)
    mine_other, = chip_sum(pm, pc0, pc1)
    from_other = swap_chip(mine_other)
    hidden_other, n1_other, r1_other, *low = norm_one(tok_other, mine_other, from_own)
    hid_other = both(low)
    act_other, slope_other, *part = feed_forward(hid_other)
    mine_other, = chip_sum(*part)
    got_own = swap_chip(mine_other)
    hidden_own, n1_own, r1_own, *low = norm_one(tokens, mine_own, from_other, (mine_other,))
    hid_own = both(low)
    act_own, slope_own, *part = feed_forward(hid_own)
    mine_own, = chip_sum(*part)
    output, dr2_own, sums_two, *low = norm_two(hidden_own, mine_own, got_own)
    low_other = [swap_chip(item) for item in low]
    ds_own = both(low)
    di_own, bup_own, *part = feed_backward(ds_own, slope_own)
    mine_own, = chip_sum(*part)
    from_own = swap_chip(mine_own)
    ds_other = both(low_other)
    di_other, bup_other, *part = feed_backward(ds_other, slope_other, (mine_own,))
    mine_other, = chip_sum(*part)
    from_other = swap_chip(mine_other)
    down = weight_grad(y_first, (*ds_own, *ds_other), (act_own, act_other), after=(mine_other,))
    down_got = swap_batch(down[1], Y)
    _, _, *low = norm_one_back(mine_other, from_own, low_other, n1_other, r1_other, down[:1])
    up = weight_grad(z_first, (*hid_own, *hid_other), (di_own, di_other), after=(low[0],))
    up_got = swap_batch(up[1], Z1)
    db_other = both(low)
    gqkv_other, bias_other, *part = attention_backward(1, db_other, kept_other, up[:1])
    mine_other, = chip_sum(*part)
    got_final = swap_chip(mine_other)
    dr1_own, sums_one, *low = norm_one_back(mine_own, from_other, (dr2_own,), n1_own, r1_own, (mine_other,))
    db_own = both(low)
    down = fold(down[0], down_got, (low[0],))
    down_got = swap_batch(down[1], Z1)
    out = weight_grad(z_first, (*db_own, *db_other), (kept_own[4], kept_other[4]), after=down[:1])
    out_got = swap_batch(out[1], Z1)
    up = fold(up[0], up_got, out[:1])
    up_got = swap_batch(up[1], Z2)
    gqkv_own, bias_own, *part = attention_backward(0, db_own, kept_own, up[:1])
    small = run_kernel(
        pack_kernel, (sums_one, sums_two, bias_own, bias_other, bup_own, bup_other), [((16, width), f32)]
    )[0]
    small_got = swap_batch(small, Y)
    seqs = (tokens, tok_own_c, tok_other, tok_other_c)
    val = weight_grad(z_first, seqs, (gqkv_own, gqkv_other), 2 * local, local, (small,))
    val_got = swap_batch(val[1], Z1)
    qk = weight_grad(y_first, seqs, (gqkv_own, gqkv_other), 0, 2 * local, val[:1])
    qk_got = swap_batch(qk[1], Y)
    down = fold(down[0], down_got, qk[:1])
    down_got = swap_batch(down[1], Z2)
    out = fold(out[0], out_got, down[:1])
    out_got = swap_batch(out[1], Z2)
    small = add(small, small_got, out[:1])
    small_got = swap_batch(small, Z1)
    grad_tokens, = run_kernel(
        last_sum_kernel,
        (part[0], *map(swap_core, part[1:]), got_final, dr1_own),
        [((rows, width), bf16)], (small,), final=(0,),
    )
    up = fold(up[0], up_got, (small,))
    up_got = swap_batch(up[1], Y)
    val = fold(val[0], val_got, up[:1])
    val_got = swap_batch(val[1], Z2)
    small = add(small, small_got, val[:1])
    small_got = swap_batch(small, Z2)
    qk = fold(qk[0], qk_got, (small,))
    qk_got = swap_batch(qk[1], Z1)
    g_down, = fold_last(down[0], down_got, qk[:1], turn=True)
    out = fold(out[0], out_got, (g_down,))
    out_got = swap_batch(out[1], Y)
    g_up, = fold_last(up[0], up_got, out[:1])
    small = add(small, small_got, (g_up,))
    small_got = swap_core(small)
    val = fold(val[0], val_got, (small,))
    val_got = swap_batch(val[1], Y)
    qk = fold(qk[0], qk_got, val[:1])
    qk_got = swap_batch(qk[1], Z2)
    small = add(small, small_got, qk[:1])
    small_got = swap_chip(small)
    g_out, = fold_last(out[0], out_got, (small,), turn=True)
    g_value, = fold_last(val[0], val_got, (g_out,))
    small = add(small, small_got, (g_value,), final=(0,))
    g_query, g_key = fold_last(qk[0], qk_got, (small,), parts=2)
    return (
        output,
        grad_tokens,
        g_query,
        small[6],
        g_key,
        g_value,
        small[7],
        g_out,
        small[2],
        small[0],
        small[1],
        g_up,
        small[8:12].reshape(-1),
        g_down,
        small[5],
        small[3],
        small[4],
    )


def solution(mesh):
    fast = mesh.shape["tp"] == 4 and mesh.shape["batch"] == 8
    return jax.shard_map(
        fast_body if fast else body,
        mesh=mesh,
        in_specs=(
            P(("batch", "tp"), None),
            P("batch"),
            P(None, "tp"),
            P("tp"),
            P(None, "tp"),
            P(None, "tp"),
            P("tp"),
            P("tp", None),
            P(),
            P(),
            P(),
            P(None, "tp"),
            P("tp"),
            P("tp", None),
            P(),
            P(),
            P(),
            P(("batch", "tp"), None),
        ),
        out_specs=(
            P(("batch", "tp"), None),
            P(("batch", "tp"), None),
            P("batch", "tp"),
            P(),
            P("batch", "tp"),
            P("batch", "tp"),
            P(),
            P("tp", "batch"),
            P(),
            P(),
            P(),
            P("batch", "tp"),
            P(),
            P("tp", "batch"),
            P(),
            P(),
            P(),
        ),
        check_vma=False,
    )
```

```python
import functools
import math

import jax
import jax.numpy as jnp
from jax import lax
from jax.experimental import pallas as pl
from jax.experimental.pallas import tpu as pltpu
from jax.sharding import PartitionSpec as P

HEAD_DIM = 64


epsilon = 1e-05
negative = -1e30


def product(left, right):
    return jnp.dot(left, right, preferred_element_type=jnp.float32)


def over_rows(left, right):
    return lax.dot_general(
        left, right, (((0,), (0,)), ((), ())), preferred_element_type=jnp.float32
    )


def against(left, right):
    return lax.dot_general(
        left, right, (((1,), (1,)), ((), ())), preferred_element_type=jnp.float32
    )


def norm_forward(resid, gain, shift):
    middle = jnp.mean(resid, axis=-1, keepdims=True)
    centred = resid - middle
    variance = jnp.mean(centred * centred, axis=-1, keepdims=True)
    inverse = lax.rsqrt(variance + epsilon)
    normed = centred * inverse
    return (normed * gain + shift, normed, inverse)


def norm_backward(upstream, normed, inverse, gain):
    scaled = upstream * gain
    first = jnp.mean(scaled, axis=-1, keepdims=True)
    second = jnp.mean(scaled * normed, axis=-1, keepdims=True)
    grad_resid = inverse * (scaled - first - normed * second)
    return (grad_resid, jnp.sum(upstream * normed, axis=0), jnp.sum(upstream, axis=0))


def gelu_slope(inner):
    cumulative = 0.5 * (1.0 + lax.erf(inner * 2.0 ** (-0.5)))
    density = jnp.exp(-0.5 * inner * inner) * (2.0 * math.pi) ** (-0.5)
    return cumulative + inner * density


def attend_forward(query, keys, values, valid):
    scores = jnp.einsum("qhd,khd->hqk", query, keys, preferred_element_type=jnp.float32)
    scores = jnp.where(valid[None, None, :], scores, negative)
    highest = jnp.max(scores, axis=-1, keepdims=True)
    exponent = jnp.exp(scores - highest)
    total = jnp.sum(exponent, axis=-1, keepdims=True)
    probs = (exponent / total).astype(jnp.bfloat16)
    mixed = jnp.einsum("hqk,khd->qhd", probs, values, preferred_element_type=jnp.float32)
    return (mixed.astype(jnp.bfloat16), highest + jnp.log(total))


def attend_backward(query, keys, values, valid, log_total, grad_mixed):
    scores = jnp.einsum("qhd,khd->hqk", query, keys, preferred_element_type=jnp.float32)
    scores = jnp.where(valid[None, None, :], scores, negative)
    probs = jnp.exp(scores - log_total)
    rounded = probs.astype(jnp.bfloat16)
    grad_values = jnp.einsum(
        "hqk,qhd->khd", rounded, grad_mixed, preferred_element_type=jnp.float32
    )
    grad_probs = jnp.einsum("qhd,khd->hqk", grad_mixed, values, preferred_element_type=jnp.float32)
    centre = jnp.sum(probs * grad_probs, axis=-1, keepdims=True)
    grad_scores = (probs * (grad_probs - centre)).astype(jnp.bfloat16)
    grad_query = jnp.einsum("hqk,khd->qhd", grad_scores, keys, preferred_element_type=jnp.float32)
    grad_keys = jnp.einsum("hqk,qhd->khd", grad_scores, query, preferred_element_type=jnp.float32)
    return (grad_query, grad_keys, grad_values)


def spread(piece):
    return lax.all_gather(piece, "tp", axis=0, tiled=True)


def collect(piece):
    return lax.psum_scatter(
        piece.astype(jnp.bfloat16), "tp", scatter_dimension=0, tiled=True
    ).astype(jnp.float32)


def forward_item(item):
    return attend_forward(item[0], item[1], item[2], item[3])


def backward_item(item):
    return attend_backward(item[0], item[1], item[2], item[3], item[4], item[5])


def body(
    tokens,
    lengths,
    w_query,
    b_query,
    w_key,
    w_value,
    b_value,
    w_out,
    b_out,
    gain_one,
    shift_one,
    w_up,
    b_up,
    w_down,
    b_down,
    gain_two,
    shift_two,
    cotangent,
):
    head_dim = HEAD_DIM
    scale = head_dim ** (-0.5)
    own_rows = tokens.shape[0]
    seq_len = 2 * own_rows
    tp_index = lax.axis_index("tp")
    upstream = cotangent.astype(jnp.float32)
    gathered = spread(tokens)
    groups = gathered.shape[0] // seq_len
    local_width = w_query.shape[1]
    local_heads = local_width // head_dim
    query = ((product(gathered, w_query) + b_query) * scale).astype(jnp.bfloat16)
    keys = product(gathered, w_key).astype(jnp.bfloat16)
    values = (product(gathered, w_value) + b_value).astype(jnp.bfloat16)
    shaped = (groups, seq_len, local_heads, head_dim)
    positions = jnp.arange(seq_len, dtype=jnp.int32)
    valid = positions[None, :] < lengths[:, None]
    query_s = query.reshape(shaped)
    keys_s = keys.reshape(shaped)
    values_s = values.reshape(shaped)
    mixed_s, log_total = lax.map(forward_item, (query_s, keys_s, values_s, valid))
    mixed = mixed_s.reshape(-1, local_width)
    branch = collect(product(mixed, w_out)) + b_out
    hidden, normed_one, inverse_one = norm_forward(
        tokens.astype(jnp.float32) + branch, gain_one, shift_one
    )
    hidden_all = spread(hidden.astype(jnp.bfloat16))
    inner = product(hidden_all, w_up) + b_up
    act = jax.nn.gelu(inner, approximate=False).astype(jnp.bfloat16)
    second = collect(product(act, w_down)) + b_down
    result, normed_two, inverse_two = norm_forward(hidden + second, gain_two, shift_two)
    grad_resid_two, grad_gain_two, grad_shift_two = norm_backward(
        upstream, normed_two, inverse_two, gain_two
    )
    grad_second = grad_resid_two.astype(jnp.bfloat16)
    grad_second_all = spread(grad_second)
    grad_w_down = over_rows(act, grad_second_all)
    grad_inner = (against(grad_second_all, w_down) * gelu_slope(inner)).astype(jnp.bfloat16)
    grad_w_up = over_rows(hidden_all, grad_inner)
    grad_hidden = collect(against(grad_inner, w_up)) + grad_resid_two
    grad_resid_one, grad_gain_one, grad_shift_one = norm_backward(
        grad_hidden, normed_one, inverse_one, gain_one
    )
    grad_branch = grad_resid_one.astype(jnp.bfloat16)
    grad_branch_all = spread(grad_branch)
    grad_w_out = over_rows(mixed, grad_branch_all)
    grad_mixed = against(grad_branch_all, w_out).astype(jnp.bfloat16)
    grad_query_s, grad_keys_s, grad_values_s = lax.map(
        backward_item, (query_s, keys_s, values_s, valid, log_total, grad_mixed.reshape(shaped))
    )
    grad_query = (grad_query_s.astype(jnp.bfloat16) * scale).reshape(-1, local_width)
    grad_keys = grad_keys_s.astype(jnp.bfloat16).reshape(-1, local_width)
    grad_values = grad_values_s.astype(jnp.bfloat16).reshape(-1, local_width)
    grad_w_query = over_rows(gathered, grad_query)
    grad_w_key = over_rows(gathered, grad_keys)
    grad_w_value = over_rows(gathered, grad_values)
    grad_input_part = (
        against(grad_query, w_query) + against(grad_keys, w_key) + against(grad_values, w_value)
    )
    grad_tokens = (collect(grad_input_part) + grad_resid_one).astype(jnp.bfloat16)
    width = w_query.shape[0]
    hidden_units = w_up.shape[1] * lax.axis_size("tp")
    query_bias = lax.dynamic_update_slice(
        jnp.zeros((width,), jnp.float32),
        jnp.sum(grad_query.astype(jnp.float32), axis=0),
        (tp_index * local_width,),
    )
    value_bias = lax.dynamic_update_slice(
        jnp.zeros((width,), jnp.float32),
        jnp.sum(grad_values.astype(jnp.float32), axis=0),
        (tp_index * local_width,),
    )
    up_bias = lax.dynamic_update_slice(
        jnp.zeros((hidden_units,), jnp.float32),
        jnp.sum(grad_inner.astype(jnp.float32), axis=0),
        (tp_index * w_up.shape[1],),
    )
    big = (grad_w_query, grad_w_key, grad_w_value, grad_w_out, grad_w_up, grad_w_down)
    out_bias = jnp.sum(grad_branch.astype(jnp.float32), axis=0)
    down_bias = jnp.sum(grad_second.astype(jnp.float32), axis=0)
    small = (
        query_bias,
        value_bias,
        out_bias,
        grad_gain_one,
        grad_shift_one,
        up_bias,
        down_bias,
        grad_gain_two,
        grad_shift_two,
    )
    summed = lax.psum(
        (small[0], small[1], small[2], small[3], small[4], small[5], small[6], small[7], small[8]),
        ("batch", "tp"),
    )
    shards = (
        lax.psum_scatter(
            big[0].astype(jnp.bfloat16), "batch", scatter_dimension=0, tiled=True
        ).astype(jnp.float32),
        lax.psum_scatter(
            big[1].astype(jnp.bfloat16), "batch", scatter_dimension=0, tiled=True
        ).astype(jnp.float32),
        lax.psum_scatter(
            big[2].astype(jnp.bfloat16), "batch", scatter_dimension=0, tiled=True
        ).astype(jnp.float32),
        lax.psum_scatter(
            big[3].astype(jnp.bfloat16), "batch", scatter_dimension=1, tiled=True
        ).astype(jnp.float32),
        lax.psum_scatter(
            big[4].astype(jnp.bfloat16), "batch", scatter_dimension=0, tiled=True
        ).astype(jnp.float32),
        lax.psum_scatter(
            big[5].astype(jnp.bfloat16), "batch", scatter_dimension=1, tiled=True
        ).astype(jnp.float32),
    )
    output = result.astype(jnp.bfloat16)
    return (
        output,
        grad_tokens,
        shards[0],
        summed[0],
        shards[1],
        shards[2],
        summed[1],
        shards[3],
        summed[2],
        summed[3],
        summed[4],
        shards[4],
        summed[5],
        shards[5],
        summed[6],
        summed[7],
        summed[8],
    )


def swap_core(piece):
    return lax.ppermute(piece, "tp", [(i, i ^ 1) for i in range(4)])


def swap_chip(piece):
    return lax.ppermute(piece, "tp", [(i, i ^ 2) for i in range(4)])


def swap_batch(piece, bits):
    return lax.ppermute(piece, "batch", [(i, i ^ bits) for i in range(8)])


MEBI = 1024 * 1024
PIECES = 2
EXTRA = 16


def run_kernel(turn, kernel, inputs, outputs, scalars=(), hbm=(), scratch=(), final=(), limit=24):
    read = len(scalars) + len(hbm) + len(inputs)

    def wrapped(*refs):
        kernel(*refs[:read], *refs[read + len(turn) :])

    results = pl.pallas_call(
        wrapped,
        out_shape=[
            (pltpu.HBM if i in final else pltpu.VMEM)(shape, kind)
            for i, (shape, kind) in enumerate(outputs)
        ],
        in_specs=[pl.BlockSpec(memory_space=pltpu.SMEM)] * len(scalars)
        + [pl.BlockSpec(memory_space=pltpu.HBM)] * len(hbm)
        + [pl.BlockSpec(memory_space=pltpu.VMEM)] * len(inputs)
        + [pl.BlockSpec(memory_space=pl.ANY)] * len(turn),
        out_specs=[pl.BlockSpec(memory_space=pltpu.VMEM)] * len(outputs),
        scratch_shapes=list(scratch),
        compiler_params=pltpu.CompilerParams(vmem_limit_bytes=limit * MEBI),
        cost_estimate=pl.CostEstimate(flops=1, bytes_accessed=1, transcendentals=0),
    )(*scalars, *[pltpu.with_memory_space_constraint(item, pltpu.HBM) for item in hbm], *inputs, *turn)
    results = list(results)
    turn[:] = [pltpu.with_memory_space_constraint(results[0], pltpu.HBM) if 0 in final else results[0]]
    return results


def fetch(sources, targets, sems):
    copies = [pltpu.make_async_copy(a, b, sems.at[i]) for i, (a, b) in enumerate(zip(sources, targets))]
    for copy in copies:
        copy.start()
    return copies


def wide(ref):
    return ref[...].astype(jnp.float32)


def head(ref, like):
    return ref[: like.shape[0], :].astype(jnp.float32)


def joined(refs):
    return refs[0][...] if len(refs) == 1 else jnp.concatenate([ref[...] for ref in refs], axis=0)


def cut_rows(whole, refs):
    at = 0
    for ref in refs:
        ref[...] = whole[at : at + ref.shape[0]]
        at += ref.shape[0]


def valid_slots(shape, axis, which, lengths):
    seq = shape[axis]
    tp_index = lax.axis_index("tp")
    slot = lax.broadcasted_iota(jnp.int32, shape, axis) + (tp_index % 2) * (seq // 2)
    slot = jnp.where(slot >= seq, slot - seq, slot)
    return slot < lengths[(tp_index // 2) ^ which]


def apart(two, lane):
    zero = jnp.zeros_like(two)
    return jnp.concatenate(
        [jnp.where(lane < HEAD_DIM, two, zero), jnp.where(lane < HEAD_DIM, zero, two)], axis=0
    )


def together(two, lane):
    half = two.shape[0] // 2
    return jnp.where(lane < HEAD_DIM, two[:half], two[half:])


def split_kernel(whole, *refs):
    cut_rows(whole[...], refs)


def attention_forward_kernel(which, count, load, lengths, *refs):
    if load:
        hbm, bq, bv, xm, refs = refs[:4], refs[4], refs[5], refs[6], refs[7:]
        xc, refs = refs[:count], refs[count:]
        q_ref, k_ref, v_ref, lse_ref, mixed_ref, pm_ref, *pc_refs = refs[: 6 + PIECES]
        wq, wk, wv, wo, sems = refs[6 + PIECES :]
        copies = fetch(hbm, (wq, wk, wv, wo), sems)
    else:
        wq, wk, wv, wo, bq, bv, xm = refs[:7]
        xc, refs = refs[7 : 7 + count], refs[7 + count :]
        q_ref, k_ref, v_ref, lse_ref, mixed_ref, pm_ref, *pc_refs = refs
        copies = []
    rows = xm.shape[0]
    seq = 2 * rows
    local = wq.shape[1]
    scale = HEAD_DIM ** (-0.5)
    x_all = (xm[...], joined(xc))
    for copy in copies[:1]:
        copy.wait()
    for i, x in enumerate(x_all):
        part = pl.ds(i * rows, rows)
        q_ref[part, :] = ((product(x, wq[...]) + wide(bq)) * scale).astype(jnp.bfloat16)
    for copy in copies[1:3]:
        copy.wait()
    for i, x in enumerate(x_all):
        part = pl.ds(i * rows, rows)
        k_ref[part, :] = product(x, wk[...]).astype(jnp.bfloat16)
        v_ref[part, :] = (product(x, wv[...]) + wide(bv)).astype(jnp.bfloat16)
    valid = valid_slots((1, seq), 1, which, lengths)
    lane = lax.broadcasted_iota(jnp.int32, (seq, 128), 1)
    lse_all = jnp.zeros((seq, 128), jnp.float32)
    for pair in range(local // (2 * HEAD_DIM)):
        cut = slice(2 * pair * HEAD_DIM, 2 * (pair + 1) * HEAD_DIM)
        scores = against(apart(q_ref[:, cut], lane), k_ref[:, cut])
        probs = []
        for i in range(2):
            some = jnp.where(valid, scores[i * seq : (i + 1) * seq], negative)
            highest = jnp.max(some, axis=-1, keepdims=True)
            exponent = jnp.exp(some - highest)
            total = jnp.sum(exponent, axis=-1, keepdims=True)
            probs.append((exponent * (1.0 / total)).astype(jnp.bfloat16))
            lse_all = jnp.where(lane == 2 * pair + i, highest + jnp.log(total), lse_all)
        mixed = product(jnp.concatenate(probs, axis=0), v_ref[:, cut])
        mixed_ref[:, cut] = together(mixed, lane).astype(jnp.bfloat16)
    lse_ref[...] = lse_all.T[:8, :]
    for copy in copies[3:]:
        copy.wait()
    cut_rows(product(mixed_ref[rows:, :], wo[...]).astype(jnp.bfloat16), pc_refs)
    pm_ref[...] = product(mixed_ref[:rows, :], wo[...]).astype(jnp.bfloat16)


def attention_backward_kernel(which, lengths, wq, wk, wv, wo, *refs):
    db, refs = refs[: 2 * PIECES], refs[2 * PIECES :]
    q_ref, k_ref, v_ref, lse_ref, mixed_ref, g_ref, bias_ref, pm_ref, *pc_refs = refs[: 8 + PIECES]
    (dm_ref,) = refs[8 + PIECES :]
    seq, local = q_ref.shape
    rows = seq // 2
    scale = HEAD_DIM ** (-0.5)
    for i in range(2):
        grad = joined(db[i * PIECES : (i + 1) * PIECES])
        dm_ref[i * rows : (i + 1) * rows, :] = against(grad, wo[...]).astype(jnp.bfloat16)
    crossed = (wide(dm_ref) * wide(mixed_ref)).T
    valid = valid_slots((seq, 1), 0, which, lengths)
    lane = lax.broadcasted_iota(jnp.int32, (seq, 2 * HEAD_DIM), 1)
    for pair in range(local // (2 * HEAD_DIM)):
        cut = slice(2 * pair * HEAD_DIM, 2 * (pair + 1) * HEAD_DIM)
        q, k, v, dm = q_ref[:, cut], k_ref[:, cut], v_ref[:, cut], dm_ref[:, cut]
        k_both, v_both = apart(k, lane), apart(v, lane)
        scores = against(k_both, q)
        change = against(v_both, dm)
        probs_low, grads = [], []
        for i in range(2):
            h = 2 * pair + i
            part = slice(i * seq, (i + 1) * seq)
            centre = jnp.sum(crossed[h * HEAD_DIM : (h + 1) * HEAD_DIM, :], axis=0, keepdims=True)
            probs = jnp.exp(jnp.where(valid, scores[part], negative) - lse_ref[h : h + 1, :])
            probs_low.append(probs.astype(jnp.bfloat16))
            grads.append((probs * (change[part] - centre)).astype(jnp.bfloat16))
        probs_low = jnp.concatenate(probs_low, axis=0)
        grads = jnp.concatenate(grads, axis=0)
        shift = lambda n: slice(n * local + 2 * pair * HEAD_DIM, n * local + 2 * (pair + 1) * HEAD_DIM)
        g_ref[:, shift(2)] = together(product(probs_low, dm), lane).astype(jnp.bfloat16)
        g_ref[:, shift(1)] = together(product(grads, q), lane).astype(jnp.bfloat16)
        grad_q = product(k_both.T, grads).astype(jnp.bfloat16) * scale
        g_ref[:, cut] = grad_q.T.astype(jnp.bfloat16)
    bias_ref[...] = jnp.sum(wide(g_ref), axis=0, keepdims=True)
    for i in (1, 0):
        part = slice(i * rows, (i + 1) * rows)
        total = (
            against(g_ref[part, :local], wq[...])
            + against(g_ref[part, local : 2 * local], wk[...])
            + against(g_ref[part, 2 * local :], wv[...])
        ).astype(jnp.bfloat16)
        cut_rows(total, pc_refs if i else [pm_ref])


def split_columns(rows, cut, total, pm_ref, pc_refs):
    pm_ref[:, cut] = total[:rows].astype(jnp.bfloat16)
    at = rows
    for ref in pc_refs:
        ref[:, cut] = total[at : at + ref.shape[0]].astype(jnp.bfloat16)
        at += ref.shape[0]


def feed_forward_kernel(*refs):
    h, refs = refs[: 2 * PIECES], refs[2 * PIECES :]
    wu, bu, wd, act_ref, slope_ref, pm_ref, *pc_refs = refs
    x = joined(h)
    step = 256
    for j in range(wu.shape[1] // step):
        cut = slice(j * step, (j + 1) * step)
        inner = product(x, wu[:, cut]) + bu[:, cut].astype(jnp.float32)
        cumulative = 0.5 * (1.0 + lax.erf(inner * 2.0 ** (-0.5)))
        density = jnp.exp(-0.5 * inner * inner) * (2.0 * math.pi) ** (-0.5)
        act_ref[:, cut] = (inner * cumulative).astype(jnp.bfloat16)
        slope_ref[:, cut] = (cumulative + inner * density).astype(jnp.bfloat16)
    for j in range(wd.shape[1] // step):
        cut = slice(j * step, (j + 1) * step)
        split_columns(x.shape[0] // 2, cut, product(act_ref[...], wd[:, cut]), pm_ref, pc_refs)


def feed_backward_kernel(*refs):
    d, refs = refs[: 2 * PIECES], refs[2 * PIECES :]
    slope, wd, wu, grad_ref, bias_ref, pm_ref, *pc_refs = refs
    x = joined(d)
    step = 256
    for j in range(wu.shape[1] // step):
        cut = slice(j * step, (j + 1) * step)
        grad = (against(x, wd[cut, :]) * slope[:, cut].astype(jnp.float32)).astype(jnp.bfloat16)
        grad_ref[:, cut] = grad
        bias_ref[:, cut] = jnp.sum(grad.astype(jnp.float32), axis=0, keepdims=True)
    for j in range(wu.shape[0] // step):
        cut = slice(j * step, (j + 1) * step)
        split_columns(x.shape[0] // 2, cut, against(grad_ref[...], wu[cut, :]), pm_ref, pc_refs)


def weight_grad_kernel(order, count, products, *refs):
    refs = list(refs)
    taken = []
    for n in count:
        taken.append((refs[:n], refs[n : n + 2]))
        del refs[: n + 2]
    *out, left_ref, low_ref = refs
    me = lax.axis_index("batch")
    width = low_ref.shape[0]
    block = width // 8
    step = 256
    done = 0
    for (lefts, (r0, r1)), columns in zip(taken, products):
        at = 0
        for left in lefts:
            left_ref[:, at : at + left.shape[0]] = left[...].T
            at += left.shape[0]
        half = r0.shape[0]
        for start in range(columns[0], columns[1], step):
            cut = slice(done, done + step)
            source = slice(start, start + step)
            total = product(left_ref[:, :half], r0[:, source]) + product(left_ref[:, half:], r1[:, source])
            done += step
            low_ref[:, cut] = total.astype(jnp.bfloat16)
            for place in range(8):
                bits = [(place >> bit) & 1 for bit in (2, 1, 0)]
                r = sum(value << bit for value, bit in zip(bits, order))
                rows = pl.ds(pl.multiple_of((me ^ r) * block, block), block)
                out[bits[0]][place % 4, :, cut] = low_ref[rows, cut]


def chip_sum_kernel(mine, *refs):
    *got, out_ref = refs
    rows = mine.shape[0]
    out_ref[:rows, :] = (wide(mine) + joined(got).astype(jnp.float32)).astype(jnp.bfloat16)
    out_ref[rows:, :] = jnp.zeros((out_ref.shape[0] - rows, out_ref.shape[1]), jnp.bfloat16)


def last_sum_kernel(mine, *refs):
    *got, other, resid, out_ref = refs
    out_ref[...] = (wide(mine) + joined(got).astype(jnp.float32) + head(other, mine) + resid[...]).astype(jnp.bfloat16)


def norm_one_kernel(tok, mine, got, bias, gain, shift, hidden_ref, normed_ref, inverse_ref, *low_refs):
    resid = wide(tok) + (head(mine, tok) + head(got, tok) + wide(bias))
    hidden, normed, inverse = norm_forward(resid, gain[...], shift[...])
    hidden_ref[...] = hidden
    normed_ref[...] = normed
    inverse_ref[...] = inverse
    cut_rows(hidden.astype(jnp.bfloat16), low_refs)


def norm_two_kernel(hidden, mine, got, bias, gain, shift, cot, out_ref, grad_ref, sums_ref, *low_refs):
    resid = hidden[...] + (head(mine, hidden) + head(got, hidden) + wide(bias))
    result, normed, inverse = norm_forward(resid, gain[...], shift[...])
    out_ref[...] = result.astype(jnp.bfloat16)
    grad, gain_sum, shift_sum = norm_backward(wide(cot), normed, inverse, gain[...])
    low = grad.astype(jnp.bfloat16)
    grad_ref[...] = grad
    cut_rows(low, low_refs)
    sums_ref[0:1, :] = gain_sum[None]
    sums_ref[1:2, :] = shift_sum[None]
    sums_ref[2:3, :] = jnp.sum(low.astype(jnp.float32), axis=0, keepdims=True)


def norm_one_back_kernel(count, mine, got, *refs):
    resid, (normed, inverse, gain, grad_ref, sums_ref, *low_refs) = refs[:count], refs[count:]
    upstream = head(mine, normed) + head(got, normed) + joined(resid).astype(jnp.float32)
    grad, gain_sum, shift_sum = norm_backward(upstream, normed[...], inverse[...], gain[...])
    low = grad.astype(jnp.bfloat16)
    grad_ref[...] = grad
    cut_rows(low, low_refs)
    sums_ref[0:1, :] = gain_sum[None]
    sums_ref[1:2, :] = shift_sum[None]
    sums_ref[2:3, :] = jnp.sum(low.astype(jnp.float32), axis=0, keepdims=True)


def fold_kernel(turn, keep, got, *out):
    count = keep.shape[0]
    if count == 1:
        full = keep[0].astype(jnp.float32) + got[0].astype(jnp.float32)
        n = full.shape[1] // len(out)
        for i, ref in enumerate(out):
            part = full[:, i * n : (i + 1) * n]
            ref[...] = part.T if turn and i == 0 else part
        return
    for r in range(count):
        full = keep[r].astype(jnp.float32) + got[r].astype(jnp.float32)
        out[(2 * r) // count][r % (count // 2)] = full.astype(jnp.bfloat16)


def pack_kernel(one, two, bias0, bias1, up0, up1, out_ref):
    tp_index = lax.axis_index("tp")
    out_ref[...] = jnp.zeros(out_ref.shape, jnp.float32)
    out_ref[0:3, :] = one[0:3, :]
    out_ref[3:6, :] = two[0:3, :]
    local = bias0.shape[1] // 3
    lanes = pl.ds(pl.multiple_of(tp_index * local, 128), local)
    bias = bias0[...] + bias1[...]
    out_ref[6:7, lanes] = bias[:, :local]
    out_ref[7:8, lanes] = bias[:, 2 * local :]
    out_ref[pl.ds(8 + tp_index, 1), :] = up0[...] + up1[...]


def add_kernel(a, b, out_ref):
    out_ref[...] = a[...] + b[...]


def fast_body(
    tokens,
    lengths,
    w_query,
    b_query,
    w_key,
    w_value,
    b_value,
    w_out,
    b_out,
    gain_one,
    shift_one,
    w_up,
    b_up,
    w_down,
    b_down,
    gain_two,
    shift_two,
    cotangent,
):
    bf16, f32 = jnp.bfloat16, jnp.float32
    rows, width = tokens.shape
    seq = 2 * rows
    local = w_query.shape[1]
    units = w_up.shape[1]
    row = lambda item: item.reshape(1, -1)
    piece_rows = [((rows // PIECES, width), bf16)] * PIECES
    part_rows = [((rows, width), bf16)] + piece_rows

    call = functools.partial(run_kernel, [])

    weights = []

    def attention_forward(which, xm, *xc):
        load = not weights
        results = call(
            functools.partial(attention_forward_kernel, which, len(xc), load),
            (*weights, row(b_query), row(b_value), xm, *xc),
            [((seq, local), bf16)] * 3
            + [((8, seq), f32), ((seq, local), bf16)]
            + part_rows
            + ([((width, local), bf16)] * 3 + [((local, width), bf16)]) * load,
            (lengths,),
            (w_query, w_key, w_value, w_out) if load else (),
            [pltpu.SemaphoreType.DMA((4,))] * load,
        )
        if load:
            weights[:] = results[-4:]
            del results[-4:]
        return results

    def attention_backward(which, db, kept):
        return call(
            functools.partial(attention_backward_kernel, which),
            (*weights, *db, *kept),
            [((seq, 3 * local), bf16), ((1, 3 * local), f32)] + part_rows,
            (lengths,),
            scratch=[pltpu.VMEM((seq, local), bf16)],
        )

    def feed_forward(h):
        return call(feed_forward_kernel, (*h, w_up, row(b_up), w_down), [((seq, units), bf16)] * 2 + part_rows)

    def feed_backward(d, slope):
        return call(
            feed_backward_kernel,
            (*d, slope, w_down, w_up),
            [((seq, units), bf16), ((1, units), f32)] + part_rows,
        )

    def weight_grad(order, *products):
        inputs, columns = [], []
        for lefts, rights, cut in products:
            inputs += [*lefts, *rights]
            columns.append(cut or (0, rights[0].shape[1]))
        n = sum(stop - start for start, stop in columns)
        return call(
            functools.partial(weight_grad_kernel, order, [len(item[0]) for item in products], columns),
            inputs,
            [((4, width // 8, n), bf16)] * 2,
            scratch=[pltpu.VMEM((width, 4 * rows), bf16), pltpu.VMEM((width, n), bf16)],
        )

    def chip_sum(mine, *theirs):
        return call(chip_sum_kernel, (mine, *map(swap_core, theirs)), [((rows + EXTRA, width), bf16)])[0]

    def norm_one(tok, mine, got):
        return call(
            norm_one_kernel,
            (tok, mine, got, row(b_out), row(gain_one), row(shift_one)),
            [((rows, width), f32), ((rows, width), f32), ((rows, 1), f32)] + piece_rows,
        )

    def norm_two(hidden, mine, got):
        return call(
            norm_two_kernel,
            (hidden, mine, got, row(b_down), row(gain_two), row(shift_two), cotangent),
            [((rows, width), bf16), ((rows, width), f32), ((8, width), f32)] + piece_rows,
            final=(0,),
        )

    def norm_one_back(mine, got, resid, normed, inverse):
        return call(
            functools.partial(norm_one_back_kernel, len(resid)),
            (mine, got, *resid, normed, inverse, row(gain_one)),
            [((rows, width), f32), ((8, width), f32)] + piece_rows,
        )

    def fold(keep, got):
        count, block, n = keep.shape
        return call(functools.partial(fold_kernel, False), (keep, got), [((count // 2, block, n), bf16)] * 2)

    def fold_last(keep, got, turn=False, parts=1):
        _, block, n = keep.shape
        shapes = [(block, n // parts)] * parts
        if turn:
            shapes[0] = shapes[0][::-1]
        return call(
            functools.partial(fold_kernel, turn), (keep, got), [(shape, f32) for shape in shapes], final=range(parts)
        )

    def add(a, b, final=()):
        return call(add_kernel, (a, b), [(a.shape, f32)], final=final)[0]

    def both(low):
        return (*low, *map(swap_core, low))

    Y, Z1, Z2 = 0, 1, 2
    swap = lambda blocks, bit: swap_batch(blocks, 1 << bit)
    tok_other = swap_chip(tokens)
    tok_own_c = swap_core(tokens)
    *kept_own, pm, pc0, pc1 = attention_forward(0, tokens, tok_own_c)
    mine_own = chip_sum(pm, pc0, pc1)
    from_own = swap_chip(mine_own)
    tok_other_c = [swap_core(item) for item in call(split_kernel, (tok_other,), piece_rows)]
    *kept_other, pm, pc0, pc1 = attention_forward(1, tok_other, *tok_other_c)
    mine_other = chip_sum(pm, pc0, pc1)
    from_other = swap_chip(mine_other)
    hidden_other, n1_other, r1_other, *low = norm_one(tok_other, mine_other, from_own)
    hid_other = both(low)
    act_other, slope_other, *part = feed_forward(hid_other)
    mine_other = chip_sum(*part)
    got_own = swap_chip(mine_other)
    hidden_own, n1_own, r1_own, *low = norm_one(tokens, mine_own, from_other)
    hid_own = both(low)
    act_own, slope_own, *part = feed_forward(hid_own)
    mine_own = chip_sum(*part)
    output, dr2_own, sums_two, *low = norm_two(hidden_own, mine_own, got_own)
    low_other = [swap_chip(item) for item in low]
    ds_own = both(low)
    di_own, bup_own, *part = feed_backward(ds_own, slope_own)
    mine_own = chip_sum(*part)
    from_own = swap_chip(mine_own)
    ds_other = both(low_other)
    order_down = (Y, Z2, Z1)
    order_up = (Z1, Y, Z2)
    order_a = (Z1, Y, Z2)
    order_b = (Y, Z1, Z2)
    down = weight_grad(order_down, ((*ds_own, *ds_other), (act_own, act_other), None))
    down_got = swap(down[1], order_down[0])
    di_other, bup_other, *part = feed_backward(ds_other, slope_other)
    up = weight_grad(order_up, ((*hid_own, *hid_other), (di_own, di_other), None))
    mine_other = chip_sum(*part)
    from_other = swap_chip(mine_other)
    up_got = swap(up[1], order_up[0])
    _, _, *low = norm_one_back(mine_other, from_own, low_other, n1_other, r1_other)
    db_other = both(low)
    gqkv_other, bias_other, *part = attention_backward(1, db_other, kept_other)
    mine_other = chip_sum(*part)
    got_final = swap_chip(mine_other)
    down = fold(down[0], down_got)
    down_got = swap(down[1], order_down[1])
    dr1_own, sums_one, *low = norm_one_back(mine_own, from_other, (dr2_own,), n1_own, r1_own)
    db_own = both(low)
    gqkv_own, bias_own, *part = attention_backward(0, db_own, kept_own)
    part_c = [swap_core(item) for item in part[1:]]
    seqs = (tokens, tok_own_c, tok_other, *tok_other_c)
    gqkv = (gqkv_own, gqkv_other)
    a = weight_grad(
        order_a,
        ((*db_own, *db_other), (kept_own[4], kept_other[4]), None),
        (seqs, gqkv, (2 * local, 3 * local)),
    )
    a_got = swap(a[1], order_a[0])
    b = weight_grad(order_b, (seqs, gqkv, (0, 2 * local)))
    b_got = swap(b[1], order_b[0])
    up = fold(up[0], up_got)
    up_got = swap(up[1], order_up[1])
    small, = call(
        pack_kernel, (sums_one, sums_two, bias_own, bias_other, bup_own, bup_other), [((16, width), f32)]
    )
    small_got = swap_core(small)
    small = add(small, small_got)
    small_got = swap(small, Z2)
    small = add(small, small_got)
    small_got = swap(small, Z1)
    down = fold(down[0], down_got)
    down_got = swap(down[1], order_down[2])
    a = fold(a[0], a_got)
    a_got = swap(a[1], order_a[1])
    small = add(small, small_got)
    small_got = swap(small, Y)
    b = fold(b[0], b_got)
    b_got = swap(b[1], order_b[1])
    up = fold(up[0], up_got)
    up_got = swap(up[1], order_up[2])
    b = fold(b[0], b_got)
    b_got = swap(b[1], order_b[2])
    small = add(small, small_got)
    small_got = swap_chip(small)
    small = add(small, small_got, final=(0,))
    a = fold(a[0], a_got)
    a_got = swap(a[1], order_a[2])
    g_up, = fold_last(up[0], up_got)
    g_down, = fold_last(down[0], down_got, turn=True)
    grad_tokens, = call(
        last_sum_kernel, (part[0], *part_c, got_final, dr1_own), [((rows, width), bf16)], final=(0,)
    )
    g_query, g_key = fold_last(b[0], b_got, parts=2)
    g_out, g_value = fold_last(a[0], a_got, turn=True, parts=2)
    return (
        output,
        grad_tokens,
        g_query,
        small[6],
        g_key,
        g_value,
        small[7],
        g_out,
        small[2],
        small[0],
        small[1],
        g_up,
        small[8:12].reshape(-1),
        g_down,
        small[5],
        small[3],
        small[4],
    )


def solution(mesh):
    fast = mesh.shape["tp"] == 4 and mesh.shape["batch"] == 8
    return jax.shard_map(
        fast_body if fast else body,
        mesh=mesh,
        in_specs=(
            P(("batch", "tp"), None),
            P("batch"),
            P(None, "tp"),
            P("tp"),
            P(None, "tp"),
            P(None, "tp"),
            P("tp"),
            P("tp", None),
            P(),
            P(),
            P(),
            P(None, "tp"),
            P("tp"),
            P("tp", None),
            P(),
            P(),
            P(),
            P(("batch", "tp"), None),
        ),
        out_specs=(
            P(("batch", "tp"), None),
            P(("batch", "tp"), None),
            P("batch", "tp"),
            P(),
            P("batch", "tp"),
            P("batch", "tp"),
            P(),
            P("tp", "batch"),
            P(),
            P(),
            P(),
            P("batch", "tp"),
            P(),
            P("tp", "batch"),
            P(),
            P(),
            P(),
        ),
        check_vma=False,
    )
```

```python
import functools
import math

import jax
import jax.numpy as jnp
from jax import lax
from jax.experimental import pallas as pl
from jax.experimental.pallas import tpu as pltpu
from jax.sharding import PartitionSpec as P

HEAD_DIM = 64


epsilon = 1e-05
negative = -1e30


def product(left, right):
    return jnp.dot(left, right, preferred_element_type=jnp.float32)


def over_rows(left, right):
    return lax.dot_general(
        left, right, (((0,), (0,)), ((), ())), preferred_element_type=jnp.float32
    )


def against(left, right):
    return lax.dot_general(
        left, right, (((1,), (1,)), ((), ())), preferred_element_type=jnp.float32
    )


def norm_forward(resid, gain, shift):
    middle = jnp.mean(resid, axis=-1, keepdims=True)
    centred = resid - middle
    variance = jnp.mean(centred * centred, axis=-1, keepdims=True)
    inverse = lax.rsqrt(variance + epsilon)
    normed = centred * inverse
    return (normed * gain + shift, normed, inverse)


def norm_backward(upstream, normed, inverse, gain):
    scaled = upstream * gain
    first = jnp.mean(scaled, axis=-1, keepdims=True)
    second = jnp.mean(scaled * normed, axis=-1, keepdims=True)
    grad_resid = inverse * (scaled - first - normed * second)
    return (grad_resid, jnp.sum(upstream * normed, axis=0), jnp.sum(upstream, axis=0))


def gelu_slope(inner):
    cumulative = 0.5 * (1.0 + lax.erf(inner * 2.0 ** (-0.5)))
    density = jnp.exp(-0.5 * inner * inner) * (2.0 * math.pi) ** (-0.5)
    return cumulative + inner * density


def attend_forward(query, keys, values, valid):
    scores = jnp.einsum("qhd,khd->hqk", query, keys, preferred_element_type=jnp.float32)
    scores = jnp.where(valid[None, None, :], scores, negative)
    highest = jnp.max(scores, axis=-1, keepdims=True)
    exponent = jnp.exp(scores - highest)
    total = jnp.sum(exponent, axis=-1, keepdims=True)
    probs = (exponent / total).astype(jnp.bfloat16)
    mixed = jnp.einsum("hqk,khd->qhd", probs, values, preferred_element_type=jnp.float32)
    return (mixed.astype(jnp.bfloat16), highest + jnp.log(total))


def attend_backward(query, keys, values, valid, log_total, grad_mixed):
    scores = jnp.einsum("qhd,khd->hqk", query, keys, preferred_element_type=jnp.float32)
    scores = jnp.where(valid[None, None, :], scores, negative)
    probs = jnp.exp(scores - log_total)
    rounded = probs.astype(jnp.bfloat16)
    grad_values = jnp.einsum(
        "hqk,qhd->khd", rounded, grad_mixed, preferred_element_type=jnp.float32
    )
    grad_probs = jnp.einsum("qhd,khd->hqk", grad_mixed, values, preferred_element_type=jnp.float32)
    centre = jnp.sum(probs * grad_probs, axis=-1, keepdims=True)
    grad_scores = (probs * (grad_probs - centre)).astype(jnp.bfloat16)
    grad_query = jnp.einsum("hqk,khd->qhd", grad_scores, keys, preferred_element_type=jnp.float32)
    grad_keys = jnp.einsum("hqk,qhd->khd", grad_scores, query, preferred_element_type=jnp.float32)
    return (grad_query, grad_keys, grad_values)


def spread(piece):
    return lax.all_gather(piece, "tp", axis=0, tiled=True)


def collect(piece):
    return lax.psum_scatter(
        piece.astype(jnp.bfloat16), "tp", scatter_dimension=0, tiled=True
    ).astype(jnp.float32)


def forward_item(item):
    return attend_forward(item[0], item[1], item[2], item[3])


def backward_item(item):
    return attend_backward(item[0], item[1], item[2], item[3], item[4], item[5])


def body(
    tokens,
    lengths,
    w_query,
    b_query,
    w_key,
    w_value,
    b_value,
    w_out,
    b_out,
    gain_one,
    shift_one,
    w_up,
    b_up,
    w_down,
    b_down,
    gain_two,
    shift_two,
    cotangent,
):
    head_dim = HEAD_DIM
    scale = head_dim ** (-0.5)
    own_rows = tokens.shape[0]
    seq_len = 2 * own_rows
    tp_index = lax.axis_index("tp")
    upstream = cotangent.astype(jnp.float32)
    gathered = spread(tokens)
    groups = gathered.shape[0] // seq_len
    local_width = w_query.shape[1]
    local_heads = local_width // head_dim
    query = ((product(gathered, w_query) + b_query) * scale).astype(jnp.bfloat16)
    keys = product(gathered, w_key).astype(jnp.bfloat16)
    values = (product(gathered, w_value) + b_value).astype(jnp.bfloat16)
    shaped = (groups, seq_len, local_heads, head_dim)
    positions = jnp.arange(seq_len, dtype=jnp.int32)
    valid = positions[None, :] < lengths[:, None]
    query_s = query.reshape(shaped)
    keys_s = keys.reshape(shaped)
    values_s = values.reshape(shaped)
    mixed_s, log_total = lax.map(forward_item, (query_s, keys_s, values_s, valid))
    mixed = mixed_s.reshape(-1, local_width)
    branch = collect(product(mixed, w_out)) + b_out
    hidden, normed_one, inverse_one = norm_forward(
        tokens.astype(jnp.float32) + branch, gain_one, shift_one
    )
    hidden_all = spread(hidden.astype(jnp.bfloat16))
    inner = product(hidden_all, w_up) + b_up
    act = jax.nn.gelu(inner, approximate=False).astype(jnp.bfloat16)
    second = collect(product(act, w_down)) + b_down
    result, normed_two, inverse_two = norm_forward(hidden + second, gain_two, shift_two)
    grad_resid_two, grad_gain_two, grad_shift_two = norm_backward(
        upstream, normed_two, inverse_two, gain_two
    )
    grad_second = grad_resid_two.astype(jnp.bfloat16)
    grad_second_all = spread(grad_second)
    grad_w_down = over_rows(act, grad_second_all)
    grad_inner = (against(grad_second_all, w_down) * gelu_slope(inner)).astype(jnp.bfloat16)
    grad_w_up = over_rows(hidden_all, grad_inner)
    grad_hidden = collect(against(grad_inner, w_up)) + grad_resid_two
    grad_resid_one, grad_gain_one, grad_shift_one = norm_backward(
        grad_hidden, normed_one, inverse_one, gain_one
    )
    grad_branch = grad_resid_one.astype(jnp.bfloat16)
    grad_branch_all = spread(grad_branch)
    grad_w_out = over_rows(mixed, grad_branch_all)
    grad_mixed = against(grad_branch_all, w_out).astype(jnp.bfloat16)
    grad_query_s, grad_keys_s, grad_values_s = lax.map(
        backward_item, (query_s, keys_s, values_s, valid, log_total, grad_mixed.reshape(shaped))
    )
    grad_query = (grad_query_s.astype(jnp.bfloat16) * scale).reshape(-1, local_width)
    grad_keys = grad_keys_s.astype(jnp.bfloat16).reshape(-1, local_width)
    grad_values = grad_values_s.astype(jnp.bfloat16).reshape(-1, local_width)
    grad_w_query = over_rows(gathered, grad_query)
    grad_w_key = over_rows(gathered, grad_keys)
    grad_w_value = over_rows(gathered, grad_values)
    grad_input_part = (
        against(grad_query, w_query) + against(grad_keys, w_key) + against(grad_values, w_value)
    )
    grad_tokens = (collect(grad_input_part) + grad_resid_one).astype(jnp.bfloat16)
    width = w_query.shape[0]
    hidden_units = w_up.shape[1] * lax.axis_size("tp")
    query_bias = lax.dynamic_update_slice(
        jnp.zeros((width,), jnp.float32),
        jnp.sum(grad_query.astype(jnp.float32), axis=0),
        (tp_index * local_width,),
    )
    value_bias = lax.dynamic_update_slice(
        jnp.zeros((width,), jnp.float32),
        jnp.sum(grad_values.astype(jnp.float32), axis=0),
        (tp_index * local_width,),
    )
    up_bias = lax.dynamic_update_slice(
        jnp.zeros((hidden_units,), jnp.float32),
        jnp.sum(grad_inner.astype(jnp.float32), axis=0),
        (tp_index * w_up.shape[1],),
    )
    big = (grad_w_query, grad_w_key, grad_w_value, grad_w_out, grad_w_up, grad_w_down)
    out_bias = jnp.sum(grad_branch.astype(jnp.float32), axis=0)
    down_bias = jnp.sum(grad_second.astype(jnp.float32), axis=0)
    small = (
        query_bias,
        value_bias,
        out_bias,
        grad_gain_one,
        grad_shift_one,
        up_bias,
        down_bias,
        grad_gain_two,
        grad_shift_two,
    )
    summed = lax.psum(
        (small[0], small[1], small[2], small[3], small[4], small[5], small[6], small[7], small[8]),
        ("batch", "tp"),
    )
    shards = (
        lax.psum_scatter(
            big[0].astype(jnp.bfloat16), "batch", scatter_dimension=0, tiled=True
        ).astype(jnp.float32),
        lax.psum_scatter(
            big[1].astype(jnp.bfloat16), "batch", scatter_dimension=0, tiled=True
        ).astype(jnp.float32),
        lax.psum_scatter(
            big[2].astype(jnp.bfloat16), "batch", scatter_dimension=0, tiled=True
        ).astype(jnp.float32),
        lax.psum_scatter(
            big[3].astype(jnp.bfloat16), "batch", scatter_dimension=1, tiled=True
        ).astype(jnp.float32),
        lax.psum_scatter(
            big[4].astype(jnp.bfloat16), "batch", scatter_dimension=0, tiled=True
        ).astype(jnp.float32),
        lax.psum_scatter(
            big[5].astype(jnp.bfloat16), "batch", scatter_dimension=1, tiled=True
        ).astype(jnp.float32),
    )
    output = result.astype(jnp.bfloat16)
    return (
        output,
        grad_tokens,
        shards[0],
        summed[0],
        shards[1],
        shards[2],
        summed[1],
        shards[3],
        summed[2],
        summed[3],
        summed[4],
        shards[4],
        summed[5],
        shards[5],
        summed[6],
        summed[7],
        summed[8],
    )


def swap_core(piece):
    return lax.ppermute(piece, "tp", [(i, i ^ 1) for i in range(4)])


def swap_chip(piece):
    return lax.ppermute(piece, "tp", [(i, i ^ 2) for i in range(4)])


def swap_batch(piece, bits):
    return lax.ppermute(piece, "batch", [(i, i ^ bits) for i in range(8)])


MEBI = 1024 * 1024
PIECES = 2
SPLIT_DS = 2
SPLIT_FB = 2
EXTRA = 16


def run_kernel(turn, kernel, inputs, outputs, scalars=(), hbm=(), scratch=(), final=(), limit=24):
    read = len(scalars) + len(hbm) + len(inputs)

    def wrapped(*refs):
        kernel(*refs[:read], *refs[read + len(turn) :])

    results = pl.pallas_call(
        wrapped,
        out_shape=[
            (pltpu.HBM if i in final else pltpu.VMEM)(shape, kind)
            for i, (shape, kind) in enumerate(outputs)
        ],
        in_specs=[pl.BlockSpec(memory_space=pltpu.SMEM)] * len(scalars)
        + [pl.BlockSpec(memory_space=pltpu.HBM)] * len(hbm)
        + [pl.BlockSpec(memory_space=pltpu.VMEM)] * len(inputs)
        + [pl.BlockSpec(memory_space=pl.ANY)] * len(turn),
        out_specs=[pl.BlockSpec(memory_space=pltpu.VMEM)] * len(outputs),
        scratch_shapes=list(scratch),
        compiler_params=pltpu.CompilerParams(vmem_limit_bytes=limit * MEBI),
        cost_estimate=pl.CostEstimate(flops=1, bytes_accessed=1, transcendentals=0),
    )(*scalars, *[pltpu.with_memory_space_constraint(item, pltpu.HBM) for item in hbm], *inputs, *turn)
    results = list(results)
    turn[:] = [pltpu.with_memory_space_constraint(results[0], pltpu.HBM) if 0 in final else results[0]]
    return results


def fetch(sources, targets, sems):
    copies = [pltpu.make_async_copy(a, b, sems.at[i]) for i, (a, b) in enumerate(zip(sources, targets))]
    for copy in copies:
        copy.start()
    return copies


def wide(ref):
    return ref[...].astype(jnp.float32)


def head(ref, like):
    return ref[: like.shape[0], :].astype(jnp.float32)


def joined(refs):
    return refs[0][...] if len(refs) == 1 else jnp.concatenate([ref[...] for ref in refs], axis=0)


def cut_rows(whole, refs):
    at = 0
    for ref in refs:
        ref[...] = whole[at : at + ref.shape[0]]
        at += ref.shape[0]


def valid_slots(shape, axis, which, lengths):
    seq = shape[axis]
    tp_index = lax.axis_index("tp")
    slot = lax.broadcasted_iota(jnp.int32, shape, axis) + (tp_index % 2) * (seq // 2)
    slot = jnp.where(slot >= seq, slot - seq, slot)
    return slot < lengths[(tp_index // 2) ^ which]


def apart(two, lane):
    zero = jnp.zeros_like(two)
    return jnp.concatenate(
        [jnp.where(lane < HEAD_DIM, two, zero), jnp.where(lane < HEAD_DIM, zero, two)], axis=0
    )


def together(two, lane):
    half = two.shape[0] // 2
    return jnp.where(lane < HEAD_DIM, two[:half], two[half:])


def split_kernel(count, *refs):
    cut_rows(joined(refs[:count]), refs[count:])


def attention_forward_kernel(which, count, load, lengths, *refs):
    if load:
        hbm, bq, bv, xm, refs = refs[:4], refs[4], refs[5], refs[6], refs[7:]
        xc, refs = refs[:count], refs[count:]
        q_ref, k_ref, v_ref, lse_ref, mixed_ref, pm_ref, *pc_refs = refs[: 6 + PIECES]
        wq, wk, wv, wo, sems = refs[6 + PIECES :]
        copies = fetch(hbm, (wq, wk, wv, wo), sems)
    else:
        wq, wk, wv, wo, bq, bv, xm = refs[:7]
        xc, refs = refs[7 : 7 + count], refs[7 + count :]
        q_ref, k_ref, v_ref, lse_ref, mixed_ref, pm_ref, *pc_refs = refs
        copies = []
    rows = xm.shape[0]
    seq = 2 * rows
    local = wq.shape[1]
    scale = HEAD_DIM ** (-0.5)
    x_all = (xm[...], joined(xc))
    for copy in copies[:1]:
        copy.wait()
    for i, x in enumerate(x_all):
        part = pl.ds(i * rows, rows)
        q_ref[part, :] = ((product(x, wq[...]) + wide(bq)) * scale).astype(jnp.bfloat16)
    for copy in copies[1:3]:
        copy.wait()
    for i, x in enumerate(x_all):
        part = pl.ds(i * rows, rows)
        k_ref[part, :] = product(x, wk[...]).astype(jnp.bfloat16)
        v_ref[part, :] = (product(x, wv[...]) + wide(bv)).astype(jnp.bfloat16)
    valid = valid_slots((1, seq), 1, which, lengths)
    lane = lax.broadcasted_iota(jnp.int32, (seq, 128), 1)
    lse_all = jnp.zeros((seq, 128), jnp.float32)
    for pair in range(local // (2 * HEAD_DIM)):
        cut = slice(2 * pair * HEAD_DIM, 2 * (pair + 1) * HEAD_DIM)
        scores = against(apart(q_ref[:, cut], lane), k_ref[:, cut])
        probs = []
        for i in range(2):
            some = jnp.where(valid, scores[i * seq : (i + 1) * seq], negative)
            highest = jnp.max(some, axis=-1, keepdims=True)
            exponent = jnp.exp(some - highest)
            total = jnp.sum(exponent, axis=-1, keepdims=True)
            probs.append((exponent * (1.0 / total)).astype(jnp.bfloat16))
            lse_all = jnp.where(lane == 2 * pair + i, highest + jnp.log(total), lse_all)
        mixed = product(jnp.concatenate(probs, axis=0), v_ref[:, cut])
        mixed_ref[:, cut] = together(mixed, lane).astype(jnp.bfloat16)
    lse_ref[...] = lse_all.T[:8, :]
    for copy in copies[3:]:
        copy.wait()
    cut_rows(product(mixed_ref[rows:, :], wo[...]).astype(jnp.bfloat16), pc_refs)
    pm_ref[...] = product(mixed_ref[:rows, :], wo[...]).astype(jnp.bfloat16)


def attention_backward_kernel(which, count, lengths, wq, wk, wv, wo, *refs):
    db, refs = refs[:count], refs[count:]
    q_ref, k_ref, v_ref, lse_ref, mixed_ref, g_ref, bias_ref, pm_ref, *pc_refs = refs[: 8 + PIECES]
    (dm_ref,) = refs[8 + PIECES :]
    seq, local = q_ref.shape
    rows = seq // 2
    scale = HEAD_DIM ** (-0.5)
    dm_ref[...] = against(joined(db), wo[...]).astype(jnp.bfloat16)
    crossed = (wide(dm_ref) * wide(mixed_ref)).T
    valid = valid_slots((seq, 1), 0, which, lengths)
    lane = lax.broadcasted_iota(jnp.int32, (seq, 2 * HEAD_DIM), 1)
    for pair in range(local // (2 * HEAD_DIM)):
        cut = slice(2 * pair * HEAD_DIM, 2 * (pair + 1) * HEAD_DIM)
        q, k, v, dm = q_ref[:, cut], k_ref[:, cut], v_ref[:, cut], dm_ref[:, cut]
        k_both, v_both = apart(k, lane), apart(v, lane)
        scores = against(k_both, q)
        change = against(v_both, dm)
        probs_low, grads = [], []
        for i in range(2):
            h = 2 * pair + i
            part = slice(i * seq, (i + 1) * seq)
            centre = jnp.sum(crossed[h * HEAD_DIM : (h + 1) * HEAD_DIM, :], axis=0, keepdims=True)
            probs = jnp.exp(jnp.where(valid, scores[part], negative) - lse_ref[h : h + 1, :])
            probs_low.append(probs.astype(jnp.bfloat16))
            grads.append((probs * (change[part] - centre)).astype(jnp.bfloat16))
        probs_low = jnp.concatenate(probs_low, axis=0)
        grads = jnp.concatenate(grads, axis=0)
        shift = lambda n: slice(n * local + 2 * pair * HEAD_DIM, n * local + 2 * (pair + 1) * HEAD_DIM)
        g_ref[:, shift(2)] = together(product(probs_low, dm), lane).astype(jnp.bfloat16)
        g_ref[:, shift(1)] = together(product(grads, q), lane).astype(jnp.bfloat16)
        grad_q = product(k_both.T, grads).astype(jnp.bfloat16) * scale
        g_ref[:, cut] = grad_q.T.astype(jnp.bfloat16)
    bias_ref[...] = jnp.sum(wide(g_ref), axis=0, keepdims=True)
    for i in (1, 0):
        part = slice(i * rows, (i + 1) * rows)
        total = (
            against(g_ref[part, :local], wq[...])
            + against(g_ref[part, local : 2 * local], wk[...])
            + against(g_ref[part, 2 * local :], wv[...])
        ).astype(jnp.bfloat16)
        cut_rows(total, pc_refs if i else [pm_ref])


def split_columns(rows, cut, total, pm_ref, pc_refs):
    pm_ref[:, cut] = total[:rows].astype(jnp.bfloat16)
    at = rows
    for ref in pc_refs:
        ref[:, cut] = total[at : at + ref.shape[0]].astype(jnp.bfloat16)
        at += ref.shape[0]


def feed_forward_kernel(count, *refs):
    h, refs = refs[:count], refs[count:]
    wu, bu, wd, act_ref, slope_ref, pm_ref, *pc_refs = refs
    x = joined(h)
    step = 256
    for j in range(wu.shape[1] // step):
        cut = slice(j * step, (j + 1) * step)
        inner = product(x, wu[:, cut]) + bu[:, cut].astype(jnp.float32)
        cumulative = 0.5 * (1.0 + lax.erf(inner * 2.0 ** (-0.5)))
        density = jnp.exp(-0.5 * inner * inner) * (2.0 * math.pi) ** (-0.5)
        act_ref[:, cut] = (inner * cumulative).astype(jnp.bfloat16)
        slope_ref[:, cut] = (cumulative + inner * density).astype(jnp.bfloat16)
    for j in range(wd.shape[1] // step):
        cut = slice(j * step, (j + 1) * step)
        split_columns(x.shape[0] // 2, cut, product(act_ref[...], wd[:, cut]), pm_ref, pc_refs)


def feed_backward_kernel(count, *refs):
    d, refs = refs[:count], refs[count:]
    slope, wd, wu, grad_ref, bias_ref, pm_ref, *pc_refs = refs
    x = joined(d)
    step = 256
    for j in range(wu.shape[1] // step):
        cut = slice(j * step, (j + 1) * step)
        grad = (against(x, wd[cut, :]) * slope[:, cut].astype(jnp.float32)).astype(jnp.bfloat16)
        grad_ref[:, cut] = grad
        bias_ref[:, cut] = jnp.sum(grad.astype(jnp.float32), axis=0, keepdims=True)
    for j in range(wu.shape[0] // step):
        cut = slice(j * step, (j + 1) * step)
        split_columns(x.shape[0] // 2, cut, against(grad_ref[...], wu[cut, :]), pm_ref, pc_refs)


def turned(lefts, left_ref):
    left_ref[...] = joined(lefts).T


def weight_part_kernel(counts, *refs):
    *refs, out_ref, left_ref = refs
    step = 256
    done = 0
    for count in counts:
        lefts, right, refs = refs[:count], refs[count], refs[count + 1 :]
        turned(lefts, left_ref)
        for start in range(0, right.shape[1], step):
            out_ref[:, done : done + step] = product(left_ref[...], right[:, start : start + step])
            done += step


def weight_grad_kernel(order, parts, tail, pieces, *refs):
    *refs, left_ref, low_ref = refs
    refs, (other_ref, keep_ref, *send_refs) = refs[: -2 - pieces], refs[-2 - pieces :]
    if tail:
        small, refs = refs[0][...], refs[1:]
        put_small(small, keep_ref, send_refs[-1])
    me = lax.axis_index("batch")
    block = low_ref.shape[0] // 8
    step = 256
    done = 0
    for count, first, last, place_other in parts:
        lefts, right, refs = refs[:count], refs[count], refs[count + 1 :]
        turned(lefts, left_ref)
        for start in range(first, last, step):
            cut = slice(done, done + step)
            at = place_other + start - first
            total = other_ref[:, at : at + step] + product(left_ref[...], right[:, start : start + step])
            done += step
            low_ref[:, cut] = total.astype(jnp.bfloat16)
            for place in range(8):
                bits = [(place >> bit) & 1 for bit in (2, 1, 0)]
                r = sum(value << bit for value, bit in zip(bits, order))
                rows = pl.ds(pl.multiple_of((me ^ r) * block, block), block)
                put_block([keep_ref] if bits[0] == 0 else send_refs, place % 4, block, 4, low_ref[rows, cut], cut)


def put_block(refs, place, block, count, value, cut=slice(None)):
    share = count // len(refs)
    at = (place % share) * block
    refs[place // share][at : at + block, cut] = value


def put_small(small, *refs):
    high = small.astype(jnp.bfloat16)
    low = (small - high.astype(jnp.float32)).astype(jnp.bfloat16)
    for ref in refs:
        n = ref.shape[1]
        at = ref.shape[0] - 2 * small.size // n
        for piece in (high, low):
            for start in range(0, small.shape[1], n):
                ref[at : at + small.shape[0], :] = piece[:, start : start + n]
                at += small.shape[0]


def take_small(ref, shape):
    n = ref.shape[1]
    count = shape[1] // n
    at = ref.shape[0] - 2 * count * shape[0]
    pieces = [ref[at + i * shape[0] : at + (i + 1) * shape[0], :].astype(jnp.float32) for i in range(2 * count)]
    return jnp.concatenate([a + b for a, b in zip(pieces[:count], pieces[count:])], axis=1)


def chip_sum_kernel(mine, *refs):
    *got, out_ref = refs
    rows = mine.shape[0]
    out_ref[:rows, :] = (wide(mine) + joined(got).astype(jnp.float32)).astype(jnp.bfloat16)
    if out_ref.shape[0] > rows:
        out_ref[rows:, :] = jnp.zeros((out_ref.shape[0] - rows, out_ref.shape[1]), jnp.bfloat16)


def last_sum_kernel(mine, *refs):
    *got, other, resid, out_ref = refs
    out_ref[...] = (wide(mine) + joined(got).astype(jnp.float32) + head(other, mine) + resid[...]).astype(jnp.bfloat16)


def norm_one_kernel(tok, mine, got, bias, gain, shift, hidden_ref, normed_ref, inverse_ref, *low_refs):
    resid = wide(tok) + (head(mine, tok) + head(got, tok) + wide(bias))
    hidden, normed, inverse = norm_forward(resid, gain[...], shift[...])
    hidden_ref[...] = hidden
    normed_ref[...] = normed
    inverse_ref[...] = inverse
    cut_rows(hidden.astype(jnp.bfloat16), low_refs)


def norm_two_kernel(count, hidden, mine, got, bias, gain, shift, cot, normed_ref, grad_ref, *low_refs):
    resid = hidden[...] + (head(mine, hidden) + head(got, hidden) + wide(bias))
    _, normed, inverse = norm_forward(resid, gain[...], shift[...])
    normed_ref[...] = normed
    grad, _, _ = norm_backward(wide(cot), normed, inverse, gain[...])
    grad_ref[...] = grad
    low = grad.astype(jnp.bfloat16)
    cut_rows(low, low_refs[:count])
    cut_rows(low, low_refs[count:])


def result_kernel(normed, gain, shift, cot, grad, out_ref, sums_ref):
    out_ref[...] = (normed[...] * gain[...] + shift[...]).astype(jnp.bfloat16)
    upstream = wide(cot)
    sums_ref[0:1, :] = jnp.sum(upstream * normed[...], axis=0, keepdims=True)
    sums_ref[1:2, :] = jnp.sum(upstream, axis=0, keepdims=True)
    low = grad[...].astype(jnp.bfloat16)
    sums_ref[2:3, :] = jnp.sum(low.astype(jnp.float32), axis=0, keepdims=True)


def norm_one_back_kernel(count, mine, got, *refs):
    resid, (normed, inverse, gain, grad_ref, sums_ref, *low_refs) = refs[:count], refs[count:]
    upstream = head(mine, normed) + head(got, normed) + joined(resid).astype(jnp.float32)
    grad, gain_sum, shift_sum = norm_backward(upstream, normed[...], inverse[...], gain[...])
    low = grad.astype(jnp.bfloat16)
    grad_ref[...] = grad
    cut_rows(low, low_refs)
    sums_ref[0:1, :] = gain_sum[None]
    sums_ref[1:2, :] = shift_sum[None]
    sums_ref[2:3, :] = jnp.sum(low.astype(jnp.float32), axis=0, keepdims=True)


def fold_kernel(block, small, count, pieces, keep, *refs):
    refs, send_refs = refs[:-pieces], refs[-pieces:]
    *got, keep_ref = refs
    share = count // len(got)
    for r in range(count):
        at = (r % share) * block
        arrived = got[r // share][at : at + block, :]
        full = (keep[r * block : (r + 1) * block, :].astype(jnp.float32) + arrived.astype(jnp.float32)).astype(jnp.bfloat16)
        put_block([keep_ref] if 2 * r < count else send_refs, r % (count // 2), block, count // 2, full)
    if small:
        put_small(take_small(keep, small) + take_small(got[-1], small), keep_ref, send_refs[-1])


def fold_last_kernel(block, small, turn, keep, got, *out):
    full = keep[:block, :].astype(jnp.float32) + got[:block, :].astype(jnp.float32)
    if small:
        *out, wide_ref = out
        out, rows = out[:-8], out[-8:]
        sums = take_small(keep, small) + take_small(got, small)
        for i, ref in enumerate(rows):
            ref[...] = sums[i : i + 1, :]
        for i in range(4):
            wide_ref[:, i * small[1] : (i + 1) * small[1]] = sums[8 + i : 9 + i, :]
    n = full.shape[1] // len(out)
    for i, ref in enumerate(out):
        part = full[:, i * n : (i + 1) * n]
        ref[...] = part.T if turn and i == 0 else part


def pack_kernel(one, two, bias0, bias1, up0, up1, out_ref):
    tp_index = lax.axis_index("tp")
    out_ref[...] = jnp.zeros(out_ref.shape, jnp.float32)
    out_ref[0:3, :] = one[0:3, :]
    out_ref[3:6, :] = two[0:3, :]
    local = bias0.shape[1] // 3
    lanes = pl.ds(pl.multiple_of(tp_index * local, 128), local)
    bias = bias0[...] + bias1[...]
    out_ref[6:7, lanes] = bias[:, :local]
    out_ref[7:8, lanes] = bias[:, 2 * local :]
    out_ref[pl.ds(8 + tp_index, 1), :] = up0[...] + up1[...]


def add_kernel(a, b, out_ref):
    out_ref[...] = a[...] + b[...]


def fast_body(
    tokens,
    lengths,
    w_query,
    b_query,
    w_key,
    w_value,
    b_value,
    w_out,
    b_out,
    gain_one,
    shift_one,
    w_up,
    b_up,
    w_down,
    b_down,
    gain_two,
    shift_two,
    cotangent,
):
    bf16, f32 = jnp.bfloat16, jnp.float32
    rows, width = tokens.shape
    seq = 2 * rows
    local = w_query.shape[1]
    units = w_up.shape[1]
    row = lambda item: item.reshape(1, -1)

    def rows_in(count):
        tile = 16
        tiles = rows // tile
        sizes = [(tiles // count + (i < tiles % count)) * tile for i in range(count)]
        return [((size, width), bf16) for size in sizes]

    piece_rows = rows_in(PIECES)
    part_rows = [((rows, width), bf16)] + piece_rows

    call = functools.partial(run_kernel, [])

    weights = []

    def attention_forward(which, xm, *xc):
        load = not weights
        results = call(
            functools.partial(attention_forward_kernel, which, len(xc), load),
            (*weights, row(b_query), row(b_value), xm, *xc),
            [((seq, local), bf16)] * 3
            + [((8, seq), f32), ((seq, local), bf16)]
            + part_rows
            + ([((width, local), bf16)] * 3 + [((local, width), bf16)]) * load,
            (lengths,),
            (w_query, w_key, w_value, w_out) if load else (),
            [pltpu.SemaphoreType.DMA((4,))] * load,
        )
        if load:
            weights[:] = results[-4:]
            del results[-4:]
        return results

    def attention_backward(which, db, kept):
        return call(
            functools.partial(attention_backward_kernel, which, len(db)),
            (*weights, *db, *kept),
            [((seq, 3 * local), bf16), ((1, 3 * local), f32)] + part_rows,
            (lengths,),
            scratch=[pltpu.VMEM((seq, local), bf16)],
        )

    def feed_forward(h):
        return call(
            functools.partial(feed_forward_kernel, len(h)),
            (*h, w_up, row(b_up), w_down), [((seq, units), bf16)] * 2 + part_rows,
        )

    def feed_backward(d, slope, pieces=PIECES):
        return call(
            functools.partial(feed_backward_kernel, len(d)),
            (*d, slope, w_down, w_up),
            [((seq, units), bf16), ((1, units), f32), ((rows, width), bf16)] + rows_in(pieces),
        )

    def weight_part(*products):
        inputs = [item for lefts, right in products for item in (*lefts, right)]
        n = sum(right.shape[1] for _, right in products)
        return call(
            functools.partial(weight_part_kernel, [len(lefts) for lefts, _ in products]),
            inputs, [((width, n), f32)], scratch=[pltpu.VMEM((width, seq), bf16)],
        )[0]

    block = width // 8
    small_shape = (16, width)

    def tail_rows(n, small):
        return 2 * 16 * width // n if small else 0

    def blocks_out(count, n, tail, pieces):
        rows_each = [count // pieces * block] * pieces
        rows_each[-1] += tail
        return [((rows, n), bf16) for rows in [count * block + tail] + rows_each]

    def weight_grad(order, other, *products, small=(), pieces=1):
        inputs, parts = [], []
        for lefts, right, columns, place_other in products:
            inputs += [*lefts, right]
            parts.append((len(lefts), *columns, place_other))
        n = sum(last - first for _, first, last, _ in parts)
        keep, *send = call(
            functools.partial(weight_grad_kernel, order, parts, len(small), pieces),
            (*small, *inputs, other), blocks_out(4, n, tail_rows(n, small), pieces),
            scratch=[pltpu.VMEM((width, seq), bf16), pltpu.VMEM((width, n), bf16)],
        )
        return keep, [swap(item, order[0]) for item in send]

    def fold(order, stage, keep, got, small=False, pieces=1):
        n = keep.shape[1]
        count = 8 >> stage
        keep, *send = call(
            functools.partial(fold_kernel, block, small and small_shape, count, pieces), (keep, *got),
            blocks_out(count // 2, n, tail_rows(n, small), pieces),
        )
        return keep, [swap(item, order[stage]) for item in send]

    def fold_last(keep, got, turn=False, parts=1, small=False):
        shapes = [(block, keep.shape[1] // parts)] * parts
        if turn:
            shapes[0] = shapes[0][::-1]
        if small:
            shapes += [(1, width)] * 8 + [(1, 4 * units)]
        return call(
            functools.partial(fold_last_kernel, block, small and small_shape, turn), (keep, *got),
            [(shape, f32) for shape in shapes], final=range(len(shapes)),
        )

    def chip_sum(mine, *theirs, extra=0):
        return call(chip_sum_kernel, (mine, *map(swap_core, theirs)), [((rows + extra, width), bf16)])[0]

    def norm_one(tok, mine, got, pieces=3):
        return call(
            norm_one_kernel,
            (tok, mine, got, row(b_out), row(gain_one), row(shift_one)),
            [((rows, width), f32), ((rows, width), f32), ((rows, 1), f32)] + rows_in(pieces),
        )

    def norm_two(hidden, mine, got):
        first = 5 * rows // 8
        sent = [((first, width), bf16), ((rows - first, width), bf16)]
        return call(
            functools.partial(norm_two_kernel, len(sent)),
            (hidden, mine, got, row(b_down), row(gain_two), row(shift_two), cotangent),
            [((rows, width), f32)] * 2 + sent + piece_rows,
        )

    def norm_one_back(mine, got, resid, normed, inverse):
        return call(
            functools.partial(norm_one_back_kernel, len(resid)),
            (mine, got, *resid, normed, inverse, row(gain_one)),
            [((rows, width), f32), ((8, width), f32)] + piece_rows,
        )

    def add(a, b, final=()):
        return call(add_kernel, (a, b), [(a.shape, f32)], final=final)[0]

    def both(low):
        return (*low, *map(swap_core, low))

    Y, Z1, Z2 = 0, 1, 2
    swap = lambda blocks, bit: swap_batch(blocks, 1 << bit)
    tok_other = swap_chip(tokens)
    tok_own_c = swap_core(tokens)
    *kept_own, pm, pc0, pc1 = attention_forward(0, tokens, tok_own_c)
    mine_own = chip_sum(pm, pc0, pc1)
    from_own = swap_chip(mine_own)
    tok_other_c = [swap_core(item) for item in call(functools.partial(split_kernel, 1), (tok_other,), rows_in(3))]
    *kept_other, pm, pc0, pc1 = attention_forward(1, tok_other, *tok_other_c)
    mine_other = chip_sum(pm, pc0, pc1)
    from_other = swap_chip(mine_other)
    hidden_other, n1_other, r1_other, *low = norm_one(tok_other, mine_other, from_own)
    hid_other = both(low)
    act_other, slope_other, *part = feed_forward(hid_other)
    mine_other = chip_sum(*part)
    got_own = swap_chip(mine_other)
    hidden_own, n1_own, r1_own, *low = norm_one(tokens, mine_own, from_other)
    hid_own = both(low)
    act_own, slope_own, *part = feed_forward(hid_own)
    mine_own = chip_sum(*part)
    n2_own, dr2_own, sent0, sent1, *low = norm_two(hidden_own, mine_own, got_own)
    low_other = [swap_chip(sent0), swap_chip(sent1)]
    ds_own = both(low)
    di_own, bup_own, *part = feed_backward(ds_own, slope_own)
    mine_own = chip_sum(*part, extra=2 * EXTRA)
    from_own = swap_chip(mine_own)
    output, sums_two = call(
        result_kernel, (n2_own, row(gain_two), row(shift_two), cotangent, dr2_own),
        [((rows, width), bf16), ((8, width), f32)], final=(0,),
    )
    down_own = weight_part((ds_own, act_own))
    up_own = weight_part((hid_own, di_own))
    ds_other = both(call(functools.partial(split_kernel, 2), low_other, rows_in(SPLIT_DS)))
    order_down = (Z1, Z2, Y)
    order_up = (Y, Z1, Z2)
    order_a = (Y, Z1, Z2)
    order_b = (Y, Z2, Z1)
    down = weight_grad(order_down, down_own, (ds_other, act_other, (0, units), 0), pieces=1)
    di_other, bup_other, *part = feed_backward(ds_other, slope_other, SPLIT_FB)
    up = weight_grad(order_up, up_own, (hid_other, di_other, (0, units), 0), pieces=1)
    mine_other = chip_sum(*part, extra=1 * EXTRA)
    from_other = swap_chip(mine_other)
    _, _, *low = norm_one_back(mine_other, from_own, low_other, n1_other, r1_other)
    db_other = both(low)
    gqkv_other, bias_other, *part = attention_backward(1, db_other, kept_other)
    tok_all = ((tokens, tok_own_c), (tok_other, *tok_other_c))
    attn_other = weight_part((db_other, kept_other[4]), (tok_all[1], gqkv_other))
    mine_other = chip_sum(*part, extra=0)
    got_final = swap_chip(mine_other)
    dr1_own, sums_one, *low = norm_one_back(mine_own, from_other, (dr2_own,), n1_own, r1_own)
    db_own = both(low)
    down = fold(order_down, 1, *down, pieces=1)
    gqkv_own, bias_own, *part = attention_backward(0, db_own, kept_own)
    part_c = [swap_core(item) for item in part[1:]]
    b = weight_grad(order_b, attn_other, (tok_all[0], gqkv_own, (0, 2 * local), local), pieces=2)
    small, = call(
        pack_kernel, (sums_one, sums_two, bias_own, bias_other, bup_own, bup_other), [((16, width), f32)]
    )
    small_got = swap_core(small)
    up = fold(order_up, 1, *up, pieces=1)
    small = add(small, small_got)
    small_got = swap_chip(small)
    small = add(small, small_got)
    a = weight_grad(
        order_a,
        attn_other,
        (db_own, kept_own[4], (0, local), 0),
        (tok_all[0], gqkv_own, (2 * local, 3 * local), 3 * local),
        small=(small,), pieces=2,
    )
    b = fold(order_b, 1, *b, pieces=1)
    down = fold(order_down, 2, *down, pieces=1)
    a = fold(order_a, 1, *a, small=True, pieces=2)
    b = fold(order_b, 2, *b, pieces=1)
    up = fold(order_up, 2, *up, pieces=1)
    g_down, = fold_last(*down, turn=True)
    a = fold(order_a, 2, *a, small=True, pieces=1)
    g_up, = fold_last(*up)
    grad_tokens, = call(
        last_sum_kernel, (part[0], *part_c, got_final, dr1_own), [((rows, width), bf16)], final=(0,)
    )
    g_out, g_value, *small = fold_last(*a, turn=True, parts=2, small=True)
    g_query, g_key = fold_last(*b, parts=2)
    gg1, gs1, gbo, gg2, gs2, gbd, gbq, gbv, gbu = [item.reshape(-1) for item in small]
    return (
        output,
        grad_tokens,
        g_query,
        gbq,
        g_key,
        g_value,
        gbv,
        g_out,
        gbo,
        gg1,
        gs1,
        g_up,
        gbu,
        g_down,
        gbd,
        gg2,
        gs2,
    )


def solution(mesh):
    fast = mesh.shape["tp"] == 4 and mesh.shape["batch"] == 8
    return jax.shard_map(
        fast_body if fast else body,
        mesh=mesh,
        in_specs=(
            P(("batch", "tp"), None),
            P("batch"),
            P(None, "tp"),
            P("tp"),
            P(None, "tp"),
            P(None, "tp"),
            P("tp"),
            P("tp", None),
            P(),
            P(),
            P(),
            P(None, "tp"),
            P("tp"),
            P("tp", None),
            P(),
            P(),
            P(),
            P(("batch", "tp"), None),
        ),
        out_specs=(
            P(("batch", "tp"), None),
            P(("batch", "tp"), None),
            P("batch", "tp"),
            P(),
            P("batch", "tp"),
            P("batch", "tp"),
            P(),
            P("tp", "batch"),
            P(),
            P(),
            P(),
            P("batch", "tp"),
            P(),
            P("tp", "batch"),
            P(),
            P(),
            P(),
        ),
        check_vma=False,
    )
```

```python
import functools
import math

import jax
import jax.numpy as jnp
from jax import lax
from jax.experimental import pallas as pl
from jax.experimental.pallas import tpu as pltpu
from jax.sharding import PartitionSpec as P

HEAD_DIM = 64


epsilon = 1e-05
negative = -1e30


def product(left, right):
    return jnp.dot(left, right, preferred_element_type=jnp.float32)


def over_rows(left, right):
    return lax.dot_general(
        left, right, (((0,), (0,)), ((), ())), preferred_element_type=jnp.float32
    )


def against(left, right):
    return lax.dot_general(
        left, right, (((1,), (1,)), ((), ())), preferred_element_type=jnp.float32
    )


def norm_forward(resid, gain, shift):
    middle = jnp.mean(resid, axis=-1, keepdims=True)
    centred = resid - middle
    variance = jnp.mean(centred * centred, axis=-1, keepdims=True)
    inverse = lax.rsqrt(variance + epsilon)
    normed = centred * inverse
    return (normed * gain + shift, normed, inverse)


def norm_backward(upstream, normed, inverse, gain):
    scaled = upstream * gain
    first = jnp.mean(scaled, axis=-1, keepdims=True)
    second = jnp.mean(scaled * normed, axis=-1, keepdims=True)
    grad_resid = inverse * (scaled - first - normed * second)
    return (grad_resid, jnp.sum(upstream * normed, axis=0), jnp.sum(upstream, axis=0))


def gelu_slope(inner):
    cumulative = 0.5 * (1.0 + lax.erf(inner * 2.0 ** (-0.5)))
    density = jnp.exp(-0.5 * inner * inner) * (2.0 * math.pi) ** (-0.5)
    return cumulative + inner * density


def attend_forward(query, keys, values, valid):
    scores = jnp.einsum("qhd,khd->hqk", query, keys, preferred_element_type=jnp.float32)
    scores = jnp.where(valid[None, None, :], scores, negative)
    highest = jnp.max(scores, axis=-1, keepdims=True)
    exponent = jnp.exp(scores - highest)
    total = jnp.sum(exponent, axis=-1, keepdims=True)
    probs = (exponent / total).astype(jnp.bfloat16)
    mixed = jnp.einsum("hqk,khd->qhd", probs, values, preferred_element_type=jnp.float32)
    return (mixed.astype(jnp.bfloat16), highest + jnp.log(total))


def attend_backward(query, keys, values, valid, log_total, grad_mixed):
    scores = jnp.einsum("qhd,khd->hqk", query, keys, preferred_element_type=jnp.float32)
    scores = jnp.where(valid[None, None, :], scores, negative)
    probs = jnp.exp(scores - log_total)
    rounded = probs.astype(jnp.bfloat16)
    grad_values = jnp.einsum(
        "hqk,qhd->khd", rounded, grad_mixed, preferred_element_type=jnp.float32
    )
    grad_probs = jnp.einsum("qhd,khd->hqk", grad_mixed, values, preferred_element_type=jnp.float32)
    centre = jnp.sum(probs * grad_probs, axis=-1, keepdims=True)
    grad_scores = (probs * (grad_probs - centre)).astype(jnp.bfloat16)
    grad_query = jnp.einsum("hqk,khd->qhd", grad_scores, keys, preferred_element_type=jnp.float32)
    grad_keys = jnp.einsum("hqk,qhd->khd", grad_scores, query, preferred_element_type=jnp.float32)
    return (grad_query, grad_keys, grad_values)


def spread(piece):
    return lax.all_gather(piece, "tp", axis=0, tiled=True)


def collect(piece):
    return lax.psum_scatter(
        piece.astype(jnp.bfloat16), "tp", scatter_dimension=0, tiled=True
    ).astype(jnp.float32)


def forward_item(item):
    return attend_forward(item[0], item[1], item[2], item[3])


def backward_item(item):
    return attend_backward(item[0], item[1], item[2], item[3], item[4], item[5])


def body(
    tokens,
    lengths,
    w_query,
    b_query,
    w_key,
    w_value,
    b_value,
    w_out,
    b_out,
    gain_one,
    shift_one,
    w_up,
    b_up,
    w_down,
    b_down,
    gain_two,
    shift_two,
    cotangent,
):
    head_dim = HEAD_DIM
    scale = head_dim ** (-0.5)
    own_rows = tokens.shape[0]
    seq_len = 2 * own_rows
    tp_index = lax.axis_index("tp")
    upstream = cotangent.astype(jnp.float32)
    gathered = spread(tokens)
    groups = gathered.shape[0] // seq_len
    local_width = w_query.shape[1]
    local_heads = local_width // head_dim
    query = ((product(gathered, w_query) + b_query) * scale).astype(jnp.bfloat16)
    keys = product(gathered, w_key).astype(jnp.bfloat16)
    values = (product(gathered, w_value) + b_value).astype(jnp.bfloat16)
    shaped = (groups, seq_len, local_heads, head_dim)
    positions = jnp.arange(seq_len, dtype=jnp.int32)
    valid = positions[None, :] < lengths[:, None]
    query_s = query.reshape(shaped)
    keys_s = keys.reshape(shaped)
    values_s = values.reshape(shaped)
    mixed_s, log_total = lax.map(forward_item, (query_s, keys_s, values_s, valid))
    mixed = mixed_s.reshape(-1, local_width)
    branch = collect(product(mixed, w_out)) + b_out
    hidden, normed_one, inverse_one = norm_forward(
        tokens.astype(jnp.float32) + branch, gain_one, shift_one
    )
    hidden_all = spread(hidden.astype(jnp.bfloat16))
    inner = product(hidden_all, w_up) + b_up
    act = jax.nn.gelu(inner, approximate=False).astype(jnp.bfloat16)
    second = collect(product(act, w_down)) + b_down
    result, normed_two, inverse_two = norm_forward(hidden + second, gain_two, shift_two)
    grad_resid_two, grad_gain_two, grad_shift_two = norm_backward(
        upstream, normed_two, inverse_two, gain_two
    )
    grad_second = grad_resid_two.astype(jnp.bfloat16)
    grad_second_all = spread(grad_second)
    grad_w_down = over_rows(act, grad_second_all)
    grad_inner = (against(grad_second_all, w_down) * gelu_slope(inner)).astype(jnp.bfloat16)
    grad_w_up = over_rows(hidden_all, grad_inner)
    grad_hidden = collect(against(grad_inner, w_up)) + grad_resid_two
    grad_resid_one, grad_gain_one, grad_shift_one = norm_backward(
        grad_hidden, normed_one, inverse_one, gain_one
    )
    grad_branch = grad_resid_one.astype(jnp.bfloat16)
    grad_branch_all = spread(grad_branch)
    grad_w_out = over_rows(mixed, grad_branch_all)
    grad_mixed = against(grad_branch_all, w_out).astype(jnp.bfloat16)
    grad_query_s, grad_keys_s, grad_values_s = lax.map(
        backward_item, (query_s, keys_s, values_s, valid, log_total, grad_mixed.reshape(shaped))
    )
    grad_query = (grad_query_s.astype(jnp.bfloat16) * scale).reshape(-1, local_width)
    grad_keys = grad_keys_s.astype(jnp.bfloat16).reshape(-1, local_width)
    grad_values = grad_values_s.astype(jnp.bfloat16).reshape(-1, local_width)
    grad_w_query = over_rows(gathered, grad_query)
    grad_w_key = over_rows(gathered, grad_keys)
    grad_w_value = over_rows(gathered, grad_values)
    grad_input_part = (
        against(grad_query, w_query) + against(grad_keys, w_key) + against(grad_values, w_value)
    )
    grad_tokens = (collect(grad_input_part) + grad_resid_one).astype(jnp.bfloat16)
    width = w_query.shape[0]
    hidden_units = w_up.shape[1] * lax.axis_size("tp")
    query_bias = lax.dynamic_update_slice(
        jnp.zeros((width,), jnp.float32),
        jnp.sum(grad_query.astype(jnp.float32), axis=0),
        (tp_index * local_width,),
    )
    value_bias = lax.dynamic_update_slice(
        jnp.zeros((width,), jnp.float32),
        jnp.sum(grad_values.astype(jnp.float32), axis=0),
        (tp_index * local_width,),
    )
    up_bias = lax.dynamic_update_slice(
        jnp.zeros((hidden_units,), jnp.float32),
        jnp.sum(grad_inner.astype(jnp.float32), axis=0),
        (tp_index * w_up.shape[1],),
    )
    big = (grad_w_query, grad_w_key, grad_w_value, grad_w_out, grad_w_up, grad_w_down)
    out_bias = jnp.sum(grad_branch.astype(jnp.float32), axis=0)
    down_bias = jnp.sum(grad_second.astype(jnp.float32), axis=0)
    small = (
        query_bias,
        value_bias,
        out_bias,
        grad_gain_one,
        grad_shift_one,
        up_bias,
        down_bias,
        grad_gain_two,
        grad_shift_two,
    )
    summed = lax.psum(
        (small[0], small[1], small[2], small[3], small[4], small[5], small[6], small[7], small[8]),
        ("batch", "tp"),
    )
    shards = (
        lax.psum_scatter(
            big[0].astype(jnp.bfloat16), "batch", scatter_dimension=0, tiled=True
        ).astype(jnp.float32),
        lax.psum_scatter(
            big[1].astype(jnp.bfloat16), "batch", scatter_dimension=0, tiled=True
        ).astype(jnp.float32),
        lax.psum_scatter(
            big[2].astype(jnp.bfloat16), "batch", scatter_dimension=0, tiled=True
        ).astype(jnp.float32),
        lax.psum_scatter(
            big[3].astype(jnp.bfloat16), "batch", scatter_dimension=1, tiled=True
        ).astype(jnp.float32),
        lax.psum_scatter(
            big[4].astype(jnp.bfloat16), "batch", scatter_dimension=0, tiled=True
        ).astype(jnp.float32),
        lax.psum_scatter(
            big[5].astype(jnp.bfloat16), "batch", scatter_dimension=1, tiled=True
        ).astype(jnp.float32),
    )
    output = result.astype(jnp.bfloat16)
    return (
        output,
        grad_tokens,
        shards[0],
        summed[0],
        shards[1],
        shards[2],
        summed[1],
        shards[3],
        summed[2],
        summed[3],
        summed[4],
        shards[4],
        summed[5],
        shards[5],
        summed[6],
        summed[7],
        summed[8],
    )


def swap_core(piece):
    return lax.ppermute(piece, "tp", [(i, i ^ 1) for i in range(4)])


def swap_chip(piece):
    return lax.ppermute(piece, "tp", [(i, i ^ 2) for i in range(4)])


def swap_batch(piece, bits):
    return lax.ppermute(piece, "batch", [(i, i ^ bits) for i in range(8)])


MEBI = 1024 * 1024
PIECES = 2
SPLIT_DS = 2
SPLIT_LOW = 2
SENT_FIRST = 10
SPLIT_FB = 2
EXTRA = 16


def run_kernel(turn, kernel, inputs, outputs, scalars=(), hbm=(), scratch=(), final=(), limit=24):
    read = len(scalars) + len(hbm) + len(inputs)

    def wrapped(*refs):
        kernel(*refs[:read], *refs[read + len(turn) :])

    results = pl.pallas_call(
        wrapped,
        out_shape=[
            (pltpu.HBM if i in final else pltpu.VMEM)(shape, kind)
            for i, (shape, kind) in enumerate(outputs)
        ],
        in_specs=[pl.BlockSpec(memory_space=pltpu.SMEM)] * len(scalars)
        + [pl.BlockSpec(memory_space=pltpu.HBM)] * len(hbm)
        + [pl.BlockSpec(memory_space=pltpu.VMEM)] * len(inputs)
        + [pl.BlockSpec(memory_space=pl.ANY)] * len(turn),
        out_specs=[pl.BlockSpec(memory_space=pltpu.VMEM)] * len(outputs),
        scratch_shapes=list(scratch),
        compiler_params=pltpu.CompilerParams(vmem_limit_bytes=limit * MEBI),
        cost_estimate=pl.CostEstimate(flops=1, bytes_accessed=1, transcendentals=0),
    )(*scalars, *[pltpu.with_memory_space_constraint(item, pltpu.HBM) for item in hbm], *inputs, *turn)
    results = list(results)
    turn[:] = [pltpu.with_memory_space_constraint(results[0], pltpu.HBM) if 0 in final else results[0]]
    return results


def fetch(sources, targets, sems):
    copies = [pltpu.make_async_copy(a, b, sems.at[i]) for i, (a, b) in enumerate(zip(sources, targets))]
    for copy in copies:
        copy.start()
    return copies


def wide(ref):
    return ref[...].astype(jnp.float32)


def head(ref, like):
    return ref[: like.shape[0], :].astype(jnp.float32)


def joined(refs):
    return refs[0][...] if len(refs) == 1 else jnp.concatenate([ref[...] for ref in refs], axis=0)


def cut_rows(whole, refs):
    at = 0
    for ref in refs:
        ref[...] = whole[at : at + ref.shape[0]]
        at += ref.shape[0]


def valid_slots(shape, axis, which, lengths):
    seq = shape[axis]
    tp_index = lax.axis_index("tp")
    slot = lax.broadcasted_iota(jnp.int32, shape, axis) + (tp_index % 2) * (seq // 2)
    slot = jnp.where(slot >= seq, slot - seq, slot)
    return slot < lengths[(tp_index // 2) ^ which]


def apart(two, lane):
    zero = jnp.zeros_like(two)
    return jnp.concatenate(
        [jnp.where(lane < HEAD_DIM, two, zero), jnp.where(lane < HEAD_DIM, zero, two)], axis=0
    )


def together(two, lane):
    half = two.shape[0] // 2
    return jnp.where(lane < HEAD_DIM, two[:half], two[half:])


def split_kernel(count, *refs):
    cut_rows(joined(refs[:count]), refs[count:])


def attention_forward_kernel(which, count, load, lengths, *refs):
    if load:
        hbm, bq, bv, xm, refs = refs[:4], refs[4], refs[5], refs[6], refs[7:]
        xc, refs = refs[:count], refs[count:]
        q_ref, k_ref, v_ref, lse_ref, mixed_ref, pm_ref, *pc_refs = refs[: 6 + PIECES]
        wq, wk, wv, wo, sems = refs[6 + PIECES :]
        copies = fetch(hbm, (wq, wk, wv, wo), sems)
    else:
        wq, wk, wv, wo, bq, bv, xm = refs[:7]
        xc, refs = refs[7 : 7 + count], refs[7 + count :]
        q_ref, k_ref, v_ref, lse_ref, mixed_ref, pm_ref, *pc_refs = refs
        copies = []
    rows = xm.shape[0]
    seq = 2 * rows
    local = wq.shape[1]
    scale = HEAD_DIM ** (-0.5)
    x_all = (xm[...], joined(xc))
    for copy in copies[:1]:
        copy.wait()
    for i, x in enumerate(x_all):
        part = pl.ds(i * rows, rows)
        q_ref[part, :] = ((product(x, wq[...]) + wide(bq)) * scale).astype(jnp.bfloat16)
    for copy in copies[1:3]:
        copy.wait()
    for i, x in enumerate(x_all):
        part = pl.ds(i * rows, rows)
        k_ref[part, :] = product(x, wk[...]).astype(jnp.bfloat16)
        v_ref[part, :] = (product(x, wv[...]) + wide(bv)).astype(jnp.bfloat16)
    valid = valid_slots((1, seq), 1, which, lengths)
    lane = lax.broadcasted_iota(jnp.int32, (seq, 128), 1)
    lse_all = jnp.zeros((seq, 128), jnp.float32)
    for pair in range(local // (2 * HEAD_DIM)):
        cut = slice(2 * pair * HEAD_DIM, 2 * (pair + 1) * HEAD_DIM)
        scores = against(apart(q_ref[:, cut], lane), k_ref[:, cut])
        probs = []
        for i in range(2):
            some = jnp.where(valid, scores[i * seq : (i + 1) * seq], negative)
            highest = jnp.max(some, axis=-1, keepdims=True)
            exponent = jnp.exp(some - highest)
            total = jnp.sum(exponent, axis=-1, keepdims=True)
            probs.append((exponent * (1.0 / total)).astype(jnp.bfloat16))
            lse_all = jnp.where(lane == 2 * pair + i, highest + jnp.log(total), lse_all)
        mixed = product(jnp.concatenate(probs, axis=0), v_ref[:, cut])
        mixed_ref[:, cut] = together(mixed, lane).astype(jnp.bfloat16)
    lse_ref[...] = lse_all.T[:8, :]
    for copy in copies[3:]:
        copy.wait()
    cut_rows(product(mixed_ref[rows:, :], wo[...]).astype(jnp.bfloat16), pc_refs)
    pm_ref[...] = product(mixed_ref[:rows, :], wo[...]).astype(jnp.bfloat16)


def attention_backward_kernel(which, count, lengths, wo, *refs):
    db, refs = refs[:count], refs[count:]
    q_ref, k_ref, v_ref, lse_ref, mixed_ref, g_ref, bias_ref, dm_ref = refs
    seq, local = q_ref.shape
    scale = HEAD_DIM ** (-0.5)
    dm_ref[...] = against(joined(db), wo[...]).astype(jnp.bfloat16)
    crossed = (wide(dm_ref) * wide(mixed_ref)).T
    valid = valid_slots((seq, 1), 0, which, lengths)
    lane = lax.broadcasted_iota(jnp.int32, (seq, 2 * HEAD_DIM), 1)
    for pair in range(local // (2 * HEAD_DIM)):
        cut = slice(2 * pair * HEAD_DIM, 2 * (pair + 1) * HEAD_DIM)
        q, k, v, dm = q_ref[:, cut], k_ref[:, cut], v_ref[:, cut], dm_ref[:, cut]
        k_both, v_both = apart(k, lane), apart(v, lane)
        scores = against(k_both, q)
        change = against(v_both, dm)
        probs_low, grads = [], []
        for i in range(2):
            h = 2 * pair + i
            part = slice(i * seq, (i + 1) * seq)
            centre = jnp.sum(crossed[h * HEAD_DIM : (h + 1) * HEAD_DIM, :], axis=0, keepdims=True)
            probs = jnp.exp(jnp.where(valid, scores[part], negative) - lse_ref[h : h + 1, :])
            probs_low.append(probs.astype(jnp.bfloat16))
            grads.append((probs * (change[part] - centre)).astype(jnp.bfloat16))
        probs_low = jnp.concatenate(probs_low, axis=0)
        grads = jnp.concatenate(grads, axis=0)
        shift = lambda n: slice(n * local + 2 * pair * HEAD_DIM, n * local + 2 * (pair + 1) * HEAD_DIM)
        g_ref[:, shift(2)] = together(product(probs_low, dm), lane).astype(jnp.bfloat16)
        g_ref[:, shift(1)] = together(product(grads, q), lane).astype(jnp.bfloat16)
        grad_q = product(k_both.T, grads).astype(jnp.bfloat16) * scale
        g_ref[:, cut] = grad_q.T.astype(jnp.bfloat16)
    bias_ref[...] = jnp.sum(wide(g_ref), axis=0, keepdims=True)


def input_grad_kernel(g_ref, wq, wk, wv, pm_ref, *pc_refs):
    rows = pm_ref.shape[0]
    local = wq.shape[1]
    total = (
        against(g_ref[:, :local], wq[...])
        + against(g_ref[:, local : 2 * local], wk[...])
        + against(g_ref[:, 2 * local :], wv[...])
    ).astype(jnp.bfloat16)
    pm_ref[...] = total[:rows]
    cut_rows(total[rows:], pc_refs)


def split_columns(rows, cut, total, pm_ref, pc_refs):
    pm_ref[:, cut] = total[:rows].astype(jnp.bfloat16)
    at = rows
    for ref in pc_refs:
        ref[:, cut] = total[at : at + ref.shape[0]].astype(jnp.bfloat16)
        at += ref.shape[0]


def feed_forward_kernel(count, *refs):
    h, refs = refs[:count], refs[count:]
    wu, bu, wd, act_ref, slope_ref, pm_ref, *pc_refs = refs
    x = joined(h)
    step = 256
    for j in range(wu.shape[1] // step):
        cut = slice(j * step, (j + 1) * step)
        inner = product(x, wu[:, cut]) + bu[:, cut].astype(jnp.float32)
        cumulative = 0.5 * (1.0 + lax.erf(inner * 2.0 ** (-0.5)))
        density = jnp.exp(-0.5 * inner * inner) * (2.0 * math.pi) ** (-0.5)
        act_ref[:, cut] = (inner * cumulative).astype(jnp.bfloat16)
        slope_ref[:, cut] = (cumulative + inner * density).astype(jnp.bfloat16)
    for j in range(wd.shape[1] // step):
        cut = slice(j * step, (j + 1) * step)
        split_columns(x.shape[0] // 2, cut, product(act_ref[...], wd[:, cut]), pm_ref, pc_refs)


def feed_backward_kernel(count, *refs):
    d, refs = refs[:count], refs[count:]
    slope, wd, wu, grad_ref, bias_ref, pm_ref, *pc_refs = refs
    x = joined(d)
    step = 256
    for j in range(wu.shape[1] // step):
        cut = slice(j * step, (j + 1) * step)
        grad = (against(x, wd[cut, :]) * slope[:, cut].astype(jnp.float32)).astype(jnp.bfloat16)
        grad_ref[:, cut] = grad
        bias_ref[:, cut] = jnp.sum(grad.astype(jnp.float32), axis=0, keepdims=True)
    for j in range(wu.shape[0] // step):
        cut = slice(j * step, (j + 1) * step)
        split_columns(x.shape[0] // 2, cut, against(grad_ref[...], wu[cut, :]), pm_ref, pc_refs)


def turned(lefts, left_ref):
    left_ref[...] = joined(lefts).T


def weight_part_kernel(counts, *refs):
    *refs, out_ref, left_ref = refs
    step = 256
    done = 0
    for count in counts:
        lefts, right, refs = refs[:count], refs[count], refs[count + 1 :]
        turned(lefts, left_ref)
        for start in range(0, right.shape[1], step):
            out_ref[:, done : done + step] = product(left_ref[...], right[:, start : start + step])
            done += step


def weight_grad_kernel(order, parts, tail, pieces, *refs):
    *refs, left_ref, low_ref = refs
    refs, (other_ref, keep_ref, *send_refs) = refs[: -2 - pieces], refs[-2 - pieces :]
    if tail:
        small, refs = refs[0][...], refs[1:]
        put_small(small, keep_ref, send_refs[-1])
    me = lax.axis_index("batch")
    block = low_ref.shape[0] // 8
    step = 256
    done = 0
    for count, first, last, place_other in parts:
        lefts, right, refs = refs[:count], refs[count], refs[count + 1 :]
        turned(lefts, left_ref)
        for start in range(first, last, step):
            cut = slice(done, done + step)
            at = place_other + start - first
            total = other_ref[:, at : at + step] + product(left_ref[...], right[:, start : start + step])
            done += step
            low_ref[:, cut] = total.astype(jnp.bfloat16)
            for place in range(8):
                bits = [(place >> bit) & 1 for bit in (2, 1, 0)]
                r = sum(value << bit for value, bit in zip(bits, order))
                rows = pl.ds(pl.multiple_of((me ^ r) * block, block), block)
                put_block([keep_ref] if bits[0] == 0 else send_refs, place % 4, block, 4, low_ref[rows, cut], cut)


def put_block(refs, place, block, count, value, cut=slice(None)):
    share = count // len(refs)
    at = (place % share) * block
    refs[place // share][at : at + block, cut] = value


def put_small(small, *refs):
    high = small.astype(jnp.bfloat16)
    low = (small - high.astype(jnp.float32)).astype(jnp.bfloat16)
    for ref in refs:
        n = ref.shape[1]
        at = ref.shape[0] - 2 * small.size // n
        for piece in (high, low):
            for start in range(0, small.shape[1], n):
                ref[at : at + small.shape[0], :] = piece[:, start : start + n]
                at += small.shape[0]


def take_small(ref, shape):
    n = ref.shape[1]
    count = shape[1] // n
    at = ref.shape[0] - 2 * count * shape[0]
    pieces = [ref[at + i * shape[0] : at + (i + 1) * shape[0], :].astype(jnp.float32) for i in range(2 * count)]
    return jnp.concatenate([a + b for a, b in zip(pieces[:count], pieces[count:])], axis=1)


def chip_sum_kernel(mine, *refs):
    *got, out_ref = refs
    rows = mine.shape[0]
    out_ref[:rows, :] = (wide(mine) + joined(got).astype(jnp.float32)).astype(jnp.bfloat16)
    if out_ref.shape[0] > rows:
        out_ref[rows:, :] = jnp.zeros((out_ref.shape[0] - rows, out_ref.shape[1]), jnp.bfloat16)


def last_sum_kernel(mine, *refs):
    *got, other, resid, out_ref = refs
    out_ref[...] = (wide(mine) + joined(got).astype(jnp.float32) + head(other, mine) + resid[...]).astype(jnp.bfloat16)


def norm_one_kernel(tok, mine, got, bias, gain, shift, hidden_ref, normed_ref, inverse_ref, *low_refs):
    resid = wide(tok) + (head(mine, tok) + head(got, tok) + wide(bias))
    hidden, normed, inverse = norm_forward(resid, gain[...], shift[...])
    hidden_ref[...] = hidden
    normed_ref[...] = normed
    inverse_ref[...] = inverse
    cut_rows(hidden.astype(jnp.bfloat16), low_refs)


def norm_two_kernel(count, hidden, mine, got, bias, gain, shift, cot, normed_ref, grad_ref, *low_refs):
    resid = hidden[...] + (head(mine, hidden) + head(got, hidden) + wide(bias))
    _, normed, inverse = norm_forward(resid, gain[...], shift[...])
    normed_ref[...] = normed
    grad, _, _ = norm_backward(wide(cot), normed, inverse, gain[...])
    grad_ref[...] = grad
    low = grad.astype(jnp.bfloat16)
    cut_rows(low, low_refs[:count])
    cut_rows(low, low_refs[count:])


def result_kernel(normed, gain, shift, cot, grad, out_ref, sums_ref):
    out_ref[...] = (normed[...] * gain[...] + shift[...]).astype(jnp.bfloat16)
    upstream = wide(cot)
    sums_ref[0:1, :] = jnp.sum(upstream * normed[...], axis=0, keepdims=True)
    sums_ref[1:2, :] = jnp.sum(upstream, axis=0, keepdims=True)
    low = grad[...].astype(jnp.bfloat16)
    sums_ref[2:3, :] = jnp.sum(low.astype(jnp.float32), axis=0, keepdims=True)


def norm_one_back_kernel(count, mine, got, *refs):
    resid, (normed, inverse, gain, grad_ref, sums_ref, *low_refs) = refs[:count], refs[count:]
    upstream = head(mine, normed) + head(got, normed) + joined(resid).astype(jnp.float32)
    grad, gain_sum, shift_sum = norm_backward(upstream, normed[...], inverse[...], gain[...])
    low = grad.astype(jnp.bfloat16)
    grad_ref[...] = grad
    cut_rows(low, low_refs)
    sums_ref[0:1, :] = gain_sum[None]
    sums_ref[1:2, :] = shift_sum[None]
    sums_ref[2:3, :] = jnp.sum(low.astype(jnp.float32), axis=0, keepdims=True)


def fold_kernel(block, small, count, pieces, keep, *refs):
    refs, send_refs = refs[:-pieces], refs[-pieces:]
    *got, keep_ref = refs
    share = count // len(got)
    for r in range(count):
        at = (r % share) * block
        arrived = got[r // share][at : at + block, :]
        full = (keep[r * block : (r + 1) * block, :].astype(jnp.float32) + arrived.astype(jnp.float32)).astype(jnp.bfloat16)
        put_block([keep_ref] if 2 * r < count else send_refs, r % (count // 2), block, count // 2, full)
    if small:
        put_small(take_small(keep, small) + take_small(got[-1], small), keep_ref, send_refs[-1])


def fold_last_kernel(block, small, turn, keep, got, *out):
    full = keep[:block, :].astype(jnp.float32) + got[:block, :].astype(jnp.float32)
    if small:
        *out, wide_ref = out
        out, rows = out[:-8], out[-8:]
        sums = take_small(keep, small) + take_small(got, small)
        for i, ref in enumerate(rows):
            ref[...] = sums[i : i + 1, :]
        for i in range(4):
            wide_ref[:, i * small[1] : (i + 1) * small[1]] = sums[8 + i : 9 + i, :]
    n = full.shape[1] // len(out)
    for i, ref in enumerate(out):
        part = full[:, i * n : (i + 1) * n]
        ref[...] = part.T if turn and i == 0 else part


def pack_kernel(one, two, bias0, bias1, up0, up1, out_ref):
    tp_index = lax.axis_index("tp")
    out_ref[...] = jnp.zeros(out_ref.shape, jnp.float32)
    out_ref[0:3, :] = one[0:3, :]
    out_ref[3:6, :] = two[0:3, :]
    local = bias0.shape[1] // 3
    lanes = pl.ds(pl.multiple_of(tp_index * local, 128), local)
    bias = bias0[...] + bias1[...]
    out_ref[6:7, lanes] = bias[:, :local]
    out_ref[7:8, lanes] = bias[:, 2 * local :]
    out_ref[pl.ds(8 + tp_index, 1), :] = up0[...] + up1[...]


def add_kernel(a, b, out_ref):
    out_ref[...] = a[...] + b[...]


def fast_body(
    tokens,
    lengths,
    w_query,
    b_query,
    w_key,
    w_value,
    b_value,
    w_out,
    b_out,
    gain_one,
    shift_one,
    w_up,
    b_up,
    w_down,
    b_down,
    gain_two,
    shift_two,
    cotangent,
):
    bf16, f32 = jnp.bfloat16, jnp.float32
    rows, width = tokens.shape
    seq = 2 * rows
    local = w_query.shape[1]
    units = w_up.shape[1]
    row = lambda item: item.reshape(1, -1)

    def rows_in(count):
        tile = 16
        tiles = rows // tile
        sizes = [(tiles // count + (i < tiles % count)) * tile for i in range(count)]
        return [((size, width), bf16) for size in sizes]

    piece_rows = rows_in(PIECES)
    part_rows = [((rows, width), bf16)] + piece_rows

    call = functools.partial(run_kernel, [])

    weights = []

    def attention_forward(which, xm, *xc):
        load = not weights
        results = call(
            functools.partial(attention_forward_kernel, which, len(xc), load),
            (*weights, row(b_query), row(b_value), xm, *xc),
            [((seq, local), bf16)] * 3
            + [((8, seq), f32), ((seq, local), bf16)]
            + part_rows
            + ([((width, local), bf16)] * 3 + [((local, width), bf16)]) * load,
            (lengths,),
            (w_query, w_key, w_value, w_out) if load else (),
            [pltpu.SemaphoreType.DMA((4,))] * load,
        )
        if load:
            weights[:] = results[-4:]
            del results[-4:]
        return results

    def attention_backward(which, db, kept):
        return call(
            functools.partial(attention_backward_kernel, which, len(db)),
            (weights[3], *db, *kept),
            [((seq, 3 * local), bf16), ((1, 3 * local), f32)],
            (lengths,),
            scratch=[pltpu.VMEM((seq, local), bf16)],
        )

    def input_grad(g):
        return call(input_grad_kernel, (g, *weights[:3]), part_rows)

    def feed_forward(h):
        return call(
            functools.partial(feed_forward_kernel, len(h)),
            (*h, w_up, row(b_up), w_down), [((seq, units), bf16)] * 2 + part_rows,
        )

    def feed_backward(d, slope, pieces=PIECES):
        return call(
            functools.partial(feed_backward_kernel, len(d)),
            (*d, slope, w_down, w_up),
            [((seq, units), bf16), ((1, units), f32), ((rows, width), bf16)] + rows_in(pieces),
        )

    def weight_part(*products):
        inputs = [item for lefts, right in products for item in (*lefts, right)]
        n = sum(right.shape[1] for _, right in products)
        return call(
            functools.partial(weight_part_kernel, [len(lefts) for lefts, _ in products]),
            inputs, [((width, n), f32)], scratch=[pltpu.VMEM((width, seq), bf16)],
        )[0]

    block = width // 8
    small_shape = (16, width)

    def tail_rows(n, small):
        return 2 * 16 * width // n if small else 0

    def blocks_out(count, n, tail, pieces):
        rows_each = [count // pieces * block] * pieces
        rows_each[-1] += tail
        return [((rows, n), bf16) for rows in [count * block + tail] + rows_each]

    def weight_grad(order, other, *products, small=(), pieces=1):
        inputs, parts = [], []
        for lefts, right, columns, place_other in products:
            inputs += [*lefts, right]
            parts.append((len(lefts), *columns, place_other))
        n = sum(last - first for _, first, last, _ in parts)
        keep, *send = call(
            functools.partial(weight_grad_kernel, order, parts, len(small), pieces),
            (*small, *inputs, other), blocks_out(4, n, tail_rows(n, small), pieces),
            scratch=[pltpu.VMEM((width, seq), bf16), pltpu.VMEM((width, n), bf16)],
        )
        return keep, [swap(item, order[0]) for item in send]

    def fold(order, stage, keep, got, small=False, pieces=1):
        n = keep.shape[1]
        count = 8 >> stage
        keep, *send = call(
            functools.partial(fold_kernel, block, small and small_shape, count, pieces), (keep, *got),
            blocks_out(count // 2, n, tail_rows(n, small), pieces),
        )
        return keep, [swap(item, order[stage]) for item in send]

    def fold_last(keep, got, turn=False, parts=1, small=False):
        shapes = [(block, keep.shape[1] // parts)] * parts
        if turn:
            shapes[0] = shapes[0][::-1]
        if small:
            shapes += [(1, width)] * 8 + [(1, 4 * units)]
        return call(
            functools.partial(fold_last_kernel, block, small and small_shape, turn), (keep, *got),
            [(shape, f32) for shape in shapes], final=range(len(shapes)),
        )

    def chip_sum(mine, *theirs, extra=0):
        return call(chip_sum_kernel, (mine, *map(swap_core, theirs)), [((rows + extra, width), bf16)])[0]

    def norm_one(tok, mine, got, pieces=3):
        return call(
            norm_one_kernel,
            (tok, mine, got, row(b_out), row(gain_one), row(shift_one)),
            [((rows, width), f32), ((rows, width), f32), ((rows, 1), f32)] + rows_in(pieces),
        )

    def norm_two(hidden, mine, got):
        first = SENT_FIRST * rows // 16
        sent = [((first, width), bf16), ((rows - first, width), bf16)]
        return call(
            functools.partial(norm_two_kernel, len(sent)),
            (hidden, mine, got, row(b_down), row(gain_two), row(shift_two), cotangent),
            [((rows, width), f32)] * 2 + sent + rows_in(SPLIT_LOW),
        )

    def norm_one_back(mine, got, resid, normed, inverse):
        return call(
            functools.partial(norm_one_back_kernel, len(resid)),
            (mine, got, *resid, normed, inverse, row(gain_one)),
            [((rows, width), f32), ((8, width), f32)] + piece_rows,
        )

    def add(a, b, final=()):
        return call(add_kernel, (a, b), [(a.shape, f32)], final=final)[0]

    def both(low):
        return (*low, *map(swap_core, low))

    Y, Z1, Z2 = 0, 1, 2
    swap = lambda blocks, bit: swap_batch(blocks, 1 << bit)
    tok_other = swap_chip(tokens)
    tok_own_c = swap_core(tokens)
    *kept_own, pm, pc0, pc1 = attention_forward(0, tokens, tok_own_c)
    mine_own = chip_sum(pm, pc0, pc1)
    from_own = swap_chip(mine_own)
    tok_other_c = [swap_core(item) for item in call(functools.partial(split_kernel, 1), (tok_other,), rows_in(3))]
    *kept_other, pm, pc0, pc1 = attention_forward(1, tok_other, *tok_other_c)
    mine_other = chip_sum(pm, pc0, pc1)
    from_other = swap_chip(mine_other)
    hidden_other, n1_other, r1_other, *low = norm_one(tok_other, mine_other, from_own)
    hid_other = both(low)
    act_other, slope_other, *part = feed_forward(hid_other)
    mine_other = chip_sum(*part)
    got_own = swap_chip(mine_other)
    hidden_own, n1_own, r1_own, *low = norm_one(tokens, mine_own, from_other)
    hid_own = both(low)
    act_own, slope_own, *part = feed_forward(hid_own)
    mine_own = chip_sum(*part)
    n2_own, dr2_own, sent0, sent1, *low = norm_two(hidden_own, mine_own, got_own)
    low_other = [swap_chip(sent0), swap_chip(sent1)]
    ds_own = both(low)
    di_own, bup_own, *part = feed_backward(ds_own, slope_own)
    mine_own = chip_sum(*part, extra=0 * EXTRA)
    from_own = swap_chip(mine_own)
    output, sums_two = call(
        result_kernel, (n2_own, row(gain_two), row(shift_two), cotangent, dr2_own),
        [((rows, width), bf16), ((8, width), f32)], final=(0,),
    )
    down_own = weight_part((ds_own, act_own))
    up_own = weight_part((hid_own, di_own))
    ds_other = both(call(functools.partial(split_kernel, 2), low_other, rows_in(SPLIT_DS)))
    order_down = (Z1, Z2, Y)
    order_up = (Y, Z1, Z2)
    order_a = (Y, Z1, Z2)
    order_b = (Y, Z2, Z1)
    down = weight_grad(order_down, down_own, (ds_other, act_other, (0, units), 0), pieces=1)
    di_other, bup_other, *part = feed_backward(ds_other, slope_other, SPLIT_FB)
    up = weight_grad(order_up, up_own, (hid_other, di_other, (0, units), 0), pieces=1)
    mine_other = chip_sum(*part, extra=1 * EXTRA)
    from_other = swap_chip(mine_other)
    _, _, *low = norm_one_back(mine_other, from_own, low_other, n1_other, r1_other)
    db_other = both(low)
    gqkv_other, bias_other = attention_backward(1, db_other, kept_other)
    part = input_grad(gqkv_other)
    tok_all = ((tokens, tok_own_c), (tok_other, *tok_other_c))
    attn_other = weight_part((db_other, kept_other[4]), (tok_all[1], gqkv_other))
    mine_other = chip_sum(*part, extra=0)
    got_final = swap_chip(mine_other)
    dr1_own, sums_one, *low = norm_one_back(mine_own, from_other, (dr2_own,), n1_own, r1_own)
    db_own = both(low)
    down = fold(order_down, 1, *down, pieces=1)
    gqkv_own, bias_own = attention_backward(0, db_own, kept_own)
    b = weight_grad(order_b, attn_other, (tok_all[0], gqkv_own, (0, 2 * local), local), pieces=2)
    up = fold(order_up, 1, *up, pieces=1)
    small, = call(
        pack_kernel, (sums_one, sums_two, bias_own, bias_other, bup_own, bup_other), [((16, width), f32)]
    )
    small_got = swap_core(small)
    small = add(small, small_got)
    small_got = swap_chip(small)
    small = add(small, small_got)
    a = weight_grad(
        order_a,
        attn_other,
        (db_own, kept_own[4], (0, local), 0),
        (tok_all[0], gqkv_own, (2 * local, 3 * local), 3 * local),
        small=(small,), pieces=2,
    )
    b = fold(order_b, 1, *b, pieces=1)
    down = fold(order_down, 2, *down, pieces=1)
    part = input_grad(gqkv_own)
    part_c = [swap_core(item) for item in part[1:]]
    a = fold(order_a, 1, *a, small=True, pieces=2)
    up = fold(order_up, 2, *up, pieces=1)
    g_down, = fold_last(*down, turn=True)
    b = fold(order_b, 2, *b, pieces=1)
    a = fold(order_a, 2, *a, small=True, pieces=1)
    g_up, = fold_last(*up)
    grad_tokens, = call(
        last_sum_kernel, (part[0], *part_c, got_final, dr1_own), [((rows, width), bf16)], final=(0,)
    )
    g_out, g_value, *small = fold_last(*a, turn=True, parts=2, small=True)
    g_query, g_key = fold_last(*b, parts=2)
    gg1, gs1, gbo, gg2, gs2, gbd, gbq, gbv, gbu = [item.reshape(-1) for item in small]
    return (
        output,
        grad_tokens,
        g_query,
        gbq,
        g_key,
        g_value,
        gbv,
        g_out,
        gbo,
        gg1,
        gs1,
        g_up,
        gbu,
        g_down,
        gbd,
        gg2,
        gs2,
    )


def solution(mesh):
    fast = mesh.shape["tp"] == 4 and mesh.shape["batch"] == 8
    return jax.shard_map(
        fast_body if fast else body,
        mesh=mesh,
        in_specs=(
            P(("batch", "tp"), None),
            P("batch"),
            P(None, "tp"),
            P("tp"),
            P(None, "tp"),
            P(None, "tp"),
            P("tp"),
            P("tp", None),
            P(),
            P(),
            P(),
            P(None, "tp"),
            P("tp"),
            P("tp", None),
            P(),
            P(),
            P(),
            P(("batch", "tp"), None),
        ),
        out_specs=(
            P(("batch", "tp"), None),
            P(("batch", "tp"), None),
            P("batch", "tp"),
            P(),
            P("batch", "tp"),
            P("batch", "tp"),
            P(),
            P("tp", "batch"),
            P(),
            P(),
            P(),
            P("batch", "tp"),
            P(),
            P("tp", "batch"),
            P(),
            P(),
            P(),
        ),
        check_vma=False,
    )
```

```python
import functools
import math

import jax
import jax.numpy as jnp
from jax import lax
from jax.experimental import pallas as pl
from jax.experimental.pallas import tpu as pltpu
from jax.sharding import PartitionSpec as P

HEAD_DIM = 64


epsilon = 1e-05
negative = -1e30


def product(left, right):
    return jnp.dot(left, right, preferred_element_type=jnp.float32)


def over_rows(left, right):
    return lax.dot_general(
        left, right, (((0,), (0,)), ((), ())), preferred_element_type=jnp.float32
    )


def against(left, right):
    return lax.dot_general(
        left, right, (((1,), (1,)), ((), ())), preferred_element_type=jnp.float32
    )


def norm_forward(resid, gain, shift):
    middle = jnp.mean(resid, axis=-1, keepdims=True)
    centred = resid - middle
    variance = jnp.mean(centred * centred, axis=-1, keepdims=True)
    inverse = lax.rsqrt(variance + epsilon)
    normed = centred * inverse
    return (normed * gain + shift, normed, inverse)


def norm_backward(upstream, normed, inverse, gain):
    scaled = upstream * gain
    first = jnp.mean(scaled, axis=-1, keepdims=True)
    second = jnp.mean(scaled * normed, axis=-1, keepdims=True)
    grad_resid = inverse * (scaled - first - normed * second)
    return (grad_resid, jnp.sum(upstream * normed, axis=0), jnp.sum(upstream, axis=0))


def gelu_slope(inner):
    cumulative = 0.5 * (1.0 + lax.erf(inner * 2.0 ** (-0.5)))
    density = jnp.exp(-0.5 * inner * inner) * (2.0 * math.pi) ** (-0.5)
    return cumulative + inner * density


def attend_forward(query, keys, values, valid):
    scores = jnp.einsum("qhd,khd->hqk", query, keys, preferred_element_type=jnp.float32)
    scores = jnp.where(valid[None, None, :], scores, negative)
    highest = jnp.max(scores, axis=-1, keepdims=True)
    exponent = jnp.exp(scores - highest)
    total = jnp.sum(exponent, axis=-1, keepdims=True)
    probs = (exponent / total).astype(jnp.bfloat16)
    mixed = jnp.einsum("hqk,khd->qhd", probs, values, preferred_element_type=jnp.float32)
    return (mixed.astype(jnp.bfloat16), highest + jnp.log(total))


def attend_backward(query, keys, values, valid, log_total, grad_mixed):
    scores = jnp.einsum("qhd,khd->hqk", query, keys, preferred_element_type=jnp.float32)
    scores = jnp.where(valid[None, None, :], scores, negative)
    probs = jnp.exp(scores - log_total)
    rounded = probs.astype(jnp.bfloat16)
    grad_values = jnp.einsum(
        "hqk,qhd->khd", rounded, grad_mixed, preferred_element_type=jnp.float32
    )
    grad_probs = jnp.einsum("qhd,khd->hqk", grad_mixed, values, preferred_element_type=jnp.float32)
    centre = jnp.sum(probs * grad_probs, axis=-1, keepdims=True)
    grad_scores = (probs * (grad_probs - centre)).astype(jnp.bfloat16)
    grad_query = jnp.einsum("hqk,khd->qhd", grad_scores, keys, preferred_element_type=jnp.float32)
    grad_keys = jnp.einsum("hqk,qhd->khd", grad_scores, query, preferred_element_type=jnp.float32)
    return (grad_query, grad_keys, grad_values)


def spread(piece):
    return lax.all_gather(piece, "tp", axis=0, tiled=True)


def collect(piece):
    return lax.psum_scatter(
        piece.astype(jnp.bfloat16), "tp", scatter_dimension=0, tiled=True
    ).astype(jnp.float32)


def forward_item(item):
    return attend_forward(item[0], item[1], item[2], item[3])


def backward_item(item):
    return attend_backward(item[0], item[1], item[2], item[3], item[4], item[5])


def body(
    tokens,
    lengths,
    w_query,
    b_query,
    w_key,
    w_value,
    b_value,
    w_out,
    b_out,
    gain_one,
    shift_one,
    w_up,
    b_up,
    w_down,
    b_down,
    gain_two,
    shift_two,
    cotangent,
):
    head_dim = HEAD_DIM
    scale = head_dim ** (-0.5)
    own_rows = tokens.shape[0]
    seq_len = 2 * own_rows
    tp_index = lax.axis_index("tp")
    upstream = cotangent.astype(jnp.float32)
    gathered = spread(tokens)
    groups = gathered.shape[0] // seq_len
    local_width = w_query.shape[1]
    local_heads = local_width // head_dim
    query = ((product(gathered, w_query) + b_query) * scale).astype(jnp.bfloat16)
    keys = product(gathered, w_key).astype(jnp.bfloat16)
    values = (product(gathered, w_value) + b_value).astype(jnp.bfloat16)
    shaped = (groups, seq_len, local_heads, head_dim)
    positions = jnp.arange(seq_len, dtype=jnp.int32)
    valid = positions[None, :] < lengths[:, None]
    query_s = query.reshape(shaped)
    keys_s = keys.reshape(shaped)
    values_s = values.reshape(shaped)
    mixed_s, log_total = lax.map(forward_item, (query_s, keys_s, values_s, valid))
    mixed = mixed_s.reshape(-1, local_width)
    branch = collect(product(mixed, w_out)) + b_out
    hidden, normed_one, inverse_one = norm_forward(
        tokens.astype(jnp.float32) + branch, gain_one, shift_one
    )
    hidden_all = spread(hidden.astype(jnp.bfloat16))
    inner = product(hidden_all, w_up) + b_up
    act = jax.nn.gelu(inner, approximate=False).astype(jnp.bfloat16)
    second = collect(product(act, w_down)) + b_down
    result, normed_two, inverse_two = norm_forward(hidden + second, gain_two, shift_two)
    grad_resid_two, grad_gain_two, grad_shift_two = norm_backward(
        upstream, normed_two, inverse_two, gain_two
    )
    grad_second = grad_resid_two.astype(jnp.bfloat16)
    grad_second_all = spread(grad_second)
    grad_w_down = over_rows(act, grad_second_all)
    grad_inner = (against(grad_second_all, w_down) * gelu_slope(inner)).astype(jnp.bfloat16)
    grad_w_up = over_rows(hidden_all, grad_inner)
    grad_hidden = collect(against(grad_inner, w_up)) + grad_resid_two
    grad_resid_one, grad_gain_one, grad_shift_one = norm_backward(
        grad_hidden, normed_one, inverse_one, gain_one
    )
    grad_branch = grad_resid_one.astype(jnp.bfloat16)
    grad_branch_all = spread(grad_branch)
    grad_w_out = over_rows(mixed, grad_branch_all)
    grad_mixed = against(grad_branch_all, w_out).astype(jnp.bfloat16)
    grad_query_s, grad_keys_s, grad_values_s = lax.map(
        backward_item, (query_s, keys_s, values_s, valid, log_total, grad_mixed.reshape(shaped))
    )
    grad_query = (grad_query_s.astype(jnp.bfloat16) * scale).reshape(-1, local_width)
    grad_keys = grad_keys_s.astype(jnp.bfloat16).reshape(-1, local_width)
    grad_values = grad_values_s.astype(jnp.bfloat16).reshape(-1, local_width)
    grad_w_query = over_rows(gathered, grad_query)
    grad_w_key = over_rows(gathered, grad_keys)
    grad_w_value = over_rows(gathered, grad_values)
    grad_input_part = (
        against(grad_query, w_query) + against(grad_keys, w_key) + against(grad_values, w_value)
    )
    grad_tokens = (collect(grad_input_part) + grad_resid_one).astype(jnp.bfloat16)
    width = w_query.shape[0]
    hidden_units = w_up.shape[1] * lax.axis_size("tp")
    query_bias = lax.dynamic_update_slice(
        jnp.zeros((width,), jnp.float32),
        jnp.sum(grad_query.astype(jnp.float32), axis=0),
        (tp_index * local_width,),
    )
    value_bias = lax.dynamic_update_slice(
        jnp.zeros((width,), jnp.float32),
        jnp.sum(grad_values.astype(jnp.float32), axis=0),
        (tp_index * local_width,),
    )
    up_bias = lax.dynamic_update_slice(
        jnp.zeros((hidden_units,), jnp.float32),
        jnp.sum(grad_inner.astype(jnp.float32), axis=0),
        (tp_index * w_up.shape[1],),
    )
    big = (grad_w_query, grad_w_key, grad_w_value, grad_w_out, grad_w_up, grad_w_down)
    out_bias = jnp.sum(grad_branch.astype(jnp.float32), axis=0)
    down_bias = jnp.sum(grad_second.astype(jnp.float32), axis=0)
    small = (
        query_bias,
        value_bias,
        out_bias,
        grad_gain_one,
        grad_shift_one,
        up_bias,
        down_bias,
        grad_gain_two,
        grad_shift_two,
    )
    summed = lax.psum(
        (small[0], small[1], small[2], small[3], small[4], small[5], small[6], small[7], small[8]),
        ("batch", "tp"),
    )
    shards = (
        lax.psum_scatter(
            big[0].astype(jnp.bfloat16), "batch", scatter_dimension=0, tiled=True
        ).astype(jnp.float32),
        lax.psum_scatter(
            big[1].astype(jnp.bfloat16), "batch", scatter_dimension=0, tiled=True
        ).astype(jnp.float32),
        lax.psum_scatter(
            big[2].astype(jnp.bfloat16), "batch", scatter_dimension=0, tiled=True
        ).astype(jnp.float32),
        lax.psum_scatter(
            big[3].astype(jnp.bfloat16), "batch", scatter_dimension=1, tiled=True
        ).astype(jnp.float32),
        lax.psum_scatter(
            big[4].astype(jnp.bfloat16), "batch", scatter_dimension=0, tiled=True
        ).astype(jnp.float32),
        lax.psum_scatter(
            big[5].astype(jnp.bfloat16), "batch", scatter_dimension=1, tiled=True
        ).astype(jnp.float32),
    )
    output = result.astype(jnp.bfloat16)
    return (
        output,
        grad_tokens,
        shards[0],
        summed[0],
        shards[1],
        shards[2],
        summed[1],
        shards[3],
        summed[2],
        summed[3],
        summed[4],
        shards[4],
        summed[5],
        shards[5],
        summed[6],
        summed[7],
        summed[8],
    )


def swap_core(piece):
    return lax.ppermute(piece, "tp", [(i, i ^ 1) for i in range(4)])


def swap_chip(piece):
    return lax.ppermute(piece, "tp", [(i, i ^ 2) for i in range(4)])


def swap_batch(piece, bits):
    return lax.ppermute(piece, "batch", [(i, i ^ bits) for i in range(8)])


MEBI = 1024 * 1024
PIECES = 2
SPLIT_DS = 2
SPLIT_LOW = 2
SENT_FIRST = 10
SPLIT_FB = 2
EXTRA = 16


def run_kernel(turn, kernel, inputs, outputs, scalars=(), hbm=(), scratch=(), final=(), limit=24):
    read = len(scalars) + len(hbm) + len(inputs)

    def wrapped(*refs):
        kernel(*refs[:read], *refs[read + len(turn) :])

    results = pl.pallas_call(
        wrapped,
        out_shape=[
            (pltpu.HBM if i in final else pltpu.VMEM)(shape, kind)
            for i, (shape, kind) in enumerate(outputs)
        ],
        in_specs=[pl.BlockSpec(memory_space=pltpu.SMEM)] * len(scalars)
        + [pl.BlockSpec(memory_space=pltpu.HBM)] * len(hbm)
        + [pl.BlockSpec(memory_space=pltpu.VMEM)] * len(inputs)
        + [pl.BlockSpec(memory_space=pl.ANY)] * len(turn),
        out_specs=[pl.BlockSpec(memory_space=pltpu.VMEM)] * len(outputs),
        scratch_shapes=list(scratch),
        compiler_params=pltpu.CompilerParams(vmem_limit_bytes=limit * MEBI),
        cost_estimate=pl.CostEstimate(flops=1, bytes_accessed=1, transcendentals=0),
    )(*scalars, *[pltpu.with_memory_space_constraint(item, pltpu.HBM) for item in hbm], *inputs, *turn)
    results = list(results)
    turn[:] = [pltpu.with_memory_space_constraint(results[0], pltpu.HBM) if 0 in final else results[0]]
    return results


def fetch(sources, targets, sems):
    copies = [pltpu.make_async_copy(a, b, sems.at[i]) for i, (a, b) in enumerate(zip(sources, targets))]
    for copy in copies:
        copy.start()
    return copies


def wide(ref):
    return ref[...].astype(jnp.float32)


def head(ref, like):
    return ref[: like.shape[0], :].astype(jnp.float32)


def joined(refs):
    return refs[0][...] if len(refs) == 1 else jnp.concatenate([ref[...] for ref in refs], axis=0)


def cut_rows(whole, refs):
    at = 0
    for ref in refs:
        ref[...] = whole[at : at + ref.shape[0]]
        at += ref.shape[0]


def valid_slots(shape, axis, which, lengths):
    seq = shape[axis]
    tp_index = lax.axis_index("tp")
    slot = lax.broadcasted_iota(jnp.int32, shape, axis) + (tp_index % 2) * (seq // 2)
    slot = jnp.where(slot >= seq, slot - seq, slot)
    return slot < lengths[(tp_index // 2) ^ which]


def apart(two, lane):
    zero = jnp.zeros_like(two)
    return jnp.concatenate(
        [jnp.where(lane < HEAD_DIM, two, zero), jnp.where(lane < HEAD_DIM, zero, two)], axis=0
    )


def together(two, lane):
    half = two.shape[0] // 2
    return jnp.where(lane < HEAD_DIM, two[:half], two[half:])


def split_kernel(count, *refs):
    cut_rows(joined(refs[:count]), refs[count:])


def attention_forward_kernel(which, count, load, lengths, *refs):
    if load:
        hbm, bq, bv, xm, refs = refs[:4], refs[4], refs[5], refs[6], refs[7:]
        xc, refs = refs[:count], refs[count:]
        q_ref, k_ref, v_ref, lse_ref, mixed_ref, pm_ref, *pc_refs = refs[: 6 + PIECES]
        wq, wk, wv, wo, sems = refs[6 + PIECES :]
        copies = fetch(hbm, (wq, wk, wv, wo), sems)
    else:
        wq, wk, wv, wo, bq, bv, xm = refs[:7]
        xc, refs = refs[7 : 7 + count], refs[7 + count :]
        q_ref, k_ref, v_ref, lse_ref, mixed_ref, pm_ref, *pc_refs = refs
        copies = []
    rows = xm.shape[0]
    seq = 2 * rows
    local = wq.shape[1]
    scale = HEAD_DIM ** (-0.5)
    x_all = (xm[...], joined(xc))
    for copy in copies[:1]:
        copy.wait()
    for i, x in enumerate(x_all):
        part = pl.ds(i * rows, rows)
        q_ref[part, :] = ((product(x, wq[...]) + wide(bq)) * scale).astype(jnp.bfloat16)
    for copy in copies[1:3]:
        copy.wait()
    for i, x in enumerate(x_all):
        part = pl.ds(i * rows, rows)
        k_ref[part, :] = product(x, wk[...]).astype(jnp.bfloat16)
        v_ref[part, :] = (product(x, wv[...]) + wide(bv)).astype(jnp.bfloat16)
    valid = valid_slots((1, seq), 1, which, lengths)
    lane = lax.broadcasted_iota(jnp.int32, (seq, 128), 1)
    lse_all = jnp.zeros((seq, 128), jnp.float32)
    for pair in range(local // (2 * HEAD_DIM)):
        cut = slice(2 * pair * HEAD_DIM, 2 * (pair + 1) * HEAD_DIM)
        scores = against(apart(q_ref[:, cut], lane), k_ref[:, cut])
        probs = []
        for i in range(2):
            some = jnp.where(valid, scores[i * seq : (i + 1) * seq], negative)
            highest = jnp.max(some, axis=-1, keepdims=True)
            exponent = jnp.exp(some - highest)
            total = jnp.sum(exponent, axis=-1, keepdims=True)
            probs.append((exponent * (1.0 / total)).astype(jnp.bfloat16))
            lse_all = jnp.where(lane == 2 * pair + i, highest + jnp.log(total), lse_all)
        mixed = product(jnp.concatenate(probs, axis=0), v_ref[:, cut])
        mixed_ref[:, cut] = together(mixed, lane).astype(jnp.bfloat16)
    lse_ref[...] = lse_all.T[:8, :]
    for copy in copies[3:]:
        copy.wait()
    cut_rows(product(mixed_ref[rows:, :], wo[...]).astype(jnp.bfloat16), pc_refs)
    pm_ref[...] = product(mixed_ref[:rows, :], wo[...]).astype(jnp.bfloat16)


def attention_backward_kernel(which, count, lengths, wo, *refs):
    db, refs = refs[:count], refs[count:]
    q_ref, k_ref, v_ref, lse_ref, mixed_ref, g_ref, bias_ref, dm_ref = refs
    seq, local = q_ref.shape
    scale = HEAD_DIM ** (-0.5)
    dm_ref[...] = against(joined(db), wo[...]).astype(jnp.bfloat16)
    crossed = (wide(dm_ref) * wide(mixed_ref)).T
    valid = valid_slots((seq, 1), 0, which, lengths)
    lane = lax.broadcasted_iota(jnp.int32, (seq, 2 * HEAD_DIM), 1)
    for pair in range(local // (2 * HEAD_DIM)):
        cut = slice(2 * pair * HEAD_DIM, 2 * (pair + 1) * HEAD_DIM)
        q, k, v, dm = q_ref[:, cut], k_ref[:, cut], v_ref[:, cut], dm_ref[:, cut]
        k_both, v_both = apart(k, lane), apart(v, lane)
        scores = against(k_both, q)
        change = against(v_both, dm)
        probs_low, grads = [], []
        for i in range(2):
            h = 2 * pair + i
            part = slice(i * seq, (i + 1) * seq)
            centre = jnp.sum(crossed[h * HEAD_DIM : (h + 1) * HEAD_DIM, :], axis=0, keepdims=True)
            probs = jnp.exp(jnp.where(valid, scores[part], negative) - lse_ref[h : h + 1, :])
            probs_low.append(probs.astype(jnp.bfloat16))
            grads.append((probs * (change[part] - centre)).astype(jnp.bfloat16))
        probs_low = jnp.concatenate(probs_low, axis=0)
        grads = jnp.concatenate(grads, axis=0)
        shift = lambda n: slice(n * local + 2 * pair * HEAD_DIM, n * local + 2 * (pair + 1) * HEAD_DIM)
        g_ref[:, shift(2)] = together(product(probs_low, dm), lane).astype(jnp.bfloat16)
        g_ref[:, shift(1)] = together(product(grads, q), lane).astype(jnp.bfloat16)
        grad_q = product(k_both.T, grads).astype(jnp.bfloat16) * scale
        g_ref[:, cut] = grad_q.T.astype(jnp.bfloat16)
    bias_ref[...] = jnp.sum(wide(g_ref), axis=0, keepdims=True)


def input_grad_kernel(g_ref, wq, wk, wv, pm_ref, *pc_refs):
    rows = pm_ref.shape[0]
    local = wq.shape[1]
    total = (
        against(g_ref[:, :local], wq[...])
        + against(g_ref[:, local : 2 * local], wk[...])
        + against(g_ref[:, 2 * local :], wv[...])
    ).astype(jnp.bfloat16)
    pm_ref[...] = total[:rows]
    cut_rows(total[rows:], pc_refs)


def split_columns(rows, cut, total, pm_ref, pc_refs):
    pm_ref[:, cut] = total[:rows].astype(jnp.bfloat16)
    at = rows
    for ref in pc_refs:
        ref[:, cut] = total[at : at + ref.shape[0]].astype(jnp.bfloat16)
        at += ref.shape[0]


def feed_forward_kernel(count, *refs):
    h, refs = refs[:count], refs[count:]
    wu, bu, wd, act_ref, slope_ref, pm_ref, *pc_refs = refs
    x = joined(h)
    step = 256
    for j in range(wu.shape[1] // step):
        cut = slice(j * step, (j + 1) * step)
        inner = product(x, wu[:, cut]) + bu[:, cut].astype(jnp.float32)
        cumulative = 0.5 * (1.0 + lax.erf(inner * 2.0 ** (-0.5)))
        density = jnp.exp(-0.5 * inner * inner) * (2.0 * math.pi) ** (-0.5)
        act_ref[:, cut] = (inner * cumulative).astype(jnp.bfloat16)
        slope_ref[:, cut] = (cumulative + inner * density).astype(jnp.bfloat16)
    for j in range(wd.shape[1] // step):
        cut = slice(j * step, (j + 1) * step)
        split_columns(x.shape[0] // 2, cut, product(act_ref[...], wd[:, cut]), pm_ref, pc_refs)


def feed_backward_kernel(count, *refs):
    d, refs = refs[:count], refs[count:]
    slope, wd, wu, grad_ref, bias_ref, pm_ref, *pc_refs = refs
    x = joined(d)
    step = 256
    for j in range(wu.shape[1] // step):
        cut = slice(j * step, (j + 1) * step)
        grad = (against(x, wd[cut, :]) * slope[:, cut].astype(jnp.float32)).astype(jnp.bfloat16)
        grad_ref[:, cut] = grad
        bias_ref[:, cut] = jnp.sum(grad.astype(jnp.float32), axis=0, keepdims=True)
    for j in range(wu.shape[0] // step):
        cut = slice(j * step, (j + 1) * step)
        split_columns(x.shape[0] // 2, cut, against(grad_ref[...], wu[cut, :]), pm_ref, pc_refs)


def turned(lefts, left_ref):
    left_ref[...] = joined(lefts).T


def weight_part_kernel(counts, *refs):
    *refs, out_ref, left_ref = refs
    step = 256
    done = 0
    for count in counts:
        lefts, right, refs = refs[:count], refs[count], refs[count + 1 :]
        turned(lefts, left_ref)
        for start in range(0, right.shape[1], step):
            out_ref[:, done : done + step] = product(left_ref[...], right[:, start : start + step])
            done += step


def weight_grad_kernel(order, parts, tail, pieces, *refs):
    *refs, left_ref, low_ref = refs
    refs, (other_ref, keep_ref, *send_refs) = refs[: -2 - pieces], refs[-2 - pieces :]
    if tail:
        small, refs = refs[0][...], refs[1:]
        put_small(small, keep_ref, send_refs[-1])
    me = lax.axis_index("batch")
    block = low_ref.shape[0] // 8
    step = 256
    done = 0
    for count, first, last, place_other in parts:
        lefts, right, refs = refs[:count], refs[count], refs[count + 1 :]
        turned(lefts, left_ref)
        for start in range(first, last, step):
            cut = slice(done, done + step)
            at = place_other + start - first
            total = other_ref[:, at : at + step] + product(left_ref[...], right[:, start : start + step])
            done += step
            low_ref[:, cut] = total.astype(jnp.bfloat16)
            for place in range(8):
                bits = [(place >> bit) & 1 for bit in (2, 1, 0)]
                r = sum(value << bit for value, bit in zip(bits, order))
                rows = pl.ds(pl.multiple_of((me ^ r) * block, block), block)
                put_block([keep_ref] if bits[0] == 0 else send_refs, place % 4, block, 4, low_ref[rows, cut], cut)


def put_block(refs, place, block, count, value, cut=slice(None)):
    share = count // len(refs)
    at = (place % share) * block
    refs[place // share][at : at + block, cut] = value


def put_small(small, *refs):
    high = small.astype(jnp.bfloat16)
    low = (small - high.astype(jnp.float32)).astype(jnp.bfloat16)
    for ref in refs:
        n = ref.shape[1]
        at = ref.shape[0] - 2 * small.size // n
        for piece in (high, low):
            for start in range(0, small.shape[1], n):
                ref[at : at + small.shape[0], :] = piece[:, start : start + n]
                at += small.shape[0]


def take_small(ref, shape):
    n = ref.shape[1]
    count = shape[1] // n
    at = ref.shape[0] - 2 * count * shape[0]
    pieces = [ref[at + i * shape[0] : at + (i + 1) * shape[0], :].astype(jnp.float32) for i in range(2 * count)]
    return jnp.concatenate([a + b for a, b in zip(pieces[:count], pieces[count:])], axis=1)


def chip_sum_kernel(mine, *refs):
    *got, out_ref = refs
    rows = mine.shape[0]
    out_ref[:rows, :] = (wide(mine) + joined(got).astype(jnp.float32)).astype(jnp.bfloat16)
    if out_ref.shape[0] > rows:
        out_ref[rows:, :] = jnp.zeros((out_ref.shape[0] - rows, out_ref.shape[1]), jnp.bfloat16)


def last_sum_kernel(mine, *refs):
    *got, other, resid, out_ref = refs
    out_ref[...] = (wide(mine) + joined(got).astype(jnp.float32) + head(other, mine) + resid[...]).astype(jnp.bfloat16)


def norm_one_kernel(tok, mine, got, bias, gain, shift, hidden_ref, normed_ref, inverse_ref, *low_refs):
    resid = wide(tok) + (head(mine, tok) + head(got, tok) + wide(bias))
    hidden, normed, inverse = norm_forward(resid, gain[...], shift[...])
    hidden_ref[...] = hidden
    normed_ref[...] = normed
    inverse_ref[...] = inverse
    cut_rows(hidden.astype(jnp.bfloat16), low_refs)


def norm_two_kernel(count, hidden, mine, got, bias, gain, shift, cot, normed_ref, grad_ref, *low_refs):
    resid = hidden[...] + (head(mine, hidden) + head(got, hidden) + wide(bias))
    _, normed, inverse = norm_forward(resid, gain[...], shift[...])
    normed_ref[...] = normed
    grad, _, _ = norm_backward(wide(cot), normed, inverse, gain[...])
    grad_ref[...] = grad
    low = grad.astype(jnp.bfloat16)
    cut_rows(low, low_refs[:count])
    cut_rows(low, low_refs[count:])


def result_kernel(normed, gain, shift, cot, grad, out_ref, sums_ref):
    out_ref[...] = (normed[...] * gain[...] + shift[...]).astype(jnp.bfloat16)
    upstream = wide(cot)
    sums_ref[0:1, :] = jnp.sum(upstream * normed[...], axis=0, keepdims=True)
    sums_ref[1:2, :] = jnp.sum(upstream, axis=0, keepdims=True)
    low = grad[...].astype(jnp.bfloat16)
    sums_ref[2:3, :] = jnp.sum(low.astype(jnp.float32), axis=0, keepdims=True)


def norm_one_back_kernel(count, mine, got, *refs):
    resid, (normed, inverse, gain, grad_ref, sums_ref, *low_refs) = refs[:count], refs[count:]
    upstream = head(mine, normed) + head(got, normed) + joined(resid).astype(jnp.float32)
    grad, gain_sum, shift_sum = norm_backward(upstream, normed[...], inverse[...], gain[...])
    low = grad.astype(jnp.bfloat16)
    grad_ref[...] = grad
    cut_rows(low, low_refs)
    sums_ref[0:1, :] = gain_sum[None]
    sums_ref[1:2, :] = shift_sum[None]
    sums_ref[2:3, :] = jnp.sum(low.astype(jnp.float32), axis=0, keepdims=True)


def fold_kernel(block, small, count, pieces, keep, *refs):
    refs, send_refs = refs[:-pieces], refs[-pieces:]
    *got, keep_ref = refs
    share = count // len(got)
    for r in range(count):
        at = (r % share) * block
        arrived = got[r // share][at : at + block, :]
        full = (keep[r * block : (r + 1) * block, :].astype(jnp.float32) + arrived.astype(jnp.float32)).astype(jnp.bfloat16)
        put_block([keep_ref] if 2 * r < count else send_refs, r % (count // 2), block, count // 2, full)
    if small:
        put_small(take_small(keep, small) + take_small(got[-1], small), keep_ref, send_refs[-1])


def fold_last_kernel(block, small, turn, keep, got, *out):
    full = keep[:block, :].astype(jnp.float32) + got[:block, :].astype(jnp.float32)
    if small:
        *out, wide_ref = out
        out, rows = out[:-8], out[-8:]
        sums = take_small(keep, small) + take_small(got, small)
        for i, ref in enumerate(rows):
            ref[...] = sums[i : i + 1, :]
        for i in range(4):
            wide_ref[:, i * small[1] : (i + 1) * small[1]] = sums[8 + i : 9 + i, :]
    n = full.shape[1] // len(out)
    for i, ref in enumerate(out):
        part = full[:, i * n : (i + 1) * n]
        ref[...] = part.T if turn and i == 0 else part


def pack_kernel(one, two, bias0, bias1, up0, up1, out_ref):
    tp_index = lax.axis_index("tp")
    out_ref[...] = jnp.zeros(out_ref.shape, jnp.float32)
    out_ref[0:3, :] = one[0:3, :]
    out_ref[3:6, :] = two[0:3, :]
    local = bias0.shape[1] // 3
    lanes = pl.ds(pl.multiple_of(tp_index * local, 128), local)
    bias = bias0[...] + bias1[...]
    out_ref[6:7, lanes] = bias[:, :local]
    out_ref[7:8, lanes] = bias[:, 2 * local :]
    out_ref[pl.ds(8 + tp_index, 1), :] = up0[...] + up1[...]


def add_kernel(a, b, out_ref):
    out_ref[...] = a[...] + b[...]


def fast_body(
    tokens,
    lengths,
    w_query,
    b_query,
    w_key,
    w_value,
    b_value,
    w_out,
    b_out,
    gain_one,
    shift_one,
    w_up,
    b_up,
    w_down,
    b_down,
    gain_two,
    shift_two,
    cotangent,
):
    bf16, f32 = jnp.bfloat16, jnp.float32
    rows, width = tokens.shape
    seq = 2 * rows
    local = w_query.shape[1]
    units = w_up.shape[1]
    row = lambda item: item.reshape(1, -1)

    def rows_in(count):
        tile = 16
        tiles = rows // tile
        sizes = [(tiles // count + (i < tiles % count)) * tile for i in range(count)]
        return [((size, width), bf16) for size in sizes]

    piece_rows = rows_in(PIECES)
    part_rows = [((rows, width), bf16)] + piece_rows

    call = functools.partial(run_kernel, [])

    weights = []

    def attention_forward(which, xm, *xc):
        load = not weights
        results = call(
            functools.partial(attention_forward_kernel, which, len(xc), load),
            (*weights, row(b_query), row(b_value), xm, *xc),
            [((seq, local), bf16)] * 3
            + [((8, seq), f32), ((seq, local), bf16)]
            + part_rows
            + ([((width, local), bf16)] * 3 + [((local, width), bf16)]) * load,
            (lengths,),
            (w_query, w_key, w_value, w_out) if load else (),
            [pltpu.SemaphoreType.DMA((4,))] * load,
        )
        if load:
            weights[:] = results[-4:]
            del results[-4:]
        return results

    def attention_backward(which, db, kept):
        return call(
            functools.partial(attention_backward_kernel, which, len(db)),
            (weights[3], *db, *kept),
            [((seq, 3 * local), bf16), ((1, 3 * local), f32)],
            (lengths,),
            scratch=[pltpu.VMEM((seq, local), bf16)],
        )

    def input_grad(g):
        return call(input_grad_kernel, (g, *weights[:3]), part_rows)

    def feed_forward(h):
        return call(
            functools.partial(feed_forward_kernel, len(h)),
            (*h, w_up, row(b_up), w_down), [((seq, units), bf16)] * 2 + part_rows,
        )

    def feed_backward(d, slope, pieces=PIECES):
        return call(
            functools.partial(feed_backward_kernel, len(d)),
            (*d, slope, w_down, w_up),
            [((seq, units), bf16), ((1, units), f32), ((rows, width), bf16)] + rows_in(pieces),
        )

    def weight_part(*products):
        inputs = [item for lefts, right in products for item in (*lefts, right)]
        n = sum(right.shape[1] for _, right in products)
        return call(
            functools.partial(weight_part_kernel, [len(lefts) for lefts, _ in products]),
            inputs, [((width, n), f32)], scratch=[pltpu.VMEM((width, seq), bf16)],
        )[0]

    block = width // 8
    small_shape = (16, width)

    def tail_rows(n, small):
        return 2 * 16 * width // n if small else 0

    def blocks_out(count, n, tail, pieces):
        rows_each = [count // pieces * block] * pieces
        rows_each[-1] += tail
        return [((rows, n), bf16) for rows in [count * block + tail] + rows_each]

    def weight_grad(order, other, *products, small=(), pieces=1):
        inputs, parts = [], []
        for lefts, right, columns, place_other in products:
            inputs += [*lefts, right]
            parts.append((len(lefts), *columns, place_other))
        n = sum(last - first for _, first, last, _ in parts)
        keep, *send = call(
            functools.partial(weight_grad_kernel, order, parts, len(small), pieces),
            (*small, *inputs, other), blocks_out(4, n, tail_rows(n, small), pieces),
            scratch=[pltpu.VMEM((width, seq), bf16), pltpu.VMEM((width, n), bf16)],
        )
        return keep, [swap(item, order[0]) for item in send]

    def fold(order, stage, keep, got, small=False, pieces=1):
        n = keep.shape[1]
        count = 8 >> stage
        keep, *send = call(
            functools.partial(fold_kernel, block, small and small_shape, count, pieces), (keep, *got),
            blocks_out(count // 2, n, tail_rows(n, small), pieces),
        )
        return keep, [swap(item, order[stage]) for item in send]

    def fold_last(keep, got, turn=False, parts=1, small=False):
        shapes = [(block, keep.shape[1] // parts)] * parts
        if turn:
            shapes[0] = shapes[0][::-1]
        if small:
            shapes += [(1, width)] * 8 + [(1, 4 * units)]
        return call(
            functools.partial(fold_last_kernel, block, small and small_shape, turn), (keep, *got),
            [(shape, f32) for shape in shapes], final=range(len(shapes)),
        )

    def chip_sum(mine, *theirs, extra=0):
        return call(chip_sum_kernel, (mine, *map(swap_core, theirs)), [((rows + extra, width), bf16)])[0]

    def norm_one(tok, mine, got, pieces=3):
        return call(
            norm_one_kernel,
            (tok, mine, got, row(b_out), row(gain_one), row(shift_one)),
            [((rows, width), f32), ((rows, width), f32), ((rows, 1), f32)] + rows_in(pieces),
        )

    def norm_two(hidden, mine, got):
        first = SENT_FIRST * rows // 16
        sent = [((first, width), bf16), ((rows - first, width), bf16)]
        return call(
            functools.partial(norm_two_kernel, len(sent)),
            (hidden, mine, got, row(b_down), row(gain_two), row(shift_two), cotangent),
            [((rows, width), f32)] * 2 + sent + rows_in(SPLIT_LOW),
        )

    def norm_one_back(mine, got, resid, normed, inverse):
        return call(
            functools.partial(norm_one_back_kernel, len(resid)),
            (mine, got, *resid, normed, inverse, row(gain_one)),
            [((rows, width), f32), ((8, width), f32)] + piece_rows,
        )

    def add(a, b, final=()):
        return call(add_kernel, (a, b), [(a.shape, f32)], final=final)[0]

    def both(low):
        return (*low, *map(swap_core, low))

    Y, Z1, Z2 = 0, 1, 2
    swap = lambda blocks, bit: swap_batch(blocks, 1 << bit)
    tok_other = swap_chip(tokens)
    tok_own_c = swap_core(tokens)
    *kept_own, pm, pc0, pc1 = attention_forward(0, tokens, tok_own_c)
    mine_own = chip_sum(pm, pc0, pc1)
    from_own = swap_chip(mine_own)
    tok_other_c = [swap_core(item) for item in call(functools.partial(split_kernel, 1), (tok_other,), rows_in(3))]
    *kept_other, pm, pc0, pc1 = attention_forward(1, tok_other, *tok_other_c)
    mine_other = chip_sum(pm, pc0, pc1)
    from_other = swap_chip(mine_other)
    hidden_other, n1_other, r1_other, *low = norm_one(tok_other, mine_other, from_own)
    hid_other = both(low)
    act_other, slope_other, *part = feed_forward(hid_other)
    mine_other = chip_sum(*part)
    got_own = swap_chip(mine_other)
    hidden_own, n1_own, r1_own, *low = norm_one(tokens, mine_own, from_other)
    hid_own = both(low)
    act_own, slope_own, *part = feed_forward(hid_own)
    mine_own = chip_sum(*part)
    n2_own, dr2_own, sent0, sent1, *low = norm_two(hidden_own, mine_own, got_own)
    low_other = [swap_chip(sent0), swap_chip(sent1)]
    ds_own = both(low)
    di_own, bup_own, *part = feed_backward(ds_own, slope_own)
    mine_own = chip_sum(*part, extra=0 * EXTRA)
    from_own = swap_chip(mine_own)
    output, sums_two = call(
        result_kernel, (n2_own, row(gain_two), row(shift_two), cotangent, dr2_own),
        [((rows, width), bf16), ((8, width), f32)], final=(0,),
    )
    down_own = weight_part((ds_own, act_own))
    up_own = weight_part((hid_own, di_own))
    ds_other = both(call(functools.partial(split_kernel, 2), low_other, rows_in(SPLIT_DS)))
    order_down = (Z1, Z2, Y)
    order_up = (Y, Z1, Z2)
    order_a = (Y, Z1, Z2)
    order_b = (Y, Z2, Z1)
    down = weight_grad(order_down, down_own, (ds_other, act_other, (0, units), 0), pieces=1)
    di_other, bup_other, *part = feed_backward(ds_other, slope_other, SPLIT_FB)
    up = weight_grad(order_up, up_own, (hid_other, di_other, (0, units), 0), pieces=1)
    mine_other = chip_sum(*part, extra=1 * EXTRA)
    from_other = swap_chip(mine_other)
    _, _, *low = norm_one_back(mine_other, from_own, low_other, n1_other, r1_other)
    db_other = both(low)
    gqkv_other, bias_other = attention_backward(1, db_other, kept_other)
    part = input_grad(gqkv_other)
    tok_all = ((tokens, tok_own_c), (tok_other, *tok_other_c))
    attn_other = weight_part((db_other, kept_other[4]), (tok_all[1], gqkv_other))
    mine_other = chip_sum(*part, extra=0)
    got_final = swap_chip(mine_other)
    dr1_own, sums_one, *low = norm_one_back(mine_own, from_other, (dr2_own,), n1_own, r1_own)
    db_own = both(low)
    down = fold(order_down, 1, *down, pieces=1)
    gqkv_own, bias_own = attention_backward(0, db_own, kept_own)
    b = weight_grad(order_b, attn_other, (tok_all[0], gqkv_own, (0, 2 * local), local), pieces=2)
    up = fold(order_up, 1, *up, pieces=1)
    small, = call(
        pack_kernel, (sums_one, sums_two, bias_own, bias_other, bup_own, bup_other), [((16, width), f32)]
    )
    small_got = swap_core(small)
    small = add(small, small_got)
    small_got = swap_chip(small)
    small = add(small, small_got)
    a = weight_grad(
        order_a,
        attn_other,
        (db_own, kept_own[4], (0, local), 0),
        (tok_all[0], gqkv_own, (2 * local, 3 * local), 3 * local),
        small=(small,), pieces=2,
    )
    b = fold(order_b, 1, *b, pieces=1)
    down = fold(order_down, 2, *down, pieces=1)
    part = input_grad(gqkv_own)
    part_c = [swap_core(item) for item in part[1:]]
    a = fold(order_a, 1, *a, small=True, pieces=2)
    up = fold(order_up, 2, *up, pieces=1)
    g_down, = fold_last(*down, turn=True)
    b = fold(order_b, 2, *b, pieces=1)
    a = fold(order_a, 2, *a, small=True, pieces=1)
    g_up, = fold_last(*up)
    g_query, g_key = fold_last(*b, parts=2)
    grad_tokens, = call(
        last_sum_kernel, (part[0], *part_c, got_final, dr1_own), [((rows, width), bf16)], final=(0,)
    )
    g_out, g_value, *small = fold_last(*a, turn=True, parts=2, small=True)
    gg1, gs1, gbo, gg2, gs2, gbd, gbq, gbv, gbu = [item.reshape(-1) for item in small]
    return (
        output,
        grad_tokens,
        g_query,
        gbq,
        g_key,
        g_value,
        gbv,
        g_out,
        gbo,
        gg1,
        gs1,
        g_up,
        gbu,
        g_down,
        gbd,
        gg2,
        gs2,
    )


def solution(mesh):
    fast = mesh.shape["tp"] == 4 and mesh.shape["batch"] == 8
    return jax.shard_map(
        fast_body if fast else body,
        mesh=mesh,
        in_specs=(
            P(("batch", "tp"), None),
            P("batch"),
            P(None, "tp"),
            P("tp"),
            P(None, "tp"),
            P(None, "tp"),
            P("tp"),
            P("tp", None),
            P(),
            P(),
            P(),
            P(None, "tp"),
            P("tp"),
            P("tp", None),
            P(),
            P(),
            P(),
            P(("batch", "tp"), None),
        ),
        out_specs=(
            P(("batch", "tp"), None),
            P(("batch", "tp"), None),
            P("batch", "tp"),
            P(),
            P("batch", "tp"),
            P("batch", "tp"),
            P(),
            P("tp", "batch"),
            P(),
            P(),
            P(),
            P("batch", "tp"),
            P(),
            P("tp", "batch"),
            P(),
            P(),
            P(),
        ),
        check_vma=False,
    )
```

```python
import functools
import math

import jax
import jax.numpy as jnp
from jax import lax
from jax.experimental import pallas as pl
from jax.experimental.pallas import tpu as pltpu
from jax.sharding import PartitionSpec as P

HEAD_DIM = 64


epsilon = 1e-05
negative = -1e30


def product(left, right):
    return jnp.dot(left, right, preferred_element_type=jnp.float32)


def over_rows(left, right):
    return lax.dot_general(
        left, right, (((0,), (0,)), ((), ())), preferred_element_type=jnp.float32
    )


def against(left, right):
    return lax.dot_general(
        left, right, (((1,), (1,)), ((), ())), preferred_element_type=jnp.float32
    )


def norm_forward(resid, gain, shift):
    middle = jnp.mean(resid, axis=-1, keepdims=True)
    centred = resid - middle
    variance = jnp.mean(centred * centred, axis=-1, keepdims=True)
    inverse = lax.rsqrt(variance + epsilon)
    normed = centred * inverse
    return (normed * gain + shift, normed, inverse)


def norm_backward(upstream, normed, inverse, gain):
    scaled = upstream * gain
    first = jnp.mean(scaled, axis=-1, keepdims=True)
    second = jnp.mean(scaled * normed, axis=-1, keepdims=True)
    grad_resid = inverse * (scaled - first - normed * second)
    return (grad_resid, jnp.sum(upstream * normed, axis=0), jnp.sum(upstream, axis=0))


def gelu_slope(inner):
    cumulative = 0.5 * (1.0 + lax.erf(inner * 2.0 ** (-0.5)))
    density = jnp.exp(-0.5 * inner * inner) * (2.0 * math.pi) ** (-0.5)
    return cumulative + inner * density


def attend_forward(query, keys, values, valid):
    scores = jnp.einsum("qhd,khd->hqk", query, keys, preferred_element_type=jnp.float32)
    scores = jnp.where(valid[None, None, :], scores, negative)
    highest = jnp.max(scores, axis=-1, keepdims=True)
    exponent = jnp.exp(scores - highest)
    total = jnp.sum(exponent, axis=-1, keepdims=True)
    probs = (exponent / total).astype(jnp.bfloat16)
    mixed = jnp.einsum("hqk,khd->qhd", probs, values, preferred_element_type=jnp.float32)
    return (mixed.astype(jnp.bfloat16), highest + jnp.log(total))


def attend_backward(query, keys, values, valid, log_total, grad_mixed):
    scores = jnp.einsum("qhd,khd->hqk", query, keys, preferred_element_type=jnp.float32)
    scores = jnp.where(valid[None, None, :], scores, negative)
    probs = jnp.exp(scores - log_total)
    rounded = probs.astype(jnp.bfloat16)
    grad_values = jnp.einsum(
        "hqk,qhd->khd", rounded, grad_mixed, preferred_element_type=jnp.float32
    )
    grad_probs = jnp.einsum("qhd,khd->hqk", grad_mixed, values, preferred_element_type=jnp.float32)
    centre = jnp.sum(probs * grad_probs, axis=-1, keepdims=True)
    grad_scores = (probs * (grad_probs - centre)).astype(jnp.bfloat16)
    grad_query = jnp.einsum("hqk,khd->qhd", grad_scores, keys, preferred_element_type=jnp.float32)
    grad_keys = jnp.einsum("hqk,qhd->khd", grad_scores, query, preferred_element_type=jnp.float32)
    return (grad_query, grad_keys, grad_values)


def spread(piece):
    return lax.all_gather(piece, "tp", axis=0, tiled=True)


def collect(piece):
    return lax.psum_scatter(
        piece.astype(jnp.bfloat16), "tp", scatter_dimension=0, tiled=True
    ).astype(jnp.float32)


def forward_item(item):
    return attend_forward(item[0], item[1], item[2], item[3])


def backward_item(item):
    return attend_backward(item[0], item[1], item[2], item[3], item[4], item[5])


def body(
    tokens,
    lengths,
    w_query,
    b_query,
    w_key,
    w_value,
    b_value,
    w_out,
    b_out,
    gain_one,
    shift_one,
    w_up,
    b_up,
    w_down,
    b_down,
    gain_two,
    shift_two,
    cotangent,
):
    head_dim = HEAD_DIM
    scale = head_dim ** (-0.5)
    own_rows = tokens.shape[0]
    seq_len = 2 * own_rows
    tp_index = lax.axis_index("tp")
    upstream = cotangent.astype(jnp.float32)
    gathered = spread(tokens)
    groups = gathered.shape[0] // seq_len
    local_width = w_query.shape[1]
    local_heads = local_width // head_dim
    query = ((product(gathered, w_query) + b_query) * scale).astype(jnp.bfloat16)
    keys = product(gathered, w_key).astype(jnp.bfloat16)
    values = (product(gathered, w_value) + b_value).astype(jnp.bfloat16)
    shaped = (groups, seq_len, local_heads, head_dim)
    positions = jnp.arange(seq_len, dtype=jnp.int32)
    valid = positions[None, :] < lengths[:, None]
    query_s = query.reshape(shaped)
    keys_s = keys.reshape(shaped)
    values_s = values.reshape(shaped)
    mixed_s, log_total = lax.map(forward_item, (query_s, keys_s, values_s, valid))
    mixed = mixed_s.reshape(-1, local_width)
    branch = collect(product(mixed, w_out)) + b_out
    hidden, normed_one, inverse_one = norm_forward(
        tokens.astype(jnp.float32) + branch, gain_one, shift_one
    )
    hidden_all = spread(hidden.astype(jnp.bfloat16))
    inner = product(hidden_all, w_up) + b_up
    act = jax.nn.gelu(inner, approximate=False).astype(jnp.bfloat16)
    second = collect(product(act, w_down)) + b_down
    result, normed_two, inverse_two = norm_forward(hidden + second, gain_two, shift_two)
    grad_resid_two, grad_gain_two, grad_shift_two = norm_backward(
        upstream, normed_two, inverse_two, gain_two
    )
    grad_second = grad_resid_two.astype(jnp.bfloat16)
    grad_second_all = spread(grad_second)
    grad_w_down = over_rows(act, grad_second_all)
    grad_inner = (against(grad_second_all, w_down) * gelu_slope(inner)).astype(jnp.bfloat16)
    grad_w_up = over_rows(hidden_all, grad_inner)
    grad_hidden = collect(against(grad_inner, w_up)) + grad_resid_two
    grad_resid_one, grad_gain_one, grad_shift_one = norm_backward(
        grad_hidden, normed_one, inverse_one, gain_one
    )
    grad_branch = grad_resid_one.astype(jnp.bfloat16)
    grad_branch_all = spread(grad_branch)
    grad_w_out = over_rows(mixed, grad_branch_all)
    grad_mixed = against(grad_branch_all, w_out).astype(jnp.bfloat16)
    grad_query_s, grad_keys_s, grad_values_s = lax.map(
        backward_item, (query_s, keys_s, values_s, valid, log_total, grad_mixed.reshape(shaped))
    )
    grad_query = (grad_query_s.astype(jnp.bfloat16) * scale).reshape(-1, local_width)
    grad_keys = grad_keys_s.astype(jnp.bfloat16).reshape(-1, local_width)
    grad_values = grad_values_s.astype(jnp.bfloat16).reshape(-1, local_width)
    grad_w_query = over_rows(gathered, grad_query)
    grad_w_key = over_rows(gathered, grad_keys)
    grad_w_value = over_rows(gathered, grad_values)
    grad_input_part = (
        against(grad_query, w_query) + against(grad_keys, w_key) + against(grad_values, w_value)
    )
    grad_tokens = (collect(grad_input_part) + grad_resid_one).astype(jnp.bfloat16)
    width = w_query.shape[0]
    hidden_units = w_up.shape[1] * lax.axis_size("tp")
    query_bias = lax.dynamic_update_slice(
        jnp.zeros((width,), jnp.float32),
        jnp.sum(grad_query.astype(jnp.float32), axis=0),
        (tp_index * local_width,),
    )
    value_bias = lax.dynamic_update_slice(
        jnp.zeros((width,), jnp.float32),
        jnp.sum(grad_values.astype(jnp.float32), axis=0),
        (tp_index * local_width,),
    )
    up_bias = lax.dynamic_update_slice(
        jnp.zeros((hidden_units,), jnp.float32),
        jnp.sum(grad_inner.astype(jnp.float32), axis=0),
        (tp_index * w_up.shape[1],),
    )
    big = (grad_w_query, grad_w_key, grad_w_value, grad_w_out, grad_w_up, grad_w_down)
    out_bias = jnp.sum(grad_branch.astype(jnp.float32), axis=0)
    down_bias = jnp.sum(grad_second.astype(jnp.float32), axis=0)
    small = (
        query_bias,
        value_bias,
        out_bias,
        grad_gain_one,
        grad_shift_one,
        up_bias,
        down_bias,
        grad_gain_two,
        grad_shift_two,
    )
    summed = lax.psum(
        (small[0], small[1], small[2], small[3], small[4], small[5], small[6], small[7], small[8]),
        ("batch", "tp"),
    )
    shards = (
        lax.psum_scatter(
            big[0].astype(jnp.bfloat16), "batch", scatter_dimension=0, tiled=True
        ).astype(jnp.float32),
        lax.psum_scatter(
            big[1].astype(jnp.bfloat16), "batch", scatter_dimension=0, tiled=True
        ).astype(jnp.float32),
        lax.psum_scatter(
            big[2].astype(jnp.bfloat16), "batch", scatter_dimension=0, tiled=True
        ).astype(jnp.float32),
        lax.psum_scatter(
            big[3].astype(jnp.bfloat16), "batch", scatter_dimension=1, tiled=True
        ).astype(jnp.float32),
        lax.psum_scatter(
            big[4].astype(jnp.bfloat16), "batch", scatter_dimension=0, tiled=True
        ).astype(jnp.float32),
        lax.psum_scatter(
            big[5].astype(jnp.bfloat16), "batch", scatter_dimension=1, tiled=True
        ).astype(jnp.float32),
    )
    output = result.astype(jnp.bfloat16)
    return (
        output,
        grad_tokens,
        shards[0],
        summed[0],
        shards[1],
        shards[2],
        summed[1],
        shards[3],
        summed[2],
        summed[3],
        summed[4],
        shards[4],
        summed[5],
        shards[5],
        summed[6],
        summed[7],
        summed[8],
    )


def swap_core(piece):
    return lax.ppermute(piece, "tp", [(i, i ^ 1) for i in range(4)])


def swap_chip(piece):
    return lax.ppermute(piece, "tp", [(i, i ^ 2) for i in range(4)])


def swap_batch(piece, bits):
    return lax.ppermute(piece, "batch", [(i, i ^ bits) for i in range(8)])


MEBI = 1024 * 1024
PIECES = 2
SPLIT_DS = 2
SPLIT_LOW = 2
SENT_FIRST = 10
SPLIT_FB = 2
EXTRA = 16


def run_kernel(turn, kernel, inputs, outputs, scalars=(), hbm=(), scratch=(), final=(), limit=24):
    read = len(scalars) + len(hbm) + len(inputs)

    def wrapped(*refs):
        kernel(*refs[:read], *refs[read + len(turn) :])

    results = pl.pallas_call(
        wrapped,
        out_shape=[
            (pltpu.HBM if i in final else pltpu.VMEM)(shape, kind)
            for i, (shape, kind) in enumerate(outputs)
        ],
        in_specs=[pl.BlockSpec(memory_space=pltpu.SMEM)] * len(scalars)
        + [pl.BlockSpec(memory_space=pltpu.HBM)] * len(hbm)
        + [pl.BlockSpec(memory_space=pltpu.VMEM)] * len(inputs)
        + [pl.BlockSpec(memory_space=pl.ANY)] * len(turn),
        out_specs=[pl.BlockSpec(memory_space=pltpu.VMEM)] * len(outputs),
        scratch_shapes=list(scratch),
        compiler_params=pltpu.CompilerParams(vmem_limit_bytes=limit * MEBI),
        cost_estimate=pl.CostEstimate(flops=1, bytes_accessed=1, transcendentals=0),
    )(*scalars, *[pltpu.with_memory_space_constraint(item, pltpu.HBM) for item in hbm], *inputs, *turn)
    results = list(results)
    turn[:] = [pltpu.with_memory_space_constraint(results[0], pltpu.HBM) if 0 in final else results[0]]
    return results


def fetch(sources, targets, sems):
    copies = [pltpu.make_async_copy(a, b, sems.at[i]) for i, (a, b) in enumerate(zip(sources, targets))]
    for copy in copies:
        copy.start()
    return copies


def wide(ref):
    return ref[...].astype(jnp.float32)


def head(ref, like):
    return ref[: like.shape[0], :].astype(jnp.float32)


def joined(refs):
    return refs[0][...] if len(refs) == 1 else jnp.concatenate([ref[...] for ref in refs], axis=0)


def cut_rows(whole, refs):
    at = 0
    for ref in refs:
        ref[...] = whole[at : at + ref.shape[0]]
        at += ref.shape[0]


def valid_slots(shape, axis, which, lengths):
    seq = shape[axis]
    tp_index = lax.axis_index("tp")
    slot = lax.broadcasted_iota(jnp.int32, shape, axis) + (tp_index % 2) * (seq // 2)
    slot = jnp.where(slot >= seq, slot - seq, slot)
    return slot < lengths[(tp_index // 2) ^ which]


def apart(two, lane):
    zero = jnp.zeros_like(two)
    return jnp.concatenate(
        [jnp.where(lane < HEAD_DIM, two, zero), jnp.where(lane < HEAD_DIM, zero, two)], axis=0
    )


def together(two, lane):
    half = two.shape[0] // 2
    return jnp.where(lane < HEAD_DIM, two[:half], two[half:])


def split_kernel(count, *refs):
    cut_rows(joined(refs[:count]), refs[count:])


def attention_forward_kernel(which, count, load, lengths, *refs):
    if load:
        hbm, bq, bv, xm, refs = refs[:4], refs[4], refs[5], refs[6], refs[7:]
        xc, refs = refs[:count], refs[count:]
        q_ref, k_ref, v_ref, lse_ref, mixed_ref, pm_ref, *pc_refs = refs[: 6 + PIECES]
        wq, wk, wv, wo, sems = refs[6 + PIECES :]
        copies = fetch(hbm, (wq, wk, wv, wo), sems)
    else:
        wq, wk, wv, wo, bq, bv, xm = refs[:7]
        xc, refs = refs[7 : 7 + count], refs[7 + count :]
        q_ref, k_ref, v_ref, lse_ref, mixed_ref, pm_ref, *pc_refs = refs
        copies = []
    rows = xm.shape[0]
    seq = 2 * rows
    local = wq.shape[1]
    scale = HEAD_DIM ** (-0.5)
    x_all = (xm[...], joined(xc))
    for copy in copies[:1]:
        copy.wait()
    for i, x in enumerate(x_all):
        part = pl.ds(i * rows, rows)
        q_ref[part, :] = ((product(x, wq[...]) + wide(bq)) * scale).astype(jnp.bfloat16)
    for copy in copies[1:3]:
        copy.wait()
    for i, x in enumerate(x_all):
        part = pl.ds(i * rows, rows)
        k_ref[part, :] = product(x, wk[...]).astype(jnp.bfloat16)
        v_ref[part, :] = (product(x, wv[...]) + wide(bv)).astype(jnp.bfloat16)
    valid = valid_slots((1, seq), 1, which, lengths)
    lane = lax.broadcasted_iota(jnp.int32, (seq, 128), 1)
    lse_all = jnp.zeros((seq, 128), jnp.float32)
    for pair in range(local // (2 * HEAD_DIM)):
        cut = slice(2 * pair * HEAD_DIM, 2 * (pair + 1) * HEAD_DIM)
        scores = against(apart(q_ref[:, cut], lane), k_ref[:, cut])
        probs = []
        for i in range(2):
            some = jnp.where(valid, scores[i * seq : (i + 1) * seq], negative)
            highest = jnp.max(some, axis=-1, keepdims=True)
            exponent = jnp.exp(some - highest)
            total = jnp.sum(exponent, axis=-1, keepdims=True)
            probs.append((exponent * (1.0 / total)).astype(jnp.bfloat16))
            lse_all = jnp.where(lane == 2 * pair + i, highest + jnp.log(total), lse_all)
        mixed = product(jnp.concatenate(probs, axis=0), v_ref[:, cut])
        mixed_ref[:, cut] = together(mixed, lane).astype(jnp.bfloat16)
    lse_ref[...] = lse_all.T[:8, :]
    for copy in copies[3:]:
        copy.wait()
    cut_rows(product(mixed_ref[rows:, :], wo[...]).astype(jnp.bfloat16), pc_refs)
    pm_ref[...] = product(mixed_ref[:rows, :], wo[...]).astype(jnp.bfloat16)


def attention_backward_kernel(which, count, lengths, wo, *refs):
    db, refs = refs[:count], refs[count:]
    q_ref, k_ref, v_ref, lse_ref, mixed_ref, g_ref, bias_ref, dm_ref = refs
    seq, local = q_ref.shape
    scale = HEAD_DIM ** (-0.5)
    dm_ref[...] = against(joined(db), wo[...]).astype(jnp.bfloat16)
    crossed = (wide(dm_ref) * wide(mixed_ref)).T
    valid = valid_slots((seq, 1), 0, which, lengths)
    lane = lax.broadcasted_iota(jnp.int32, (seq, 2 * HEAD_DIM), 1)
    for pair in range(local // (2 * HEAD_DIM)):
        cut = slice(2 * pair * HEAD_DIM, 2 * (pair + 1) * HEAD_DIM)
        q, k, v, dm = q_ref[:, cut], k_ref[:, cut], v_ref[:, cut], dm_ref[:, cut]
        k_both, v_both = apart(k, lane), apart(v, lane)
        scores = against(k_both, q)
        change = against(v_both, dm)
        probs_low, grads = [], []
        for i in range(2):
            h = 2 * pair + i
            part = slice(i * seq, (i + 1) * seq)
            centre = jnp.sum(crossed[h * HEAD_DIM : (h + 1) * HEAD_DIM, :], axis=0, keepdims=True)
            probs = jnp.exp(jnp.where(valid, scores[part], negative) - lse_ref[h : h + 1, :])
            probs_low.append(probs.astype(jnp.bfloat16))
            grads.append((probs * (change[part] - centre)).astype(jnp.bfloat16))
        probs_low = jnp.concatenate(probs_low, axis=0)
        grads = jnp.concatenate(grads, axis=0)
        shift = lambda n: slice(n * local + 2 * pair * HEAD_DIM, n * local + 2 * (pair + 1) * HEAD_DIM)
        g_ref[:, shift(2)] = together(product(probs_low, dm), lane).astype(jnp.bfloat16)
        g_ref[:, shift(1)] = together(product(grads, q), lane).astype(jnp.bfloat16)
        grad_q = product(k_both.T, grads).astype(jnp.bfloat16) * scale
        g_ref[:, cut] = grad_q.T.astype(jnp.bfloat16)
    bias_ref[...] = jnp.sum(wide(g_ref), axis=0, keepdims=True)


def input_grad_kernel(g_ref, wq, wk, wv, pm_ref, *pc_refs):
    rows = pm_ref.shape[0]
    local = wq.shape[1]
    total = (
        against(g_ref[:, :local], wq[...])
        + against(g_ref[:, local : 2 * local], wk[...])
        + against(g_ref[:, 2 * local :], wv[...])
    ).astype(jnp.bfloat16)
    pm_ref[...] = total[:rows]
    cut_rows(total[rows:], pc_refs)


def split_columns(rows, cut, total, pm_ref, pc_refs):
    pm_ref[:, cut] = total[:rows].astype(jnp.bfloat16)
    at = rows
    for ref in pc_refs:
        ref[:, cut] = total[at : at + ref.shape[0]].astype(jnp.bfloat16)
        at += ref.shape[0]


def feed_forward_kernel(count, *refs):
    h, refs = refs[:count], refs[count:]
    wu, bu, wd, act_ref, slope_ref, pm_ref, *pc_refs = refs
    x = joined(h)
    step = 256
    for j in range(wu.shape[1] // step):
        cut = slice(j * step, (j + 1) * step)
        inner = product(x, wu[:, cut]) + bu[:, cut].astype(jnp.float32)
        cumulative = 0.5 * (1.0 + lax.erf(inner * 2.0 ** (-0.5)))
        density = jnp.exp(-0.5 * inner * inner) * (2.0 * math.pi) ** (-0.5)
        act_ref[:, cut] = (inner * cumulative).astype(jnp.bfloat16)
        slope_ref[:, cut] = (cumulative + inner * density).astype(jnp.bfloat16)
    for j in range(wd.shape[1] // step):
        cut = slice(j * step, (j + 1) * step)
        split_columns(x.shape[0] // 2, cut, product(act_ref[...], wd[:, cut]), pm_ref, pc_refs)


def feed_backward_kernel(count, *refs):
    d, refs = refs[:count], refs[count:]
    slope, wd, wu, grad_ref, bias_ref, pm_ref, *pc_refs = refs
    x = joined(d)
    step = 256
    for j in range(wu.shape[1] // step):
        cut = slice(j * step, (j + 1) * step)
        grad = (against(x, wd[cut, :]) * slope[:, cut].astype(jnp.float32)).astype(jnp.bfloat16)
        grad_ref[:, cut] = grad
        bias_ref[:, cut] = jnp.sum(grad.astype(jnp.float32), axis=0, keepdims=True)
    for j in range(wu.shape[0] // step):
        cut = slice(j * step, (j + 1) * step)
        split_columns(x.shape[0] // 2, cut, against(grad_ref[...], wu[cut, :]), pm_ref, pc_refs)


def turned(lefts, left_ref):
    left_ref[...] = joined(lefts).T


def weight_part_kernel(counts, *refs):
    *refs, out_ref, left_ref = refs
    step = 256
    done = 0
    for count in counts:
        lefts, right, refs = refs[:count], refs[count], refs[count + 1 :]
        turned(lefts, left_ref)
        for start in range(0, right.shape[1], step):
            out_ref[:, done : done + step] = product(left_ref[...], right[:, start : start + step])
            done += step


def weight_grad_kernel(order, parts, tail, pieces, *refs):
    *refs, left_ref, low_ref = refs
    refs, (other_ref, keep_ref, *send_refs) = refs[: -2 - pieces], refs[-2 - pieces :]
    if tail:
        small, refs = refs[0][...], refs[1:]
        put_small(small, keep_ref, send_refs[-1])
    me = lax.axis_index("batch")
    block = low_ref.shape[0] // 8
    step = 256
    done = 0
    for count, first, last, place_other in parts:
        lefts, right, refs = refs[:count], refs[count], refs[count + 1 :]
        turned(lefts, left_ref)
        for start in range(first, last, step):
            cut = slice(done, done + step)
            at = place_other + start - first
            total = other_ref[:, at : at + step] + product(left_ref[...], right[:, start : start + step])
            done += step
            low_ref[:, cut] = total.astype(jnp.bfloat16)
            for place in range(8):
                bits = [(place >> bit) & 1 for bit in (2, 1, 0)]
                r = sum(value << bit for value, bit in zip(bits, order))
                rows = pl.ds(pl.multiple_of((me ^ r) * block, block), block)
                put_block([keep_ref] if bits[0] == 0 else send_refs, place % 4, block, 4, low_ref[rows, cut], cut)


def put_block(refs, place, block, count, value, cut=slice(None)):
    share = count // len(refs)
    at = (place % share) * block
    refs[place // share][at : at + block, cut] = value


def put_small(small, *refs):
    high = small.astype(jnp.bfloat16)
    low = (small - high.astype(jnp.float32)).astype(jnp.bfloat16)
    for ref in refs:
        n = ref.shape[1]
        at = ref.shape[0] - 2 * small.size // n
        for piece in (high, low):
            for start in range(0, small.shape[1], n):
                ref[at : at + small.shape[0], :] = piece[:, start : start + n]
                at += small.shape[0]


def take_small(ref, shape):
    n = ref.shape[1]
    count = shape[1] // n
    at = ref.shape[0] - 2 * count * shape[0]
    pieces = [ref[at + i * shape[0] : at + (i + 1) * shape[0], :].astype(jnp.float32) for i in range(2 * count)]
    return jnp.concatenate([a + b for a, b in zip(pieces[:count], pieces[count:])], axis=1)


def chip_sum_kernel(mine, *refs):
    *got, out_ref = refs
    rows = mine.shape[0]
    out_ref[:rows, :] = (wide(mine) + joined(got).astype(jnp.float32)).astype(jnp.bfloat16)
    if out_ref.shape[0] > rows:
        out_ref[rows:, :] = jnp.zeros((out_ref.shape[0] - rows, out_ref.shape[1]), jnp.bfloat16)


def last_sum_kernel(mine, *refs):
    *got, other, resid, out_ref = refs
    out_ref[...] = (wide(mine) + joined(got).astype(jnp.float32) + head(other, mine) + resid[...]).astype(jnp.bfloat16)


def norm_one_kernel(tok, mine, got, bias, gain, shift, hidden_ref, normed_ref, inverse_ref, *low_refs):
    resid = wide(tok) + (head(mine, tok) + head(got, tok) + wide(bias))
    hidden, normed, inverse = norm_forward(resid, gain[...], shift[...])
    hidden_ref[...] = hidden
    normed_ref[...] = normed
    inverse_ref[...] = inverse
    cut_rows(hidden.astype(jnp.bfloat16), low_refs)


def norm_two_kernel(count, hidden, mine, got, bias, gain, shift, cot, normed_ref, grad_ref, *low_refs):
    resid = hidden[...] + (head(mine, hidden) + head(got, hidden) + wide(bias))
    _, normed, inverse = norm_forward(resid, gain[...], shift[...])
    normed_ref[...] = normed
    grad, _, _ = norm_backward(wide(cot), normed, inverse, gain[...])
    grad_ref[...] = grad
    low = grad.astype(jnp.bfloat16)
    cut_rows(low, low_refs[:count])
    cut_rows(low, low_refs[count:])


def result_kernel(normed, gain, shift, cot, grad, out_ref, sums_ref):
    out_ref[...] = (normed[...] * gain[...] + shift[...]).astype(jnp.bfloat16)
    upstream = wide(cot)
    sums_ref[0:1, :] = jnp.sum(upstream * normed[...], axis=0, keepdims=True)
    sums_ref[1:2, :] = jnp.sum(upstream, axis=0, keepdims=True)
    low = grad[...].astype(jnp.bfloat16)
    sums_ref[2:3, :] = jnp.sum(low.astype(jnp.float32), axis=0, keepdims=True)


def norm_one_back_kernel(count, mine, got, *refs):
    resid, (normed, inverse, gain, grad_ref, sums_ref, *low_refs) = refs[:count], refs[count:]
    upstream = head(mine, normed) + head(got, normed) + joined(resid).astype(jnp.float32)
    grad, gain_sum, shift_sum = norm_backward(upstream, normed[...], inverse[...], gain[...])
    low = grad.astype(jnp.bfloat16)
    grad_ref[...] = grad
    cut_rows(low, low_refs)
    sums_ref[0:1, :] = gain_sum[None]
    sums_ref[1:2, :] = shift_sum[None]
    sums_ref[2:3, :] = jnp.sum(low.astype(jnp.float32), axis=0, keepdims=True)


def fold_kernel(block, small, count, pieces, keep, *refs):
    refs, send_refs = refs[:-pieces], refs[-pieces:]
    *got, keep_ref = refs
    share = count // len(got)
    for r in range(count):
        at = (r % share) * block
        arrived = got[r // share][at : at + block, :]
        full = (keep[r * block : (r + 1) * block, :].astype(jnp.float32) + arrived.astype(jnp.float32)).astype(jnp.bfloat16)
        put_block([keep_ref] if 2 * r < count else send_refs, r % (count // 2), block, count // 2, full)
    if small:
        put_small(take_small(keep, small) + take_small(got[-1], small), keep_ref, send_refs[-1])


def fold_last_kernel(block, small, turn, keep, got, *out):
    full = keep[:block, :].astype(jnp.float32) + got[:block, :].astype(jnp.float32)
    if small:
        *out, wide_ref = out
        out, rows = out[:-8], out[-8:]
        sums = take_small(keep, small) + take_small(got, small)
        for i, ref in enumerate(rows):
            ref[...] = sums[i : i + 1, :]
        for i in range(4):
            wide_ref[:, i * small[1] : (i + 1) * small[1]] = sums[8 + i : 9 + i, :]
    n = full.shape[1] // len(out)
    for i, ref in enumerate(out):
        part = full[:, i * n : (i + 1) * n]
        ref[...] = part.T if turn and i == 0 else part


def pack_kernel(one, two, bias0, bias1, up0, up1, out_ref):
    tp_index = lax.axis_index("tp")
    out_ref[...] = jnp.zeros(out_ref.shape, jnp.float32)
    out_ref[0:3, :] = one[0:3, :]
    out_ref[3:6, :] = two[0:3, :]
    local = bias0.shape[1] // 3
    lanes = pl.ds(pl.multiple_of(tp_index * local, 128), local)
    bias = bias0[...] + bias1[...]
    out_ref[6:7, lanes] = bias[:, :local]
    out_ref[7:8, lanes] = bias[:, 2 * local :]
    out_ref[pl.ds(8 + tp_index, 1), :] = up0[...] + up1[...]


def add_kernel(a, b, out_ref):
    out_ref[...] = a[...] + b[...]


def fast_body(
    tokens,
    lengths,
    w_query,
    b_query,
    w_key,
    w_value,
    b_value,
    w_out,
    b_out,
    gain_one,
    shift_one,
    w_up,
    b_up,
    w_down,
    b_down,
    gain_two,
    shift_two,
    cotangent,
):
    bf16, f32 = jnp.bfloat16, jnp.float32
    rows, width = tokens.shape
    seq = 2 * rows
    local = w_query.shape[1]
    units = w_up.shape[1]
    row = lambda item: item.reshape(1, -1)

    def rows_in(count):
        tile = 16
        tiles = rows // tile
        sizes = [(tiles // count + (i < tiles % count)) * tile for i in range(count)]
        return [((size, width), bf16) for size in sizes]

    piece_rows = rows_in(PIECES)
    part_rows = [((rows, width), bf16)] + piece_rows

    call = functools.partial(run_kernel, [])

    weights = []

    def attention_forward(which, xm, *xc):
        load = not weights
        results = call(
            functools.partial(attention_forward_kernel, which, len(xc), load),
            (*weights, row(b_query), row(b_value), xm, *xc),
            [((seq, local), bf16)] * 3
            + [((8, seq), f32), ((seq, local), bf16)]
            + part_rows
            + ([((width, local), bf16)] * 3 + [((local, width), bf16)]) * load,
            (lengths,),
            (w_query, w_key, w_value, w_out) if load else (),
            [pltpu.SemaphoreType.DMA((4,))] * load,
        )
        if load:
            weights[:] = results[-4:]
            del results[-4:]
        return results

    def attention_backward(which, db, kept):
        return call(
            functools.partial(attention_backward_kernel, which, len(db)),
            (weights[3], *db, *kept),
            [((seq, 3 * local), bf16), ((1, 3 * local), f32)],
            (lengths,),
            scratch=[pltpu.VMEM((seq, local), bf16)],
        )

    def input_grad(g):
        return call(input_grad_kernel, (g, *weights[:3]), part_rows)

    def feed_forward(h):
        return call(
            functools.partial(feed_forward_kernel, len(h)),
            (*h, w_up, row(b_up), w_down), [((seq, units), bf16)] * 2 + part_rows,
        )

    def feed_backward(d, slope, pieces=PIECES):
        return call(
            functools.partial(feed_backward_kernel, len(d)),
            (*d, slope, w_down, w_up),
            [((seq, units), bf16), ((1, units), f32), ((rows, width), bf16)] + rows_in(pieces),
        )

    def weight_part(*products):
        inputs = [item for lefts, right in products for item in (*lefts, right)]
        n = sum(right.shape[1] for _, right in products)
        return call(
            functools.partial(weight_part_kernel, [len(lefts) for lefts, _ in products]),
            inputs, [((width, n), f32)], scratch=[pltpu.VMEM((width, seq), bf16)],
        )[0]

    block = width // 8
    small_shape = (16, width)

    def tail_rows(n, small):
        return 2 * 16 * width // n if small else 0

    def blocks_out(count, n, tail, pieces):
        rows_each = [count // pieces * block] * pieces
        rows_each[-1] += tail
        return [((rows, n), bf16) for rows in [count * block + tail] + rows_each]

    def weight_grad(order, other, *products, small=(), pieces=1):
        inputs, parts = [], []
        for lefts, right, columns, place_other in products:
            inputs += [*lefts, right]
            parts.append((len(lefts), *columns, place_other))
        n = sum(last - first for _, first, last, _ in parts)
        keep, *send = call(
            functools.partial(weight_grad_kernel, order, parts, len(small), pieces),
            (*small, *inputs, other), blocks_out(4, n, tail_rows(n, small), pieces),
            scratch=[pltpu.VMEM((width, seq), bf16), pltpu.VMEM((width, n), bf16)],
        )
        return keep, [swap(item, order[0]) for item in send]

    def fold(order, stage, keep, got, small=False, pieces=1):
        n = keep.shape[1]
        count = 8 >> stage
        keep, *send = call(
            functools.partial(fold_kernel, block, small and small_shape, count, pieces), (keep, *got),
            blocks_out(count // 2, n, tail_rows(n, small), pieces),
        )
        return keep, [swap(item, order[stage]) for item in send]

    def fold_last(keep, got, turn=False, parts=1, small=False):
        shapes = [(block, keep.shape[1] // parts)] * parts
        if turn:
            shapes[0] = shapes[0][::-1]
        if small:
            shapes += [(1, width)] * 8 + [(1, 4 * units)]
        return call(
            functools.partial(fold_last_kernel, block, small and small_shape, turn), (keep, *got),
            [(shape, f32) for shape in shapes], final=range(len(shapes)),
        )

    def chip_sum(mine, *theirs, extra=0):
        return call(chip_sum_kernel, (mine, *map(swap_core, theirs)), [((rows + extra, width), bf16)])[0]

    def norm_one(tok, mine, got, pieces=3):
        return call(
            norm_one_kernel,
            (tok, mine, got, row(b_out), row(gain_one), row(shift_one)),
            [((rows, width), f32), ((rows, width), f32), ((rows, 1), f32)] + rows_in(pieces),
        )

    def norm_two(hidden, mine, got):
        first = SENT_FIRST * rows // 16
        sent = [((first, width), bf16), ((rows - first, width), bf16)]
        return call(
            functools.partial(norm_two_kernel, len(sent)),
            (hidden, mine, got, row(b_down), row(gain_two), row(shift_two), cotangent),
            [((rows, width), f32)] * 2 + sent + rows_in(SPLIT_LOW),
        )

    def norm_one_back(mine, got, resid, normed, inverse):
        return call(
            functools.partial(norm_one_back_kernel, len(resid)),
            (mine, got, *resid, normed, inverse, row(gain_one)),
            [((rows, width), f32), ((8, width), f32)] + piece_rows,
        )

    def add(a, b, final=()):
        return call(add_kernel, (a, b), [(a.shape, f32)], final=final)[0]

    def both(low):
        return (*low, *map(swap_core, low))

    Y, Z1, Z2 = 0, 1, 2
    swap = lambda blocks, bit: swap_batch(blocks, 1 << bit)
    tok_other = swap_chip(tokens)
    tok_own_c = swap_core(tokens)
    *kept_own, pm, pc0, pc1 = attention_forward(0, tokens, tok_own_c)
    mine_own = chip_sum(pm, pc0, pc1)
    from_own = swap_chip(mine_own)
    tok_other_c = [swap_core(item) for item in call(functools.partial(split_kernel, 1), (tok_other,), rows_in(3))]
    *kept_other, pm, pc0, pc1 = attention_forward(1, tok_other, *tok_other_c)
    mine_other = chip_sum(pm, pc0, pc1)
    from_other = swap_chip(mine_other)
    hidden_other, n1_other, r1_other, *low = norm_one(tok_other, mine_other, from_own)
    hid_other = both(low)
    act_other, slope_other, *part = feed_forward(hid_other)
    mine_other = chip_sum(*part)
    got_own = swap_chip(mine_other)
    hidden_own, n1_own, r1_own, *low = norm_one(tokens, mine_own, from_other)
    hid_own = both(low)
    act_own, slope_own, *part = feed_forward(hid_own)
    mine_own = chip_sum(*part)
    n2_own, dr2_own, sent0, sent1, *low = norm_two(hidden_own, mine_own, got_own)
    low_other = [swap_chip(sent0), swap_chip(sent1)]
    ds_own = both(low)
    di_own, bup_own, *part = feed_backward(ds_own, slope_own)
    mine_own = chip_sum(*part, extra=2 * EXTRA)
    from_own = swap_chip(mine_own)
    output, sums_two = call(
        result_kernel, (n2_own, row(gain_two), row(shift_two), cotangent, dr2_own),
        [((rows, width), bf16), ((8, width), f32)], final=(0,),
    )
    down_own = weight_part((ds_own, act_own))
    up_own = weight_part((hid_own, di_own))
    ds_other = both(call(functools.partial(split_kernel, 2), low_other, rows_in(SPLIT_DS)))
    order_down = (Z1, Z2, Y)
    order_up = (Y, Z1, Z2)
    order_a = (Y, Z1, Z2)
    order_b = (Y, Z2, Z1)
    down = weight_grad(order_down, down_own, (ds_other, act_other, (0, units), 0), pieces=1)
    di_other, bup_other, *part = feed_backward(ds_other, slope_other, SPLIT_FB)
    up = weight_grad(order_up, up_own, (hid_other, di_other, (0, units), 0), pieces=1)
    mine_other = chip_sum(*part, extra=1 * EXTRA)
    from_other = swap_chip(mine_other)
    _, _, *low = norm_one_back(mine_other, from_own, low_other, n1_other, r1_other)
    db_other = both(low)
    gqkv_other, bias_other = attention_backward(1, db_other, kept_other)
    part = input_grad(gqkv_other)
    tok_all = ((tokens, tok_own_c), (tok_other, *tok_other_c))
    attn_other = weight_part((db_other, kept_other[4]), (tok_all[1], gqkv_other))
    mine_other = chip_sum(*part, extra=0)
    got_final = swap_chip(mine_other)
    dr1_own, sums_one, *low = norm_one_back(mine_own, from_other, (dr2_own,), n1_own, r1_own)
    db_own = both(low)
    down = fold(order_down, 1, *down, pieces=1)
    gqkv_own, bias_own = attention_backward(0, db_own, kept_own)
    b = weight_grad(order_b, attn_other, (tok_all[0], gqkv_own, (0, 2 * local), local), pieces=2)
    up = fold(order_up, 1, *up, pieces=1)
    small, = call(
        pack_kernel, (sums_one, sums_two, bias_own, bias_other, bup_own, bup_other), [((16, width), f32)]
    )
    small_got = swap_core(small)
    small = add(small, small_got)
    small_got = swap_chip(small)
    small = add(small, small_got)
    a = weight_grad(
        order_a,
        attn_other,
        (db_own, kept_own[4], (0, local), 0),
        (tok_all[0], gqkv_own, (2 * local, 3 * local), 3 * local),
        small=(small,), pieces=2,
    )
    b = fold(order_b, 1, *b, pieces=1)
    down = fold(order_down, 2, *down, pieces=1)
    part = input_grad(gqkv_own)
    part_c = [swap_core(item) for item in part[1:]]
    a = fold(order_a, 1, *a, small=True, pieces=2)
    up = fold(order_up, 2, *up, pieces=1)
    g_down, = fold_last(*down, turn=True)
    b = fold(order_b, 2, *b, pieces=1)
    a = fold(order_a, 2, *a, small=True, pieces=1)
    g_up, = fold_last(*up)
    g_query, g_key = fold_last(*b, parts=2)
    grad_tokens, = call(
        last_sum_kernel, (part[0], *part_c, got_final, dr1_own), [((rows, width), bf16)], final=(0,)
    )
    g_out, g_value, *small = fold_last(*a, turn=True, parts=2, small=True)
    gg1, gs1, gbo, gg2, gs2, gbd, gbq, gbv, gbu = [item.reshape(-1) for item in small]
    return (
        output,
        grad_tokens,
        g_query,
        gbq,
        g_key,
        g_value,
        gbv,
        g_out,
        gbo,
        gg1,
        gs1,
        g_up,
        gbu,
        g_down,
        gbd,
        gg2,
        gs2,
    )


def solution(mesh):
    fast = mesh.shape["tp"] == 4 and mesh.shape["batch"] == 8
    return jax.shard_map(
        fast_body if fast else body,
        mesh=mesh,
        in_specs=(
            P(("batch", "tp"), None),
            P("batch"),
            P(None, "tp"),
            P("tp"),
            P(None, "tp"),
            P(None, "tp"),
            P("tp"),
            P("tp", None),
            P(),
            P(),
            P(),
            P(None, "tp"),
            P("tp"),
            P("tp", None),
            P(),
            P(),
            P(),
            P(("batch", "tp"), None),
        ),
        out_specs=(
            P(("batch", "tp"), None),
            P(("batch", "tp"), None),
            P("batch", "tp"),
            P(),
            P("batch", "tp"),
            P("batch", "tp"),
            P(),
            P("tp", "batch"),
            P(),
            P(),
            P(),
            P("batch", "tp"),
            P(),
            P("tp", "batch"),
            P(),
            P(),
            P(),
        ),
        check_vma=False,
    )
```
